32 devices in a mesh: grp: 2 (over y), row: 4 (over z), col: 4 (over x, core).
Axes of the slice: x: 2, y: 2, z: 4, core: 2. Of those that a mesh axis runs over, the one named last changes fastest.
Arguments:
- x_state: float32 [4096, 256], P(('col', 'row'), 'grp'), parts along dimension 1, may hold values from -6 to 6
- q_lin: float32 [4096, 256], P(('col', 'row'), 'grp'), parts along dimension 1, may hold values from -6 to 6
- p_diag: float32 [4096], P(('col', 'row')), may hold values from 0.5 to 2
- z_state: float32 [3072, 256], P('row', 'grp'), parts along dimension 1, may hold values from -3 to 3
- y_state: float32 [3072, 256], P('row', 'grp'), parts along dimension 1, may hold values from -3 to 3
- lower_bound: float32 [3072, 256], P('row', 'grp'), parts along dimension 1, may hold values from -1.5 to -0.3
- upper_bound: float32 [3072, 256], P('row', 'grp'), parts along dimension 1, may hold values from 0.3 to 1.5
- a_blocks: float32 [24, 16, 128, 128], P('row', 'col'), may hold values from -0.125 to 0.125
- a_cols: int32 [24, 16], P('row', 'col'), may hold values from 0 to 7, as said below
- p_blocks: float32 [4, 16, 128, 128], P('col', 'row'), as said below
- p_pairs: int32 [4, 4, 2], P('col', 'row'), may hold values from 0 to 7, as said below
Outputs:
- x_next: float32 [4096, 256], P(('col', 'row'), 'grp'), parts along dimension 1
- z_next: float32 [3072, 256], P('row', 'grp'), parts along dimension 1
- y_next: float32 [3072, 256], P('row', 'grp'), parts along dimension 1
The draws below stay inside these ranges and needn't reach their ends.
There are 2 independent parts, one for each index of `grp`. The reference program is written for one: setup_inputs(seed, part) draws one part's arguments, and reference() takes and returns one part's arrays. A program takes and returns all parts, laid end to end along the dimension named above; an argument that names none is the same for every part. Nothing has to cross between parts.
Inputs may be any that keep to these rules, and one draw needn't show every extreme that they name: `a_cols`: in each block row, the 4 entries of one variable range are distinct local block columns of that range. `p_pairs`: each entry holds local block rows i and j of one pair term within its variable range, with i different from j. `p_blocks`: for pair k the slots 4k, 4k+1, 4k+2, 4k+3 hold F F^T, F H^T, H F^T, H H^T of one positive semidefinite term, so that P is symmetric positive definite.
All inputs are finite; a program needn't handle non-finite values.
Results may differ from the reference program's by a relative error of at most 0.00026.
Values sent between devices are 32-bit elements; how exact they have to be, the bound alone decides.
No kernel may reach another device: no remote copies, remote signals or barrier semaphores. Data moves between devices by JAX's collectives and lax.ppermute only.
A program may use at most 64 MiB of HBM per device.

```python
import math
import jax
import jax.numpy as jnp
from jax import lax

BLK = 128
QPS = 128
CB = 8
KA_ROW = 4
ADMM_ITERS = 2
CG_STEPS = 2
MB = 24
NCON = 3072
NVAR = 4096
N_ROW = 4
N_COL = 4


def draw_a_cols(key, part):
    key = jax.random.fold_in(key, 11)
    row_keys = jax.random.split(key, MB * N_COL)
    chosen = jax.vmap(lambda single: jax.random.permutation(single, CB)[:KA_ROW])(row_keys)
    return chosen.reshape(MB, N_COL * KA_ROW).astype(jnp.int32)


def draw_p_pairs(key, part):
    key = jax.random.fold_in(key, 12)
    key_first, key_offset = jax.random.split(key)
    pair_first = jax.random.randint(key_first, (N_COL, N_ROW), 0, CB)
    offsets = jax.random.randint(key_offset, (N_COL, N_ROW), 1, CB)
    pair_second = (pair_first + offsets) % CB
    return jnp.stack([pair_first, pair_second], axis=2).astype(jnp.int32)


def draw_p_blocks(key, part):
    key = jax.random.fold_in(key, 13)
    key_left, key_right = jax.random.split(key)
    factor = 0.8 / math.sqrt(BLK)
    left_factor = jax.random.normal(key_left, (N_COL, N_ROW, BLK, BLK), jnp.float32) * factor
    right_factor = jax.random.normal(key_right, (N_COL, N_ROW, BLK, BLK), jnp.float32) * factor
    prec = lax.Precision.HIGHEST
    block_ll = jnp.einsum('crik,crjk->crij', left_factor, left_factor, precision=prec)
    block_lr = jnp.einsum('crik,crjk->crij', left_factor, right_factor, precision=prec)
    block_rl = jnp.swapaxes(block_lr, -1, -2)
    block_rr = jnp.einsum('crik,crjk->crij', right_factor, right_factor, precision=prec)
    stacked = jnp.stack([block_ll, block_lr, block_rl, block_rr], axis=2)
    return stacked.reshape(N_COL, 4 * N_ROW, BLK, BLK).astype(jnp.float32)


def block_scale(stream_key, dims, shards, smallest, largest):
    loudness = 1.0
    for axis_at, blocks in shards:
        heights = jax.random.uniform(jax.random.fold_in(jax.random.fold_in(stream_key, 6), axis_at), (blocks,), jnp.float32, smallest / len(shards), largest / len(shards))
        loudness = loudness * jnp.repeat(jnp.exp(heights), dims[axis_at] // blocks).reshape((-1,) + (1,) * (len(dims) - 1 - axis_at))
    return loudness


def noise(own_key, shape, scale, most, cuts=(), kind=jnp.bfloat16):
    result = jax.random.normal(own_key, shape, jnp.float32) * scale
    if len(cuts) > 0:
        result = block_scale(own_key, shape, cuts, -0.22, 0.18) * result
    return jnp.clip(result, min=-most, max=most).astype(kind)


def setup_inputs(seed: int = 0, part: int = 0) -> dict:
    key_of = jax.random.split(jax.random.key(seed), 12)
    part_splits = jax.random.split(jax.random.fold_in(key_of[11], part), 12)
    x_state = noise(part_splits[0], (NVAR, QPS), 1.0, 6.0, ((0, 16),), jnp.float32)
    q_lin = noise(part_splits[1], (NVAR, QPS), 1.0, 6.0, ((0, 16),), jnp.float32)
    p_diag = jnp.clip(0.5 + 1.5 * jax.random.uniform(key_of[2], (NVAR,), jnp.float32) ** block_scale(key_of[2], (NVAR,), ((0, 16),), -0.2, 0.2), 0.5, 2.0)
    z_state = noise(part_splits[3], (NCON, QPS), 0.5, 3.0, ((0, 4),), jnp.float32)
    y_state = noise(part_splits[4], (NCON, QPS), 0.5, 3.0, ((0, 4),), jnp.float32)
    lower_bound = jnp.clip(-1.5 + 1.2 * jax.random.uniform(part_splits[5], (NCON, QPS), jnp.float32) ** block_scale(part_splits[5], (NCON, QPS), ((0, 4),), -0.2, 0.2), -1.5, -0.3)
    upper_bound = jnp.clip(0.3 + 1.2 * jax.random.uniform(part_splits[6], (NCON, QPS), jnp.float32) ** block_scale(part_splits[6], (NCON, QPS), ((0, 4),), -0.2, 0.2), 0.3, 1.5)
    a_blocks = noise(key_of[7], (MB, KA_ROW * N_COL, BLK, BLK), (KA_ROW * N_COL * BLK) ** -0.5, 0.125, ((0, 4), (1, 4)), jnp.float32)
    a_cols = draw_a_cols(jax.random.fold_in(key_of[11], 71), part)
    p_blocks = draw_p_blocks(jax.random.fold_in(key_of[11], 71), part)
    p_pairs = draw_p_pairs(jax.random.fold_in(key_of[11], 71), part)
    return dict(x_state=x_state, q_lin=q_lin, p_diag=p_diag, z_state=z_state, y_state=y_state, lower_bound=lower_bound, upper_bound=upper_bound, a_blocks=a_blocks, a_cols=a_cols, p_blocks=p_blocks, p_pairs=p_pairs)


rho_penalty = 0.5
sigma_shift = 1e-6
relaxation = 1.6
highest = lax.Precision.HIGHEST


def range_of_slot():
    return jnp.arange(N_COL * KA_ROW, dtype=jnp.int32) // KA_ROW


def apply_a(a_blocks, a_cols, vector):
    grid = vector.reshape(N_COL, CB, BLK, QPS)
    ranges = range_of_slot()

    def one_row(row_item):
        row_blocks, row_cols = row_item
        picked = grid[ranges, row_cols]
        return jnp.einsum('kij,kjq->iq', row_blocks, picked, precision=highest)

    return lax.map(one_row, (a_blocks, a_cols)).reshape(MB * BLK, QPS)


def apply_at(a_blocks, a_cols, slab_vec):
    ranges = range_of_slot()
    rows_w = slab_vec.reshape(MB, BLK, QPS)

    def one_step(running, row_item):
        row_blocks, row_cols, row_w = row_item
        pieces = jnp.einsum('kij,iq->kjq', row_blocks, row_w, precision=highest)
        return running.at[ranges * CB + row_cols].add(pieces), None

    start = jnp.zeros((N_COL * CB, BLK, QPS), jnp.float32)
    running, _ = lax.scan(one_step, start, (a_blocks, a_cols, rows_w))
    return running.reshape(NVAR, QPS)


def pair_index(p_pairs):
    pair_first = p_pairs[:, :, 0]
    pair_second = p_pairs[:, :, 1]
    rows_idx = jnp.stack([pair_first, pair_first, pair_second, pair_second], axis=2).reshape(N_COL, 4 * N_ROW)
    cols_idx = jnp.stack([pair_first, pair_second, pair_first, pair_second], axis=2).reshape(N_COL, 4 * N_ROW)
    return rows_idx.astype(jnp.int32), cols_idx.astype(jnp.int32)


def apply_p(p_blocks, p_pairs, vector):
    grid = vector.reshape(N_COL, CB, BLK, QPS)
    rows_idx, cols_idx = pair_index(p_pairs)
    ranges = jnp.arange(N_COL, dtype=jnp.int32)[:, None]
    picked = grid[ranges, cols_idx]
    pieces = jnp.einsum('ckij,ckjq->ckiq', p_blocks, picked, precision=highest)
    running = jnp.zeros((N_COL, CB, BLK, QPS), jnp.float32).at[ranges, rows_idx].add(pieces)
    return running.reshape(NVAR, QPS)


def jacobi(p_diag, a_blocks, a_cols, p_blocks, p_pairs):
    ranges = range_of_slot()
    col_squares = jnp.sum(a_blocks * a_blocks, axis=2)
    flat_index = (ranges[None, :] * CB + a_cols).reshape(-1)
    col_total = jnp.zeros((N_COL * CB, BLK), jnp.float32).at[flat_index].add(col_squares.reshape(-1, BLK))
    grouped = p_blocks.reshape(N_COL, N_ROW, 4, BLK, BLK)
    diag_first = jnp.diagonal(grouped[:, :, 0], axis1=-2, axis2=-1)
    diag_second = jnp.diagonal(grouped[:, :, 3], axis1=-2, axis2=-1)
    col_range = jnp.arange(N_COL, dtype=jnp.int32)[:, None]
    pair_total = jnp.zeros((N_COL, CB, BLK), jnp.float32)
    pair_total = pair_total.at[col_range, p_pairs[:, :, 0]].add(diag_first)
    pair_total = pair_total.at[col_range, p_pairs[:, :, 1]].add(diag_second)
    local_terms = pair_total.reshape(-1) + rho_penalty * col_total.reshape(-1)
    return p_diag + sigma_shift + local_terms


def reference(x_state, q_lin, p_diag, z_state, y_state, lower_bound, upper_bound, a_blocks, a_cols, p_blocks, p_pairs):
    diag_k = jacobi(p_diag, a_blocks, a_cols, p_blocks, p_pairs)[:, None]
    shift_k = (p_diag + sigma_shift)[:, None]
    primal, slack, duals = x_state, z_state, y_state
    for outer_step in range(ADMM_ITERS):
        slab_now = apply_a(a_blocks, a_cols, primal)
        coupled = apply_p(p_blocks, p_pairs, primal) + apply_at(a_blocks, a_cols, rho_penalty * slab_now - (rho_penalty * slack - duals))
        residual = -q_lin - p_diag[:, None] * primal - coupled
        precond = residual / diag_k
        rz_now = jnp.sum(residual * precond, axis=0)
        direction = precond
        x_hat, ax_hat = primal, slab_now
        for inner_step in range(CG_STEPS):
            a_dir = apply_a(a_blocks, a_cols, direction)
            k_dir = shift_k * direction + (apply_p(p_blocks, p_pairs, direction) + apply_at(a_blocks, a_cols, rho_penalty * a_dir))
            curvature = jnp.sum(direction * k_dir, axis=0)
            step_size = rz_now / curvature
            x_hat = x_hat + step_size * direction
            ax_hat = ax_hat + step_size * a_dir
            if inner_step + 1 < CG_STEPS:
                residual = residual - step_size * k_dir
                precond = residual / diag_k
                rz_next = jnp.sum(residual * precond, axis=0)
                direction = precond + (rz_next / rz_now) * direction
                rz_now = rz_next
        relaxed = relaxation * ax_hat + (1.0 - relaxation) * slack
        z_new = jnp.clip(relaxed + duals / rho_penalty, lower_bound, upper_bound)
        duals = duals + rho_penalty * (relaxed - z_new)
        primal = relaxation * x_hat + (1.0 - relaxation) * primal
        slack = z_new
    return primal, slack, duals
```

```python
import functools

import jax
import jax.numpy as jnp
from jax import lax
from jax.experimental import pallas as pl
from jax.experimental.pallas import tpu as pltpu
from jax.sharding import PartitionSpec as P

ADMM_ITERS = 2
RHO = 0.5
SIGMA = 1e-06
RELAX = 1.6
BLK = 128
LANES = 128
HALF = 64
SC = 8
F32 = jnp.float32
BF16 = jnp.bfloat16

VMEM = pl.BlockSpec(memory_space=pltpu.VMEM)
SMEM = pl.BlockSpec(memory_space=pltpu.SMEM)


def call(body, outs, ins, smem=(), scratch=(), flops=0):
    n_bytes = sum(v.size * v.dtype.itemsize for v in ins)
    return pl.pallas_call(
        body,
        out_shape=[jax.ShapeDtypeStruct(s, d) for s, d in outs],
        in_specs=[SMEM] * len(smem) + [VMEM] * len(ins),
        out_specs=[VMEM] * len(outs),
        scratch_shapes=list(scratch),
        compiler_params=pltpu.CompilerParams(vmem_limit_bytes=30 * 1024 * 1024),
        cost_estimate=pl.CostEstimate(flops=flops, bytes_accessed=n_bytes, transcendentals=0),
    )(*smem, *ins)


def low_half(shape):
    return lax.broadcasted_iota(jnp.int32, shape, 1) < HALF


def turn(v):
    return pltpu.roll(v, HALF, 1)


def fold(v):
    return v + turn(v)


def col_sum(v):
    return fold(jnp.sum(v, axis=0, keepdims=True))


def split_bf16(v):
    hi = v.astype(BF16).astype(F32)
    return hi, v - hi


def pair_up(v):
    hi, lo = split_bf16(v)
    low = low_half(v.shape)
    first = jnp.where(low, hi, turn(lo)).astype(BF16)
    second = jnp.where(low, turn(hi), lo).astype(BF16)
    return first, second


def dot(a, b):
    return jnp.dot(a, b, preferred_element_type=F32)


def pack_rows(*rows):
    at = lax.broadcasted_iota(jnp.int32, (SC, LANES), 0)
    tile = jnp.zeros((SC, LANES), F32)
    for k, row in enumerate(rows):
        tile = jnp.where(at == k, row, tile)
    return tile


def send_kernel(place, x, q, msg):
    core = place[1]
    low = low_half(x.shape)
    xv = jnp.where(core == 0, turn(x[...]), x[...])
    qv = jnp.where(core == 0, q[...], turn(q[...]))
    msg[...] = jnp.where(low, xv, qv)


def recv_kernel(place, x, q, got, x_own, q_own):
    core = place[1]
    low = low_half(x.shape)
    xv = jnp.where(core == 0, x[...], turn(x[...]))
    qv = jnp.where(core == 0, q[...], turn(q[...]))
    x_own[...] = jnp.where(low, xv, turn(got[...]))
    q_own[...] = jnp.where(low, qv, got[...])


def slab_kernel(place, *refs):
    core = place[1]
    count = len(refs) // 2
    for src, dst in zip(refs[:count], refs[count:]):
        rows = dst.shape[0]
        v = jnp.where(core == 0, src[...], turn(src[...]))
        dst[...] = jnp.where(low_half(dst.shape), v[:rows], turn(v[rows:]))


def prep_kernel(slab, per, cols, pairs, a_mine, a_other, p_mine, p_other, a_hi, a_lo, t_hi, t_lo, p_hi, p_lo, diag):
    span = a_hi.shape[1] // 2
    n_range = span // BLK
    for ref in (a_hi, a_lo, t_hi, t_lo):
        ref[...] = jnp.zeros(ref.shape, BF16)
    diag[...] = jnp.zeros(diag.shape, F32)
    for t, src in enumerate((a_mine, a_other)):
        for m in range(slab):
            rows = slice(m * BLK, (m + 1) * BLK)
            for s in range(per):
                k = m * per + s
                col = cols[t * slab * per + k]
                at = pl.multiple_of(t * span + col * BLK, BLK)
                block = src[k]
                hi, lo = split_bf16(block)
                a_hi[rows, pl.ds(at, BLK)] = hi.astype(BF16)
                a_lo[rows, pl.ds(at, BLK)] = lo.astype(BF16)
                hi, lo = split_bf16(block.T)
                t_hi[pl.ds(at, BLK), rows] = hi.astype(BF16)
                t_lo[pl.ds(at, BLK), rows] = lo.astype(BF16)
                here = pl.ds(t * n_range + col, 1)
                diag[here, :] += RHO * jnp.sum(block * block, axis=0, keepdims=True)
    shape = (BLK, BLK)
    eye = lax.broadcasted_iota(jnp.int32, shape, 0) == lax.broadcasted_iota(jnp.int32, shape, 1)
    for t, src in enumerate((p_mine, p_other)):
        for e in range(4):
            hi, lo = split_bf16(src[e])
            rows = slice((e // 2) * BLK, (e // 2 + 1) * BLK)
            lanes = slice((e % 2) * BLK, (e % 2 + 1) * BLK)
            p_hi[t, rows, lanes] = hi.astype(BF16)
            p_lo[t, rows, lanes] = lo.astype(BF16)
        for e in range(2):
            here = pl.ds(t * n_range + pairs[2 * t + e], 1)
            diag[here, :] += jnp.sum(jnp.where(eye, src[3 * e], 0.0), axis=0, keepdims=True)


def forward_kernel(n, own, scalars, place, pairs, *refs):
    msgs, rest = refs[:n], refs[n:]
    a_hi, a_lo, p_hi, p_lo = rest[:4]
    rest = rest[4:]
    if scalars == 2:
        pp_first, rest = rest[0], rest[1:]
    msg, pp, whole, wide = rest
    row = place[0]
    span = whole.shape[0]
    for k in range(n):
        at = lax.rem(row + n - k, n) * own
        at = pl.multiple_of(at, own)
        v = msgs[k][0:own, :]
        whole[pl.ds(at, own), :] = v
        first, second = pair_up(v)
        wide[pl.ds(at, own), :] = first
        wide[pl.ds(pl.multiple_of(span + at, own), own), :] = second
    x = wide[...]
    total = fold(dot(a_hi[...], x) + dot(a_lo[...], x))
    rows = total.shape[0] // 2
    msg[0:rows, :] = jnp.where(low_half((rows, LANES)), total[:rows], total[rows:])
    parts = []
    for t in range(2):
        at_i = pl.multiple_of(t * span + pairs[2 * t] * BLK, BLK)
        at_j = pl.multiple_of(t * span + pairs[2 * t + 1] * BLK, BLK)
        v = jnp.concatenate([wide[pl.ds(at_i, BLK), :], wide[pl.ds(at_j, BLK), :]], axis=0)
        parts.append(fold(dot(p_hi[t], v) + dot(p_lo[t], v)))
    low2 = low_half((2 * BLK, LANES))
    pp_now = jnp.where(low2, parts[0], parts[1])
    pp[...] = pp_now
    if scalars:
        picked = []
        for t in range(2):
            at_i = pl.multiple_of(pairs[2 * t] * BLK, BLK)
            at_j = pl.multiple_of(pairs[2 * t + 1] * BLK, BLK)
            picked.append(jnp.concatenate([whole[pl.ds(at_i, BLK), :], whole[pl.ds(at_j, BLK), :]], axis=0))
        vec = jnp.where(low2, picked[0], picked[1])
        tile = msgs[0][own : own + SC, :]
        for k in range(1, n):
            tile = tile + msgs[k][own : own + SC, :]
        tile = fold(tile)
        at = lax.broadcasted_iota(jnp.int32, (SC, LANES), 0)
        tile = jnp.where(at == 3, col_sum(vec * pp_now), tile)
        if scalars == 2:
            tile = jnp.where(at == 4, col_sum(vec * pp_first[...]), tile)
        msg[rows : rows + SC, :] = tile


def back_product(n, own, place, pairs, w, pp_now, t_hi, t_lo, total, outs, extra):
    row = place[0]
    span = total.shape[0]
    first, second = pair_up(w)
    wide = jnp.concatenate([first, second], axis=0)
    part = fold(dot(t_hi[...], wide) + dot(t_lo[...], wide))
    low = low_half((span, LANES))
    total[...] = jnp.where(low, part[:span], part[span:])
    low1 = low_half((BLK, LANES))
    for t in range(2):
        side = low1 if t == 0 else jnp.logical_not(low1)
        for e in range(2):
            at = pl.ds(pl.multiple_of(pairs[2 * t + e] * BLK, BLK), BLK)
            total[at, :] += jnp.where(side, pp_now[e * BLK : (e + 1) * BLK], 0.0)
    for k in range(n):
        at = pl.multiple_of(lax.rem(row + k, n) * own, own)
        outs[k][0:own, :] = total[pl.ds(at, own), :]
        if extra is not None:
            outs[k][own : own + extra.shape[0], :] = extra


def start_back_kernel(n, nx, own, place, pairs, *refs):
    msgs, rest = refs[:nx], refs[nx:]
    z, y, pp, diag, t_hi, t_lo = rest[:6]
    outs, (ax, total) = rest[6 : 6 + n], rest[6 + n :]
    ax_now = msgs[0][...]
    for k in range(1, nx):
        ax_now = ax_now + msgs[k][...]
    ax[...] = ax_now
    w = RHO * ax_now - (RHO * z[...] - y[...])
    back_product(n, own, place, pairs, w, pp[...], t_hi, t_lo, total, outs, diag[...])


def step_back_kernel(n, nx, own, place, pairs, *refs):
    msgs, rest = refs[:nx], refs[nx:]
    pp, t_hi, t_lo = rest[:3]
    outs, (ad, scal, total) = rest[3 : 3 + n], rest[3 + n :]
    rows = ad.shape[0]
    v = msgs[0][...]
    for k in range(1, nx):
        v = v + msgs[k][...]
    ad_now = v[:rows]
    tile = v[rows:]
    ad[...] = ad_now
    scal[...] = tile
    curve = RHO * col_sum(ad_now * ad_now) + tile[3:4]
    back_product(
        n, own, place, pairs, RHO * ad_now, pp[...], t_hi, t_lo, total, outs, pack_rows(curve)
    )


def residual_kernel(n, own, first, place, *refs):
    msgs, rest = refs[:n], refs[n:]
    if first:
        x, q, pd, msg, res, dk, full = rest
        rows = msgs[0].shape[0] - own
        tile = msgs[0][own:, :]
        for k in range(1, n):
            tile = tile + msgs[k][own:, :]
        n_range = rows // 2
        low1 = low_half((BLK, LANES))
        for b in range(n_range):
            mine = jnp.broadcast_to(tile[b : b + 1], (BLK, LANES)).T
            other = jnp.broadcast_to(tile[n_range + b : n_range + b + 1], (BLK, LANES)).T
            full[b * BLK : (b + 1) * BLK, :] = jnp.where(low1, mine, other)
        at = pl.multiple_of(place[0] * own, own)
        diag = pd[...] + SIGMA + full[pl.ds(at, own), :]
        dk[...] = diag
    else:
        x, q, pd, dk, msg, res = rest
        diag = dk[...]
    total = msgs[0][0:own, :]
    for k in range(1, n):
        total = total + msgs[k][0:own, :]
    r = -q[...] - pd[...] * x[...] - total
    s = r / diag
    res[...] = r
    msg[0:own, :] = s
    shift = pd[...] + SIGMA
    rz = jnp.sum(r * s, axis=0, keepdims=True)
    dd = jnp.sum(shift * s * s, axis=0, keepdims=True)
    msg[own : own + SC, :] = pack_rows(rz, dd)


def step_kernel(n, own, *refs):
    msgs, rest = refs[:n], refs[n:]
    scal, prev, r, pd, dk, msg, step_out = rest
    total = msgs[0][...]
    for k in range(1, n):
        total = total + msgs[k][...]
    shift = pd[...] + SIGMA
    d = prev[0:own, :]
    kd = shift * d + total[:own]
    curve = total[own : own + 1] + scal[1:2, :]
    step = scal[0:1, :] / curve
    r_new = r[...] - step * kd
    s = r_new / dk[...]
    msg[0:own, :] = s
    rz = jnp.sum(r_new * s, axis=0, keepdims=True)
    ss = jnp.sum(shift * s * s, axis=0, keepdims=True)
    sd = jnp.sum(shift * s * d, axis=0, keepdims=True)
    msg[own : own + SC, :] = pack_rows(rz, ss, sd)
    step_out[...] = jnp.broadcast_to(step, step_out.shape)


def curve_kernel(nx, *refs):
    msgs, rest = refs[:nx], refs[nx:]
    scal, ad, ad2, share, keep = rest
    rows = ad.shape[0]
    v = msgs[0][...]
    for k in range(1, nx):
        v = v + msgs[k][...]
    tile = v[rows:]
    beta = tile[0:1] / scal[0:1, :]
    ad_now = v[:rows] + beta * ad[...]
    ad2[...] = ad_now
    flat = tile[1:2] + 2.0 * beta * tile[2:3] + beta * beta * scal[1:2, :]
    pair = tile[3:4] + 2.0 * beta * tile[4:5] + beta * beta * scal[3:4, :]
    share[...] = pack_rows(RHO * col_sum(ad_now * ad_now) + pair)
    keep[...] = pack_rows(tile[0:1], beta, flat)


def admm_update(n, own, refs):
    shares, rest = refs[:n], refs[n:]
    keep, step_in, ax, ad, ad2, z, y, lower, upper, x, msg1, msg2 = rest[:12]
    tile = shares[0][...]
    for k in range(1, n):
        tile = tile + shares[k][...]
    beta = keep[1:2, :]
    step1 = step_in[0:1, :]
    step2 = keep[0:1, :] / (tile[0:1] + keep[2:3, :])
    d1 = msg1[0:own, :]
    d2 = msg2[0:own, :] + beta * d1
    x_hat = x[...] + step1 * d1 + step2 * d2
    x_new = RELAX * x_hat + (1.0 - RELAX) * x[...]
    ax_hat = ax[...] + step1 * ad[...] + step2 * ad2[...]
    relaxed = RELAX * ax_hat + (1.0 - RELAX) * z[...]
    z_new = jnp.clip(relaxed + y[...] / RHO, lower[...], upper[...])
    y_new = y[...] + RHO * (relaxed - z_new)
    return beta, step1, step2, x_new, ax_hat, z_new, y_new, rest[12:]


def update_kernel(n, own, place, pairs, *refs):
    beta, step1, step2, x_new, ax_hat, z_new, y_new, rest = admm_update(n, own, refs)
    ax = refs[n + 2]
    ppx, pp1, pp2, t_hi, t_lo = rest[:5]
    outs, (x_out, z_out, y_out, ax_out, ppx_out, total) = rest[5 : 5 + n], rest[5 + n :]
    x_out[...] = x_new
    z_out[...] = z_new
    y_out[...] = y_new
    ax_new = RELAX * ax_hat + (1.0 - RELAX) * ax[...]
    ax_out[...] = ax_new
    pp_hat = ppx[...] + step1 * pp1[...] + step2 * (pp2[...] + beta * pp1[...])
    pp_new = RELAX * pp_hat + (1.0 - RELAX) * ppx[...]
    ppx_out[...] = pp_new
    w = RHO * ax_new - (RHO * z_new - y_new)
    back_product(n, own, place, pairs, w, pp_new, t_hi, t_lo, total, outs, None)


def last_kernel(n, own, *refs):
    _, _, _, x_new, _, z_new, y_new, rest = admm_update(n, own, refs)
    (out,) = rest
    rows = z_new.shape[0]
    out[0:rows, :] = z_new
    out[rows : 2 * rows, :] = y_new
    out[2 * rows :, :] = x_new


def finish_kernel(place, mine, got, x, z, y):
    core = place[1]
    rows = z.shape[0] // 2
    for k, dst in enumerate((z, y)):
        a = mine[k * rows : (k + 1) * rows, :]
        b = got[k * rows : (k + 1) * rows, :]
        low = low_half(a.shape)
        left = jnp.where(core == 0, a, b)
        right = jnp.where(core == 0, b, a)
        dst[0:rows, :] = jnp.where(low, left, turn(right))
        dst[rows : 2 * rows, :] = jnp.where(low, turn(left), right)
    a = mine[2 * rows :, :]
    b = got[2 * rows :, :]
    low = low_half(a.shape)
    x[...] = jnp.where(core == 0, jnp.where(low, a, b), jnp.where(low, turn(b), turn(a)))


def local(x_state, q_lin, p_diag, z_state, y_state, lower_bound, upper_bound, a_blocks, a_cols, p_blocks, p_pairs):
    slab, per = a_cols.shape
    n = lax.axis_size("row")
    n_col = lax.axis_size("col")
    nx = n_col // 2
    own = x_state.shape[0]
    span = own * n
    n_range = span // BLK
    slab_rows = slab * BLK
    half_rows = slab_rows // 2
    row_at = lax.axis_index("row")
    core_at = lax.axis_index("col") % 2
    place = jnp.stack([row_at, core_at]).astype(jnp.int32)

    def to_core(v):
        return lax.ppermute(v, "col", [(c, c ^ 1) for c in range(n_col)])

    def to_x(v):
        got = [lax.ppermute(v, "col", [(c, (c + 2 * k) % n_col) for c in range(n_col)]) for k in range(1, nx)]
        return [v] + got

    def to_row(pieces):
        got = [lax.ppermute(pieces[k], "row", [(i, (i + k) % n) for i in range(n)]) for k in range(1, n)]
        return [pieces[0]] + got

    a_mine = a_blocks.reshape(slab * per, BLK, BLK)
    p_mine = p_blocks.reshape(4, BLK, BLK)
    ints = jnp.concatenate([a_cols.reshape(-1), p_pairs.reshape(-1)])
    (send,) = call(send_kernel, [((own, LANES), F32)], [x_state, q_lin], [place])
    got_xq = to_core(send)
    a_other = to_core(a_mine)
    ints_other = to_core(ints)
    p_other = to_core(p_mine)
    pd_other = to_core(p_diag)
    count = slab * per
    cols = jnp.concatenate([ints[:count], ints_other[:count]])
    pairs = jnp.concatenate([ints[count:], ints_other[count:]])
    pd = jnp.concatenate(
        [jnp.broadcast_to(p_diag[:, None], (own, HALF)), jnp.broadcast_to(pd_other[:, None], (own, HALF))], axis=1
    )
    x, q = call(recv_kernel, [((own, LANES), F32)] * 2, [x_state, q_lin, got_xq], [place])
    x_parts = to_row([x] * n)
    z, y, lower, upper = call(
        slab_kernel, [((half_rows, LANES), F32)] * 4, [z_state, y_state, lower_bound, upper_bound], [place]
    )
    wide = 2 * span
    a_hi, a_lo, t_hi, t_lo, p_hi, p_lo, diag = call(
        functools.partial(prep_kernel, slab, per),
        [((slab_rows, wide), BF16)] * 2
        + [((wide, slab_rows), BF16)] * 2
        + [((2, 2 * BLK, 2 * BLK), BF16)] * 2
        + [((2 * n_range, LANES), F32)],
        [a_mine, a_other, p_mine, p_other],
        [cols, pairs],
        flops=10**8,
    )
    prod_flops = 4 * slab_rows * wide * LANES
    total_scratch = [pltpu.VMEM((span, LANES), F32)]

    def forward(msgs, scalars, pp_first=()):
        extra = SC if scalars else 0
        return call(
            functools.partial(forward_kernel, n, own, scalars),
            [((half_rows + extra, LANES), F32), ((2 * BLK, LANES), F32)],
            [*msgs, a_hi, a_lo, p_hi, p_lo, *pp_first],
            [place, pairs],
            total_scratch + [pltpu.VMEM((wide, LANES), BF16)],
            flops=prod_flops,
        )

    msg, ppx = forward(x_parts, 0)
    *pieces, ax = call(
        functools.partial(start_back_kernel, n, nx, own),
        [((own + 2 * n_range, LANES), F32)] * n + [((half_rows, LANES), F32)],
        [*to_x(msg), z, y, ppx, diag, t_hi, t_lo],
        [place, pairs],
        total_scratch,
        flops=prod_flops,
    )
    own_shape = ((own, LANES), F32)
    msg_shape = ((own + SC, LANES), F32)
    tile_shape = ((SC, LANES), F32)
    slab_shape = ((half_rows, LANES), F32)
    for outer in range(ADMM_ITERS):
        if outer == 0:
            msg1, r, dk = call(
                functools.partial(residual_kernel, n, own, True),
                [msg_shape, own_shape, own_shape],
                [*to_row(pieces), x, q, pd],
                [place],
                total_scratch,
            )
        else:
            msg1, r = call(
                functools.partial(residual_kernel, n, own, False),
                [msg_shape, own_shape],
                [*to_row(pieces), x, q, pd, dk],
                [place],
            )
        msg, pp1 = forward(to_row([msg1] * n), 1)
        *pieces, ad, scal = call(
            functools.partial(step_back_kernel, n, nx, own),
            [msg_shape] * n + [slab_shape, tile_shape],
            [*to_x(msg), pp1, t_hi, t_lo],
            [place, pairs],
            total_scratch,
            flops=prod_flops,
        )
        msg2, step = call(
            functools.partial(step_kernel, n, own),
            [msg_shape, tile_shape],
            [*to_row(pieces), scal, msg1, r, pd, dk],
        )
        msg, pp2 = forward(to_row([msg2] * n), 2, (pp1,))
        ad2, share, keep = call(
            functools.partial(curve_kernel, nx),
            [slab_shape, tile_shape, tile_shape],
            [*to_x(msg), scal, ad],
        )
        shares = to_row([share] * n)
        state = [*shares, keep, step, ax, ad, ad2, z, y, lower, upper, x, msg1, msg2]
        if outer + 1 < ADMM_ITERS:
            *pieces, x, z, y, ax, ppx = call(
                functools.partial(update_kernel, n, own),
                [own_shape] * n + [own_shape, slab_shape, slab_shape, slab_shape, ((2 * BLK, LANES), F32)],
                [*state, ppx, pp1, pp2, t_hi, t_lo],
                [place, pairs],
                total_scratch,
                flops=prod_flops,
            )
        else:
            (out,) = call(
                functools.partial(last_kernel, n, own), [((2 * half_rows + own, LANES), F32)], state
            )
    return call(
        finish_kernel,
        [own_shape, ((slab_rows, LANES), F32), ((slab_rows, LANES), F32)],
        [out, to_core(out)],
        [place],
    )


def solution(mesh):
    placed = (
        P(("col", "row"), "grp"),
        P(("col", "row"), "grp"),
        P(("col", "row")),
        P("row", "grp"),
        P("row", "grp"),
        P("row", "grp"),
        P("row", "grp"),
        P("row", "col", None, None),
        P("row", "col"),
        P("col", "row", None, None),
        P("col", "row", None),
    )

    def run(*args):
        return tuple(local(*args))

    return jax.shard_map(
        run,
        mesh=mesh,
        in_specs=placed,
        out_specs=(P(("col", "row"), "grp"), P("row", "grp"), P("row", "grp")),
        check_vma=False,
    )
```

```python
import functools

import jax
import jax.numpy as jnp
from jax import lax
from jax.experimental import pallas as pl
from jax.experimental.pallas import tpu as pltpu
from jax.sharding import PartitionSpec as P

ADMM_ITERS = 2
RHO = 0.5
SIGMA = 1e-06
RELAX = 1.6
BLK = 128
LANES = 128
HALF = 64
SC = 8
F32 = jnp.float32
BF16 = jnp.bfloat16

VMEM = pl.BlockSpec(memory_space=pltpu.VMEM)
SMEM = pl.BlockSpec(memory_space=pltpu.SMEM)


def call(body, outs, ins, smem=(), scratch=(), flops=0):
    n_bytes = sum(v.size * v.dtype.itemsize for v in ins)
    return pl.pallas_call(
        body,
        out_shape=[jax.ShapeDtypeStruct(s, d) for s, d in outs],
        in_specs=[SMEM] * len(smem) + [VMEM] * len(ins),
        out_specs=[VMEM] * len(outs),
        scratch_shapes=list(scratch),
        compiler_params=pltpu.CompilerParams(vmem_limit_bytes=30 * 1024 * 1024),
        cost_estimate=pl.CostEstimate(flops=flops, bytes_accessed=n_bytes, transcendentals=0),
    )(*smem, *ins)


def low_half(shape):
    return lax.broadcasted_iota(jnp.int32, shape, 1) < HALF


def turn(v):
    return pltpu.roll(v, HALF, 1)


def fold(v):
    return v + turn(v)


def col_sum(v):
    return fold(jnp.sum(v, axis=0, keepdims=True))


def split_bf16(v):
    hi = v.astype(BF16).astype(F32)
    return hi, v - hi


def pair_up(v):
    hi, lo = split_bf16(v)
    low = low_half(v.shape)
    first = jnp.where(low, hi, turn(lo)).astype(BF16)
    second = jnp.where(low, turn(hi), lo).astype(BF16)
    return first, second


def dot(a, b):
    return jnp.dot(a, b, preferred_element_type=F32)


def pack_rows(*rows):
    at = lax.broadcasted_iota(jnp.int32, (SC, LANES), 0)
    tile = jnp.zeros((SC, LANES), F32)
    for k, row in enumerate(rows):
        tile = jnp.where(at == k, row, tile)
    return tile


def mix_cores(core, mine, other):
    low = low_half(mine.shape)
    a = jnp.where(core == 0, mine, turn(mine))
    b = jnp.where(core == 0, turn(other), other)
    return jnp.where(low, a, b)


def own_kernel(place, x, x_other, q, q_other, x_own, q_own):
    core = place[1]
    x_own[...] = mix_cores(core, x[...], x_other[...])
    q_own[...] = mix_cores(core, q[...], q_other[...])


def slab_kernel(place, *refs):
    core = place[1]
    count = len(refs) // 2
    for src, dst in zip(refs[:count], refs[count:]):
        rows = dst.shape[0]
        v = jnp.where(core == 0, src[...], turn(src[...]))
        dst[...] = jnp.where(low_half(dst.shape), v[:rows], turn(v[rows:]))


def prep_kernel(slab, per, cols, pairs, a_mine, a_other, p_mine, p_other, a_hi, a_lo, t_hi, t_lo, p_hi, p_lo, diag):
    span = a_hi.shape[1] // 2
    n_range = span // BLK
    for ref in (a_hi, a_lo, t_hi, t_lo):
        ref[...] = jnp.zeros(ref.shape, BF16)
    diag[...] = jnp.zeros(diag.shape, F32)
    for t, src in enumerate((a_mine, a_other)):
        for m in range(slab):
            rows = slice(m * BLK, (m + 1) * BLK)
            for s in range(per):
                k = m * per + s
                col = cols[t * slab * per + k]
                at = pl.multiple_of(t * span + col * BLK, BLK)
                block = src[k]
                hi, lo = split_bf16(block)
                a_hi[rows, pl.ds(at, BLK)] = hi.astype(BF16)
                a_lo[rows, pl.ds(at, BLK)] = lo.astype(BF16)
                hi, lo = split_bf16(block.T)
                t_hi[pl.ds(at, BLK), rows] = hi.astype(BF16)
                t_lo[pl.ds(at, BLK), rows] = lo.astype(BF16)
                here = pl.ds(t * n_range + col, 1)
                diag[here, :] += RHO * jnp.sum(block * block, axis=0, keepdims=True)
    shape = (BLK, BLK)
    eye = lax.broadcasted_iota(jnp.int32, shape, 0) == lax.broadcasted_iota(jnp.int32, shape, 1)
    for t, src in enumerate((p_mine, p_other)):
        for e in range(4):
            hi, lo = split_bf16(src[e])
            rows = slice((e // 2) * BLK, (e // 2 + 1) * BLK)
            lanes = slice((e % 2) * BLK, (e % 2 + 1) * BLK)
            p_hi[t, rows, lanes] = hi.astype(BF16)
            p_lo[t, rows, lanes] = lo.astype(BF16)
        for e in range(2):
            here = pl.ds(t * n_range + pairs[2 * t + e], 1)
            diag[here, :] += jnp.sum(jnp.where(eye, src[3 * e], 0.0), axis=0, keepdims=True)


def forward_kernel(n, own, scalars, place, pairs, *refs):
    msgs, rest = refs[:n], refs[n:]
    if scalars == 0:
        others, rest = rest[:n], rest[n:]
    a_hi, a_lo, p_hi, p_lo = rest[:4]
    rest = rest[4:]
    if scalars == 2:
        pp_first, rest = rest[0], rest[1:]
    msg, pp, whole, wide = rest
    row = place[0]
    span = whole.shape[0]
    for k in range(n):
        at = pl.multiple_of(lax.bitwise_xor(row, k) * own, own)
        v = msgs[k][0:own, :]
        if scalars == 0:
            v = mix_cores(place[1], v, others[k][...])
        whole[pl.ds(at, own), :] = v
        first, second = pair_up(v)
        wide[pl.ds(at, own), :] = first
        wide[pl.ds(pl.multiple_of(span + at, own), own), :] = second
    x = wide[...]
    total = fold(dot(a_hi[...], x) + dot(a_lo[...], x))
    rows = total.shape[0] // 2
    msg[0:rows, :] = jnp.where(low_half((rows, LANES)), total[:rows], total[rows:])
    parts = []
    for t in range(2):
        at_i = pl.multiple_of(t * span + pairs[2 * t] * BLK, BLK)
        at_j = pl.multiple_of(t * span + pairs[2 * t + 1] * BLK, BLK)
        v = jnp.concatenate([wide[pl.ds(at_i, BLK), :], wide[pl.ds(at_j, BLK), :]], axis=0)
        parts.append(fold(dot(p_hi[t], v) + dot(p_lo[t], v)))
    low2 = low_half((2 * BLK, LANES))
    pp_now = jnp.where(low2, parts[0], parts[1])
    pp[...] = pp_now
    if scalars:
        picked = []
        for t in range(2):
            at_i = pl.multiple_of(pairs[2 * t] * BLK, BLK)
            at_j = pl.multiple_of(pairs[2 * t + 1] * BLK, BLK)
            picked.append(jnp.concatenate([whole[pl.ds(at_i, BLK), :], whole[pl.ds(at_j, BLK), :]], axis=0))
        vec = jnp.where(low2, picked[0], picked[1])
        tile = msgs[0][own : own + SC, :]
        for k in range(1, n):
            tile = tile + msgs[k][own : own + SC, :]
        tile = fold(tile)
        at = lax.broadcasted_iota(jnp.int32, (SC, LANES), 0)
        tile = jnp.where(at == 3, col_sum(vec * pp_now), tile)
        if scalars == 2:
            tile = jnp.where(at == 4, col_sum(vec * pp_first[...]), tile)
        msg[rows : rows + SC, :] = tile


def back_product(n, own, place, pairs, w, pp_now, t_hi, t_lo, total, outs, extra):
    row = place[0]
    span = total.shape[0]
    first, second = pair_up(w)
    wide = jnp.concatenate([first, second], axis=0)
    part = fold(dot(t_hi[...], wide) + dot(t_lo[...], wide))
    low = low_half((span, LANES))
    total[...] = jnp.where(low, part[:span], part[span:])
    low1 = low_half((BLK, LANES))
    for t in range(2):
        side = low1 if t == 0 else jnp.logical_not(low1)
        for e in range(2):
            at = pl.ds(pl.multiple_of(pairs[2 * t + e] * BLK, BLK), BLK)
            total[at, :] += jnp.where(side, pp_now[e * BLK : (e + 1) * BLK], 0.0)
    for k in range(n):
        at = pl.multiple_of(lax.bitwise_xor(row, k) * own, own)
        outs[k][0:own, :] = total[pl.ds(at, own), :]
        if extra is not None:
            outs[k][own : own + extra.shape[0], :] = extra


def start_back_kernel(n, nx, own, place, pairs, *refs):
    msgs, rest = refs[:nx], refs[nx:]
    z, y, pp, diag, t_hi, t_lo = rest[:6]
    outs, (ax, total) = rest[6 : 6 + n], rest[6 + n :]
    ax_now = msgs[0][...]
    for k in range(1, nx):
        ax_now = ax_now + msgs[k][...]
    ax[...] = ax_now
    w = RHO * ax_now - (RHO * z[...] - y[...])
    back_product(n, own, place, pairs, w, pp[...], t_hi, t_lo, total, outs, diag[...])


def step_back_kernel(n, nx, own, place, pairs, *refs):
    msgs, rest = refs[:nx], refs[nx:]
    pp, t_hi, t_lo = rest[:3]
    outs, (ad, scal, total) = rest[3 : 3 + n], rest[3 + n :]
    rows = ad.shape[0]
    v = msgs[0][...]
    for k in range(1, nx):
        v = v + msgs[k][...]
    ad_now = v[:rows]
    tile = v[rows:]
    ad[...] = ad_now
    scal[...] = tile
    curve = RHO * col_sum(ad_now * ad_now) + tile[3:4]
    back_product(
        n, own, place, pairs, RHO * ad_now, pp[...], t_hi, t_lo, total, outs, pack_rows(curve)
    )


def residual_kernel(n, own, first, place, *refs):
    msgs, rest = refs[:n], refs[n:]
    if first:
        x, q, pd, msg, res, dk, full = rest
        rows = msgs[0].shape[0] - own
        tile = msgs[0][own:, :]
        for k in range(1, n):
            tile = tile + msgs[k][own:, :]
        n_range = rows // 2
        low1 = low_half((BLK, LANES))
        for b in range(n_range):
            mine = jnp.broadcast_to(tile[b : b + 1], (BLK, LANES)).T
            other = jnp.broadcast_to(tile[n_range + b : n_range + b + 1], (BLK, LANES)).T
            full[b * BLK : (b + 1) * BLK, :] = jnp.where(low1, mine, other)
        at = pl.multiple_of(place[0] * own, own)
        diag = pd[...] + SIGMA + full[pl.ds(at, own), :]
        dk[...] = diag
    else:
        x, q, pd, dk, msg, res = rest
        diag = dk[...]
    total = msgs[0][0:own, :]
    for k in range(1, n):
        total = total + msgs[k][0:own, :]
    r = -q[...] - pd[...] * x[...] - total
    s = r / diag
    res[...] = r
    msg[0:own, :] = s
    shift = pd[...] + SIGMA
    rz = jnp.sum(r * s, axis=0, keepdims=True)
    dd = jnp.sum(shift * s * s, axis=0, keepdims=True)
    msg[own : own + SC, :] = pack_rows(rz, dd)


def step_kernel(n, own, *refs):
    msgs, rest = refs[:n], refs[n:]
    scal, prev, r, pd, dk, msg, step_out = rest
    total = msgs[0][...]
    for k in range(1, n):
        total = total + msgs[k][...]
    shift = pd[...] + SIGMA
    d = prev[0:own, :]
    kd = shift * d + total[:own]
    curve = total[own : own + 1] + scal[1:2, :]
    step = scal[0:1, :] / curve
    r_new = r[...] - step * kd
    s = r_new / dk[...]
    msg[0:own, :] = s
    rz = jnp.sum(r_new * s, axis=0, keepdims=True)
    ss = jnp.sum(shift * s * s, axis=0, keepdims=True)
    sd = jnp.sum(shift * s * d, axis=0, keepdims=True)
    msg[own : own + SC, :] = pack_rows(rz, ss, sd)
    step_out[...] = jnp.broadcast_to(step, step_out.shape)


def curve_kernel(nx, *refs):
    msgs, rest = refs[:nx], refs[nx:]
    scal, ad, ad2, share, keep = rest
    rows = ad.shape[0]
    v = msgs[0][...]
    for k in range(1, nx):
        v = v + msgs[k][...]
    tile = v[rows:]
    beta = tile[0:1] / scal[0:1, :]
    ad_now = v[:rows] + beta * ad[...]
    ad2[...] = ad_now
    flat = tile[1:2] + 2.0 * beta * tile[2:3] + beta * beta * scal[1:2, :]
    pair = tile[3:4] + 2.0 * beta * tile[4:5] + beta * beta * scal[3:4, :]
    share[...] = pack_rows(RHO * col_sum(ad_now * ad_now) + pair)
    keep[...] = pack_rows(tile[0:1], beta, flat)


def admm_update(n, own, refs):
    shares, rest = refs[:n], refs[n:]
    keep, step_in, ax, ad, ad2, z, y, lower, upper, x, msg1, msg2 = rest[:12]
    tile = shares[0][...]
    for k in range(1, n):
        tile = tile + shares[k][...]
    beta = keep[1:2, :]
    step1 = step_in[0:1, :]
    step2 = keep[0:1, :] / (tile[0:1] + keep[2:3, :])
    d1 = msg1[0:own, :]
    d2 = msg2[0:own, :] + beta * d1
    x_hat = x[...] + step1 * d1 + step2 * d2
    x_new = RELAX * x_hat + (1.0 - RELAX) * x[...]
    ax_hat = ax[...] + step1 * ad[...] + step2 * ad2[...]
    relaxed = RELAX * ax_hat + (1.0 - RELAX) * z[...]
    z_new = jnp.clip(relaxed + y[...] / RHO, lower[...], upper[...])
    y_new = y[...] + RHO * (relaxed - z_new)
    return beta, step1, step2, x_new, ax_hat, z_new, y_new, rest[12:]


def update_kernel(n, own, place, pairs, *refs):
    beta, step1, step2, x_new, ax_hat, z_new, y_new, rest = admm_update(n, own, refs)
    ax = refs[n + 2]
    ppx, pp1, pp2, t_hi, t_lo = rest[:5]
    outs, (x_out, z_out, y_out, ax_out, ppx_out, total) = rest[5 : 5 + n], rest[5 + n :]
    x_out[...] = x_new
    z_out[...] = z_new
    y_out[...] = y_new
    ax_new = RELAX * ax_hat + (1.0 - RELAX) * ax[...]
    ax_out[...] = ax_new
    pp_hat = ppx[...] + step1 * pp1[...] + step2 * (pp2[...] + beta * pp1[...])
    pp_new = RELAX * pp_hat + (1.0 - RELAX) * ppx[...]
    ppx_out[...] = pp_new
    w = RHO * ax_new - (RHO * z_new - y_new)
    back_product(n, own, place, pairs, w, pp_new, t_hi, t_lo, total, outs, None)


def last_kernel(n, own, *refs):
    _, _, _, x_new, _, z_new, y_new, rest = admm_update(n, own, refs)
    (out,) = rest
    rows = z_new.shape[0]
    out[0:rows, :] = z_new
    out[rows : 2 * rows, :] = y_new
    out[2 * rows :, :] = x_new


def finish_kernel(place, mine, got, x, z, y):
    core = place[1]
    rows = z.shape[0] // 2
    for k, dst in enumerate((z, y)):
        a = mine[k * rows : (k + 1) * rows, :]
        b = got[k * rows : (k + 1) * rows, :]
        low = low_half(a.shape)
        left = jnp.where(core == 0, a, b)
        right = jnp.where(core == 0, b, a)
        dst[0:rows, :] = jnp.where(low, left, turn(right))
        dst[rows : 2 * rows, :] = jnp.where(low, turn(left), right)
    a = mine[2 * rows :, :]
    b = got[2 * rows :, :]
    low = low_half(a.shape)
    x[...] = jnp.where(core == 0, jnp.where(low, a, b), jnp.where(low, turn(b), turn(a)))


def local(x_state, q_lin, p_diag, z_state, y_state, lower_bound, upper_bound, a_blocks, a_cols, p_blocks, p_pairs):
    slab, per = a_cols.shape
    n = lax.axis_size("row")
    n_col = lax.axis_size("col")
    nx = n_col // 2
    own = x_state.shape[0]
    span = own * n
    n_range = span // BLK
    slab_rows = slab * BLK
    half_rows = slab_rows // 2
    row_at = lax.axis_index("row")
    core_at = lax.axis_index("col") % 2
    place = jnp.stack([row_at, core_at]).astype(jnp.int32)

    def to_core(v):
        return lax.ppermute(v, "col", [(c, c ^ 1) for c in range(n_col)])

    def to_x(v):
        return [v] + [lax.ppermute(v, "col", [(c, c ^ (2 * k)) for c in range(n_col)]) for k in range(1, nx)]

    swaps = [2, 3, 1] if n == 4 else list(range(1, n))

    def to_row(pieces, order=None):
        got = {0: pieces[0]}
        for k in order or swaps:
            got[k] = lax.ppermute(pieces[k], "row", [(i, i ^ k) for i in range(n)])
        return [got[k] for k in range(n)]

    def to_all_rows(v):
        return to_row([v] * n, swaps[::-1])

    a_mine = a_blocks.reshape(slab * per, BLK, BLK)
    p_mine = p_blocks.reshape(4, BLK, BLK)
    ints = jnp.concatenate([a_cols.reshape(-1), p_pairs.reshape(-1)])
    x_rows = to_all_rows(x_state)
    a_other = to_core(a_mine)
    ints_other = to_core(ints)
    p_other = to_core(p_mine)
    pd_other = to_core(p_diag)
    count = slab * per
    cols = jnp.concatenate([ints[:count], ints_other[:count]])
    pairs = jnp.concatenate([ints[count:], ints_other[count:]])
    pd = jnp.concatenate(
        [jnp.broadcast_to(p_diag[:, None], (own, HALF)), jnp.broadcast_to(pd_other[:, None], (own, HALF))], axis=1
    )
    x_others = [to_core(v) for v in x_rows]
    x, q = call(own_kernel, [((own, LANES), F32)] * 2, [x_state, x_others[0], q_lin, to_core(q_lin)], [place])
    z, y, lower, upper = call(
        slab_kernel, [((half_rows, LANES), F32)] * 4, [z_state, y_state, lower_bound, upper_bound], [place]
    )
    wide = 2 * span
    a_hi, a_lo, t_hi, t_lo, p_hi, p_lo, diag = call(
        functools.partial(prep_kernel, slab, per),
        [((slab_rows, wide), BF16)] * 2
        + [((wide, slab_rows), BF16)] * 2
        + [((2, 2 * BLK, 2 * BLK), BF16)] * 2
        + [((2 * n_range, LANES), F32)],
        [a_mine, a_other, p_mine, p_other],
        [cols, pairs],
        flops=10**8,
    )
    prod_flops = 4 * slab_rows * wide * LANES
    total_scratch = [pltpu.VMEM((span, LANES), F32)]

    def forward(msgs, scalars, pp_first=()):
        extra = SC if scalars else 0
        return call(
            functools.partial(forward_kernel, n, own, scalars),
            [((half_rows + extra, LANES), F32), ((2 * BLK, LANES), F32)],
            [*msgs, a_hi, a_lo, p_hi, p_lo, *pp_first],
            [place, pairs],
            total_scratch + [pltpu.VMEM((wide, LANES), BF16)],
            flops=prod_flops,
        )

    msg, ppx = forward(x_rows + x_others, 0)
    *pieces, ax = call(
        functools.partial(start_back_kernel, n, nx, own),
        [((own + 2 * n_range, LANES), F32)] * n + [((half_rows, LANES), F32)],
        [*to_x(msg), z, y, ppx, diag, t_hi, t_lo],
        [place, pairs],
        total_scratch,
        flops=prod_flops,
    )
    own_shape = ((own, LANES), F32)
    msg_shape = ((own + SC, LANES), F32)
    tile_shape = ((SC, LANES), F32)
    slab_shape = ((half_rows, LANES), F32)
    for outer in range(ADMM_ITERS):
        if outer == 0:
            msg1, r, dk = call(
                functools.partial(residual_kernel, n, own, True),
                [msg_shape, own_shape, own_shape],
                [*to_row(pieces), x, q, pd],
                [place],
                total_scratch,
            )
        else:
            msg1, r = call(
                functools.partial(residual_kernel, n, own, False),
                [msg_shape, own_shape],
                [*to_row(pieces), x, q, pd, dk],
                [place],
            )
        msg, pp1 = forward(to_all_rows(msg1), 1)
        *pieces, ad, scal = call(
            functools.partial(step_back_kernel, n, nx, own),
            [msg_shape] * n + [slab_shape, tile_shape],
            [*to_x(msg), pp1, t_hi, t_lo],
            [place, pairs],
            total_scratch,
            flops=prod_flops,
        )
        msg2, step = call(
            functools.partial(step_kernel, n, own),
            [msg_shape, tile_shape],
            [*to_row(pieces), scal, msg1, r, pd, dk],
        )
        msg, pp2 = forward(to_all_rows(msg2), 2, (pp1,))
        ad2, share, keep = call(
            functools.partial(curve_kernel, nx),
            [slab_shape, tile_shape, tile_shape],
            [*to_x(msg), scal, ad],
        )
        shares = to_all_rows(share)
        state = [*shares, keep, step, ax, ad, ad2, z, y, lower, upper, x, msg1, msg2]
        if outer + 1 < ADMM_ITERS:
            *pieces, x, z, y, ax, ppx = call(
                functools.partial(update_kernel, n, own),
                [own_shape] * n + [own_shape, slab_shape, slab_shape, slab_shape, ((2 * BLK, LANES), F32)],
                [*state, ppx, pp1, pp2, t_hi, t_lo],
                [place, pairs],
                total_scratch,
                flops=prod_flops,
            )
        else:
            (out,) = call(
                functools.partial(last_kernel, n, own), [((2 * half_rows + own, LANES), F32)], state
            )
    return call(
        finish_kernel,
        [own_shape, ((slab_rows, LANES), F32), ((slab_rows, LANES), F32)],
        [out, to_core(out)],
        [place],
    )


def solution(mesh):
    placed = (
        P(("col", "row"), "grp"),
        P(("col", "row"), "grp"),
        P(("col", "row")),
        P("row", "grp"),
        P("row", "grp"),
        P("row", "grp"),
        P("row", "grp"),
        P("row", "col", None, None),
        P("row", "col"),
        P("col", "row", None, None),
        P("col", "row", None),
    )

    def run(*args):
        return tuple(local(*args))

    return jax.shard_map(
        run,
        mesh=mesh,
        in_specs=placed,
        out_specs=(P(("col", "row"), "grp"), P("row", "grp"), P("row", "grp")),
        check_vma=False,
    )
```

```python
import functools

import jax
import jax.numpy as jnp
from jax import lax
from jax.experimental import pallas as pl
from jax.experimental.pallas import tpu as pltpu
from jax.sharding import PartitionSpec as P

ADMM_ITERS = 2
RHO = 0.5
SIGMA = 1e-06
RELAX = 1.6
BLK = 128
LANES = 128
HALF = 64
SC = 8
F32 = jnp.float32
BF16 = jnp.bfloat16

VMEM = pl.BlockSpec(memory_space=pltpu.VMEM)
SMEM = pl.BlockSpec(memory_space=pltpu.SMEM)


def call(body, outs, ins, smem=(), scratch=(), flops=0):
    n_bytes = sum(v.size * v.dtype.itemsize for v in ins)
    return pl.pallas_call(
        body,
        out_shape=[jax.ShapeDtypeStruct(s, d) for s, d in outs],
        in_specs=[SMEM] * len(smem) + [VMEM] * len(ins),
        out_specs=[VMEM] * len(outs),
        scratch_shapes=list(scratch),
        compiler_params=pltpu.CompilerParams(vmem_limit_bytes=30 * 1024 * 1024),
        cost_estimate=pl.CostEstimate(flops=flops, bytes_accessed=n_bytes, transcendentals=0),
    )(*smem, *ins)


def low_half(shape):
    return lax.broadcasted_iota(jnp.int32, shape, 1) < HALF


def turn(v):
    return pltpu.roll(v, HALF, 1)


def fold(v):
    return v + turn(v)


def col_sum(v):
    return fold(jnp.sum(v, axis=0, keepdims=True))


def split_bf16(v):
    hi = v.astype(BF16).astype(F32)
    return hi, v - hi


def pair_up(v):
    hi, lo = split_bf16(v)
    low = low_half(v.shape)
    first = jnp.where(low, hi, turn(lo)).astype(BF16)
    second = jnp.where(low, turn(hi), lo).astype(BF16)
    return first, second


def dot(a, b):
    return jnp.dot(a, b, preferred_element_type=F32)


def pack_rows(*rows):
    at = lax.broadcasted_iota(jnp.int32, (SC, LANES), 0)
    tile = jnp.zeros((SC, LANES), F32)
    for k, row in enumerate(rows):
        tile = jnp.where(at == k, row, tile)
    return tile


def pick(near, a, b):
    low = low_half(a.shape)
    return jnp.where(low, jnp.where(near == 0, a, turn(a)), jnp.where(near == 0, turn(b), b))


def pack_kernel(place, x, q, z, y, lower, upper, same, diff, zy, bounds):
    mine = place[1]
    theirs = 1 - mine
    same[...] = pick(mine, x[...], q[...])
    diff[...] = pick(theirs, x[...], q[...])
    zy[...] = pick(theirs, z[...], y[...])
    bounds[...] = pick(theirs, lower[...], upper[...])


def gather_kernel(n, own, place, *refs):
    msgs, (x, q, full) = refs[:n], refs[n:]
    half = x.shape[0]
    for k in range(n):
        at = pl.multiple_of(lax.bitwise_xor(place[0], k) * own, own)
        full[pl.ds(at, own), :] = msgs[k][...]
    first, second = full[0:half, :], full[half:, :]
    low = low_half(first.shape)
    x[...] = jnp.where(low, first, turn(second))
    q[...] = jnp.where(low, turn(first), second)


def slab_kernel(place, a, b, got, a_out, b_out):
    mine = place[1]
    low = low_half(a.shape)
    av = jnp.where(mine == 0, a[...], turn(a[...]))
    bv = jnp.where(mine == 0, b[...], turn(b[...]))
    a_out[...] = jnp.where(low, av, turn(got[...]))
    b_out[...] = jnp.where(low, bv, got[...])


def prep_kernel(slab, per, cols, pairs, a_mine, a_other, p_mine, p_other, a_hi, a_lo, t_hi, t_lo, p_hi, p_lo, diag):
    for ref in (a_hi, a_lo, t_hi, t_lo):
        ref[...] = jnp.zeros(ref.shape, BF16)
    diag[...] = jnp.zeros(diag.shape, F32)
    for t, src in enumerate((a_mine, a_other)):
        for m in range(slab):
            rows = slice((t * slab + m) * BLK, (t * slab + m + 1) * BLK)
            for s in range(per):
                k = m * per + s
                col = cols[t * slab * per + k]
                at = pl.multiple_of(col * BLK, BLK)
                block = src[k]
                hi, lo = split_bf16(block)
                a_hi[rows, pl.ds(at, BLK)] = hi.astype(BF16)
                a_lo[rows, pl.ds(at, BLK)] = lo.astype(BF16)
                hi, lo = split_bf16(block.T)
                t_hi[pl.ds(at, BLK), rows] = hi.astype(BF16)
                t_lo[pl.ds(at, BLK), rows] = lo.astype(BF16)
                diag[pl.ds(col, 1), :] += RHO * jnp.sum(block * block, axis=0, keepdims=True)
    shape = (BLK, BLK)
    eye = lax.broadcasted_iota(jnp.int32, shape, 0) == lax.broadcasted_iota(jnp.int32, shape, 1)
    for t, src in enumerate((p_mine, p_other)):
        for e in range(4):
            hi, lo = split_bf16(src[e])
            rows = slice((e // 2) * BLK, (e // 2 + 1) * BLK)
            lanes = slice((e % 2) * BLK, (e % 2 + 1) * BLK)
            p_hi[t, rows, lanes] = hi.astype(BF16)
            p_lo[t, rows, lanes] = lo.astype(BF16)
        for e in range(2):
            here = pl.ds(pairs[2 * t + e], 1)
            diag[here, :] += jnp.sum(jnp.where(eye, src[3 * e], 0.0), axis=0, keepdims=True)


def forward(pairs, vec, mats, wide, msg, pp, tile=None, pp_first=None):
    a_hi, a_lo, p_hi, p_lo = mats
    half = vec.shape[0]
    first, second = pair_up(vec)
    wide[0:half, :] = first
    wide[half:, :] = second
    x = wide[...]
    total = fold(dot(a_hi[...], x) + dot(a_lo[...], x))
    rows = total.shape[0] // 2
    msg[0:rows, :] = jnp.where(low_half((rows, LANES)), total[:rows], total[rows:])
    parts, picked = [], []
    for t in range(2):
        at_i = pl.multiple_of(pairs[2 * t] * BLK, BLK)
        at_j = pl.multiple_of(pairs[2 * t + 1] * BLK, BLK)
        v = jnp.concatenate([wide[pl.ds(at_i, BLK), :], wide[pl.ds(at_j, BLK), :]], axis=0)
        parts.append(fold(dot(p_hi[t], v) + dot(p_lo[t], v)))
        picked.append(fold(v.astype(F32)))
    low2 = low_half((2 * BLK, LANES))
    pp_now = jnp.where(low2, parts[0], parts[1])
    pp[...] = pp_now
    if tile is not None:
        at = lax.broadcasted_iota(jnp.int32, (SC, LANES), 0)
        here = jnp.where(low2, picked[0], picked[1])
        tile = jnp.where(at == 3, col_sum(here * pp_now), tile)
        if pp_first is not None:
            tile = jnp.where(at == 4, col_sum(here * pp_first), tile)
        msg[rows : rows + SC, :] = tile


def backward(pairs, w, pp_now, t_hi, t_lo, full, out, extra=()):
    half = full.shape[0] // 2
    wide = jnp.concatenate(pair_up(w), axis=0)
    full[...] = fold(dot(t_hi[...], wide) + dot(t_lo[...], wide))
    turned = turn(pp_now)
    low2 = low_half(pp_now.shape)
    for t in range(2):
        both = jnp.where(low2, pp_now, turned) if t == 0 else jnp.where(low2, turned, pp_now)
        for e in range(2):
            at = pl.ds(pl.multiple_of(pairs[2 * t + e] * BLK, BLK), BLK)
            full[at, :] += both[e * BLK : (e + 1) * BLK]
    out[0:half, :] = jnp.where(low_half((half, LANES)), full[0:half, :], full[half:, :])
    at = half
    for rows in extra:
        out[at : at + rows.shape[0], :] = rows
        at += rows.shape[0]


def add_kernel(a, b, out):
    out[...] = a[...] + b[...]


def first_kernel(pairs, x, a_hi, a_lo, p_hi, p_lo, msg, pp, wide):
    forward(pairs, x[...], (a_hi, a_lo, p_hi, p_lo), wide, msg, pp)


def start_back_kernel(pairs, m1, m2, z, y, pp, diag, pd, t_hi, t_lo, out, ax, full):
    ax_now = m1[...] + m2[...]
    ax[...] = ax_now
    w = RHO * ax_now - (RHO * z[...] - y[...])
    backward(pairs, w, pp[...], t_hi, t_lo, full, out, (diag[...], pd[...]))


def step_back_kernel(pairs, m1, m2, pp, t_hi, t_lo, out, ad, scal, full):
    rows = ad.shape[0]
    ad_now = m1[0:rows, :] + m2[0:rows, :]
    tile = m1[rows:, :] + m2[rows:, :]
    ad[...] = ad_now
    scal[...] = tile
    curve = RHO * col_sum(ad_now * ad_now) + tile[3:4]
    backward(pairs, RHO * ad_now, pp[...], t_hi, t_lo, full, out, (pack_rows(curve),))


def to_columns(tile):
    half = tile.shape[0] // 2
    low = low_half((BLK, LANES))
    blocks = []
    for b in range(half):
        first = jnp.broadcast_to(tile[b : b + 1], (BLK, LANES)).T
        second = jnp.broadcast_to(tile[half + b : half + b + 1], (BLK, LANES)).T
        blocks.append(jnp.where(low, first, second))
    return jnp.concatenate(blocks, axis=0)


def residual_kernel(fresh, pairs, m1, m2, x, q, *refs):
    half = x.shape[0]
    if fresh:
        mats, (msg, pp, s_out, res, pd_out, dk_out, wide) = refs[:4], refs[4:]
        n_range = (m1.shape[0] - half) // 2
        pd = to_columns(m1[half + n_range :, :] + m2[half + n_range :, :])
        dk = pd + SIGMA + to_columns(m1[half : half + n_range, :] + m2[half : half + n_range, :])
        pd_out[...] = pd
        dk_out[...] = dk
    else:
        pd, dk = refs[0][...], refs[1][...]
        mats, (msg, pp, s_out, res, wide) = refs[2:6], refs[6:]
    total = m1[0:half, :] + m2[0:half, :]
    r = -q[...] - pd * x[...] - total
    s = r / dk
    res[...] = r
    s_out[...] = s
    tile = pack_rows(col_sum(r * s), col_sum((pd + SIGMA) * s * s))
    forward(pairs, s, mats, wide, msg, pp, tile)


def step_kernel(pairs, m1, m2, scal, d_in, r, pd, dk, pp_first, a_hi, a_lo, p_hi, p_lo, msg, pp, s_out, step_out, wide):
    half = d_in.shape[0]
    shift = pd[...] + SIGMA
    d = d_in[...]
    kd = shift * d + (m1[0:half, :] + m2[0:half, :])
    curve = m1[half : half + 1, :] + m2[half : half + 1, :] + scal[1:2, :]
    step = scal[0:1, :] / curve
    r_new = r[...] - step * kd
    s = r_new / dk[...]
    s_out[...] = s
    step_out[...] = jnp.broadcast_to(step, step_out.shape)
    tile = pack_rows(col_sum(r_new * s), col_sum(shift * s * s), col_sum(shift * s * d))
    forward(pairs, s, (a_hi, a_lo, p_hi, p_lo), wide, msg, pp, tile, pp_first[...])


def curve_kernel(m1, m2, scal, ad, ad2, share, keep):
    rows = ad.shape[0]
    tile = m1[rows:, :] + m2[rows:, :]
    beta = tile[0:1] / scal[0:1, :]
    ad_now = m1[0:rows, :] + m2[0:rows, :] + beta * ad[...]
    ad2[...] = ad_now
    flat = tile[1:2] + 2.0 * beta * tile[2:3] + beta * beta * scal[1:2, :]
    pair = tile[3:4] + 2.0 * beta * tile[4:5] + beta * beta * scal[3:4, :]
    share[...] = pack_rows(RHO * col_sum(ad_now * ad_now) + pair)
    keep[...] = pack_rows(tile[0:1], beta, flat)


def admm_update(s1, s2, keep, step_in, ax, ad, ad2, z, y, lower, upper, x, d1_in, s2_in):
    beta = keep[1:2, :]
    step1 = step_in[0:1, :]
    step2 = keep[0:1, :] / (s1[0:1, :] + s2[0:1, :] + keep[2:3, :])
    d1 = d1_in[...]
    d2 = s2_in[...] + beta * d1
    x_hat = x[...] + step1 * d1 + step2 * d2
    x_new = RELAX * x_hat + (1.0 - RELAX) * x[...]
    ax_hat = ax[...] + step1 * ad[...] + step2 * ad2[...]
    relaxed = RELAX * ax_hat + (1.0 - RELAX) * z[...]
    z_new = jnp.clip(relaxed + y[...] / RHO, lower[...], upper[...])
    y_new = y[...] + RHO * (relaxed - z_new)
    return beta, step1, step2, x_new, ax_hat, z_new, y_new


def update_kernel(pairs, *refs):
    state, rest = refs[:14], refs[14:]
    ppx, pp1, pp2, t_hi, t_lo, out, x_out, z_out, y_out, ax_out, ppx_out, full = rest
    beta, step1, step2, x_new, ax_hat, z_new, y_new = admm_update(*state)
    ax = state[4]
    x_out[...] = x_new
    z_out[...] = z_new
    y_out[...] = y_new
    ax_new = RELAX * ax_hat + (1.0 - RELAX) * ax[...]
    ax_out[...] = ax_new
    pp_hat = ppx[...] + step1 * pp1[...] + step2 * (pp2[...] + beta * pp1[...])
    pp_new = RELAX * pp_hat + (1.0 - RELAX) * ppx[...]
    ppx_out[...] = pp_new
    w = RHO * ax_new - (RHO * z_new - y_new)
    backward(pairs, w, pp_new, t_hi, t_lo, full, out)


def last_kernel(own, place, *refs):
    state, (send, z_out, y_out, x_out, full) = refs[:14], refs[14:]
    _, _, _, x_new, _, z_new, y_new = admm_update(*state)
    rows, half = z_new.shape[0], x_new.shape[0]
    low = low_half(x_new.shape)
    full[0:half, :] = jnp.where(low, x_new, turn(x_new))
    full[half:, :] = jnp.where(low, turn(x_new), x_new)
    z_out[...] = z_new
    y_out[...] = y_new
    x_out[...] = full[pl.ds(pl.multiple_of(place[0] * own, own), own), :]
    low = low_half(z_new.shape)
    send[0:rows, :] = jnp.where(low, turn(z_new), y_new)
    at = pl.multiple_of(lax.bitwise_xor(place[0], 1) * own, own)
    part = full[pl.ds(at, own), :]
    send[rows:, :] = jnp.where(low_half((own // 2, LANES)), part[: own // 2], part[own // 2 :])


def finish_kernel(place, z_in, y_in, x_in, got, x, z, y):
    mine = place[1]
    rows = z.shape[0]
    low = low_half(z.shape)
    zy = got[0:rows, :]
    z_other = jnp.where(low, zy, turn(zy))
    y_other = jnp.where(low, turn(zy), zy)
    side = jnp.where(low, 0, 1) == mine
    z_mine = jnp.where(low, z_in[...], turn(z_in[...]))
    y_mine = jnp.where(low, y_in[...], turn(y_in[...]))
    z[...] = jnp.where(side, z_mine, z_other)
    y[...] = jnp.where(side, y_mine, y_other)
    part = got[rows:, :]
    low = low_half(part.shape)
    n_half = part.shape[0]
    side = jnp.where(low, 0, 1) == mine
    x[0:n_half, :] = jnp.where(side, x_in[0:n_half, :], jnp.where(low, part, turn(part)))
    x[n_half:, :] = jnp.where(side, x_in[n_half:, :], jnp.where(low, turn(part), part))


def local(x_state, q_lin, p_diag, z_state, y_state, lower_bound, upper_bound, a_blocks, a_cols, p_blocks, p_pairs):
    slab, per = a_cols.shape
    n = lax.axis_size("row")
    n_col = lax.axis_size("col")
    own = x_state.shape[0]
    span = own * n
    half = span // 2
    n_range = span // BLK
    slab_rows = slab * BLK
    wide_rows = 2 * slab_rows
    row_at = lax.axis_index("row").astype(jnp.int32)
    place = jnp.stack([row_at, row_at % 2])

    def swap(v, axis, size, mask):
        return lax.ppermute(v, axis, [(i, i ^ mask) for i in range(size)])

    def to_partner(v):
        return swap(v, "row", n, 1)

    def reduce_over(v, axis, size, mask):
        while mask * 2 < size:
            (v,) = call(add_kernel, [(v.shape, F32)], [v, swap(v, axis, size, mask)])
            mask *= 2
        return [v, swap(v, axis, size, mask)]

    def over_col(v):
        return reduce_over(v, "col", n_col, 1)

    def over_row(v):
        return reduce_over(v, "row", n, 2)

    a_mine = a_blocks.reshape(slab * per, BLK, BLK)
    p_mine = p_blocks.reshape(4, BLK, BLK)
    a_other = to_partner(a_mine)
    p_other = to_partner(p_mine)
    ints = jnp.concatenate([a_cols.reshape(-1), p_pairs.reshape(-1)])
    ints_other = to_partner(ints)
    pd_other = to_partner(p_diag)
    count = slab * per
    cols = jnp.concatenate([ints[:count], ints_other[:count]])
    pairs = jnp.concatenate([ints[count:], ints_other[count:]])
    pd_rows = jnp.zeros((span,), F32)
    pd_rows = lax.dynamic_update_slice(pd_rows, p_diag, (row_at * own,))
    pd_rows = lax.dynamic_update_slice(pd_rows, pd_other, ((row_at ^ 1) * own,))
    pd_rows = pd_rows.reshape(n_range, BLK)
    own_shape = ((own, LANES), F32)
    vec_shape = ((half, LANES), F32)
    slab_shape = ((slab_rows, LANES), F32)
    tile_shape = ((SC, LANES), F32)
    pp_shape = ((2 * BLK, LANES), F32)
    same, diff, zy, bounds = call(
        pack_kernel,
        [own_shape, own_shape, slab_shape, slab_shape],
        [x_state, q_lin, z_state, y_state, lower_bound, upper_bound],
        [place],
    )
    swaps = [2, 3, 1] if n == 4 else list(range(1, n))
    got = {k: swap(diff if k % 2 else same, "row", n, k) for k in swaps}
    x, q = call(
        functools.partial(gather_kernel, n, own),
        [vec_shape, vec_shape],
        [same] + [got[k] for k in range(1, n)],
        [place],
        [pltpu.VMEM((span, LANES), F32)],
    )
    z, y = call(slab_kernel, [slab_shape] * 2, [z_state, y_state, to_partner(zy)], [place])
    lower, upper = call(slab_kernel, [slab_shape] * 2, [lower_bound, upper_bound, to_partner(bounds)], [place])
    *mats, t_hi, t_lo, p_hi, p_lo, diag = call(
        functools.partial(prep_kernel, slab, per),
        [((wide_rows, span), BF16)] * 2
        + [((span, wide_rows), BF16)] * 2
        + [((2, 2 * BLK, 2 * BLK), BF16)] * 2
        + [((n_range, LANES), F32)],
        [a_mine, a_other, p_mine, p_other],
        [cols, pairs],
        flops=10**8,
    )
    mats = [*mats, p_hi, p_lo]
    backs = [t_hi, t_lo]
    flops = 4 * span * wide_rows * LANES
    wide = [pltpu.VMEM((span, LANES), BF16)]
    full = [pltpu.VMEM((span, LANES), F32)]
    msg_shape = ((slab_rows + SC, LANES), F32)

    msg, ppx = call(first_kernel, [slab_shape, pp_shape], [x, *mats], [pairs], wide, flops)
    part, ax = call(
        start_back_kernel,
        [((half + 2 * n_range, LANES), F32), slab_shape],
        [*over_col(msg), z, y, ppx, diag, pd_rows, *backs],
        [pairs],
        full,
        flops,
    )
    for outer in range(ADMM_ITERS):
        if outer == 0:
            msg, pp1, d1, r, pd, dk = call(
                functools.partial(residual_kernel, True),
                [msg_shape, pp_shape] + [vec_shape] * 4,
                [*over_row(part), x, q, *mats],
                [pairs],
                wide,
                flops,
            )
        else:
            msg, pp1, d1, r = call(
                functools.partial(residual_kernel, False),
                [msg_shape, pp_shape, vec_shape, vec_shape],
                [*over_row(part), x, q, pd, dk, *mats],
                [pairs],
                wide,
                flops,
            )
        part, ad, scal = call(
            step_back_kernel,
            [((half + SC, LANES), F32), slab_shape, tile_shape],
            [*over_col(msg), pp1, *backs],
            [pairs],
            full,
            flops,
        )
        msg, pp2, s2, step = call(
            step_kernel,
            [msg_shape, pp_shape, vec_shape, tile_shape],
            [*over_row(part), scal, d1, r, pd, dk, pp1, *mats],
            [pairs],
            wide,
            flops,
        )
        ad2, share, keep = call(
            curve_kernel, [slab_shape, tile_shape, tile_shape], [*over_col(msg), scal, ad]
        )
        state = [*over_row(share), keep, step, ax, ad, ad2, z, y, lower, upper, x, d1, s2]
        if outer + 1 < ADMM_ITERS:
            part, x, z, y, ax, ppx = call(
                update_kernel,
                [vec_shape, vec_shape, slab_shape, slab_shape, slab_shape, pp_shape],
                [*state, ppx, pp1, pp2, *backs],
                [pairs],
                full,
                flops,
            )
        else:
            send, z, y, x = call(
                functools.partial(last_kernel, own),
                [((slab_rows + own // 2, LANES), F32), slab_shape, slab_shape, own_shape],
                state,
                [place],
                full,
            )
    return call(finish_kernel, [own_shape, slab_shape, slab_shape], [z, y, x, to_partner(send)], [place])


def solution(mesh):
    placed = (
        P(("col", "row"), "grp"),
        P(("col", "row"), "grp"),
        P(("col", "row")),
        P("row", "grp"),
        P("row", "grp"),
        P("row", "grp"),
        P("row", "grp"),
        P("row", "col", None, None),
        P("row", "col"),
        P("col", "row", None, None),
        P("col", "row", None),
    )

    def run(*args):
        return tuple(local(*args))

    return jax.shard_map(
        run,
        mesh=mesh,
        in_specs=placed,
        out_specs=(P(("col", "row"), "grp"), P("row", "grp"), P("row", "grp")),
        check_vma=False,
    )
```

```python
import functools

import jax
import jax.numpy as jnp
from jax import lax
from jax.experimental import pallas as pl
from jax.experimental.pallas import tpu as pltpu
from jax.sharding import PartitionSpec as P

ADMM_ITERS = 2
RHO = 0.5
SIGMA = 1e-06
RELAX = 1.6
BLK = 128
LANES = 128
HALF = 64
SC = 8
F32 = jnp.float32
BF16 = jnp.bfloat16

VMEM = pl.BlockSpec(memory_space=pltpu.VMEM)
SMEM = pl.BlockSpec(memory_space=pltpu.SMEM)
ANY = pl.BlockSpec(memory_space=pl.ANY)


def call(body, outs, ins, smem=(), scratch=(), flops=0, after=None):
    n_bytes = sum(v.size * v.dtype.itemsize for v in ins)
    tied = [] if after is None else [after]

    def run(*refs):
        body(*refs[len(tied) :])

    return pl.pallas_call(
        run,
        out_shape=[jax.ShapeDtypeStruct(s, d) for s, d in outs],
        in_specs=[ANY] * len(tied) + [SMEM] * len(smem) + [VMEM] * len(ins),
        out_specs=[VMEM] * len(outs),
        scratch_shapes=list(scratch),
        compiler_params=pltpu.CompilerParams(vmem_limit_bytes=30 * 1024 * 1024),
        cost_estimate=pl.CostEstimate(flops=flops, bytes_accessed=n_bytes, transcendentals=0),
    )(*tied, *smem, *ins)


def low_half(shape):
    return lax.broadcasted_iota(jnp.int32, shape, 1) < HALF


def turn(v):
    return pltpu.roll(v, HALF, 1)


def fold(v):
    return v + turn(v)


def col_sum(v):
    return fold(jnp.sum(v, axis=0, keepdims=True))


def split_bf16(v):
    hi = v.astype(BF16).astype(F32)
    return hi, v - hi


def pair_up(v):
    hi, lo = split_bf16(v)
    low = low_half(v.shape)
    first = jnp.where(low, hi, turn(lo)).astype(BF16)
    second = jnp.where(low, turn(hi), lo).astype(BF16)
    return first, second


def dot(a, b):
    return jnp.dot(a, b, preferred_element_type=F32)


def pack_rows(*rows):
    at = lax.broadcasted_iota(jnp.int32, (SC, LANES), 0)
    tile = jnp.zeros((SC, LANES), F32)
    for k, row in enumerate(rows):
        tile = jnp.where(at == k, row, tile)
    return tile


def add_all(refs, rows=None):
    total = refs[0][...] if rows is None else refs[0][rows]
    for ref in refs[1:]:
        total = total + (ref[...] if rows is None else ref[rows])
    return total


def half_of(part, v):
    rows = v.shape[0] // 2
    first, second = v[:rows], v[rows:]
    low = low_half(first.shape)
    if part == 0:
        return jnp.where(low, first, turn(second))
    return jnp.where(low, turn(first), second)


def join_halves(a, b, out):
    rows = a.shape[0]
    low = low_half(a.shape)
    out[0:rows, :] = jnp.where(low, a, turn(b))
    out[rows:, :] = jnp.where(low, turn(a), b)


def side_by_side(v):
    rows = v.shape[0] // 2
    return jnp.where(low_half((rows, LANES)), v[:rows], v[rows:])


def cut_kernel(*refs):
    count = len(refs) // 3
    for k in range(count):
        v = refs[k][...]
        refs[count + 2 * k][...] = half_of(0, v)
        refs[count + 2 * k + 1][...] = half_of(1, v)


def prep_kernel(slab, per, cols, pairs, a_in, p_in, a_hi, a_lo, t_hi, t_lo, p_hi, p_lo, diag):
    for ref in (a_hi, a_lo, t_hi, t_lo):
        ref[...] = jnp.zeros(ref.shape, BF16)
    diag[...] = jnp.zeros(diag.shape, F32)
    for m in range(slab):
        rows = slice(m * BLK, (m + 1) * BLK)
        for s in range(per):
            k = m * per + s
            col = cols[k]
            at = pl.multiple_of(col * BLK, BLK)
            block = a_in[k]
            hi, lo = split_bf16(block)
            a_hi[rows, pl.ds(at, BLK)] = hi.astype(BF16)
            a_lo[rows, pl.ds(at, BLK)] = lo.astype(BF16)
            hi, lo = split_bf16(block.T)
            t_hi[pl.ds(at, BLK), rows] = hi.astype(BF16)
            t_lo[pl.ds(at, BLK), rows] = lo.astype(BF16)
            diag[pl.ds(col, 1), :] += RHO * jnp.sum(block * block, axis=0, keepdims=True)
    shape = (BLK, BLK)
    eye = lax.broadcasted_iota(jnp.int32, shape, 0) == lax.broadcasted_iota(jnp.int32, shape, 1)
    for e in range(4):
        hi, lo = split_bf16(p_in[e])
        rows = slice((e // 2) * BLK, (e // 2 + 1) * BLK)
        lanes = slice((e % 2) * BLK, (e % 2 + 1) * BLK)
        p_hi[rows, lanes] = hi.astype(BF16)
        p_lo[rows, lanes] = lo.astype(BF16)
    for e in range(2):
        diag[pl.ds(pairs[e], 1), :] += jnp.sum(jnp.where(eye, p_in[3 * e], 0.0), axis=0, keepdims=True)


def forward(pairs, mats, wide, msg, pp, tile=None, pp_first=None):
    a_hi, a_lo, p_hi, p_lo = mats
    x = wide[...]
    total = fold(dot(a_hi[...], x) + dot(a_lo[...], x))
    rows = total.shape[0] // 2
    msg[0:rows, :] = side_by_side(total)
    at_i = pl.ds(pl.multiple_of(pairs[0] * BLK, BLK), BLK)
    at_j = pl.ds(pl.multiple_of(pairs[1] * BLK, BLK), BLK)
    v = jnp.concatenate([wide[at_i, :], wide[at_j, :]], axis=0)
    pp_now = side_by_side(fold(dot(p_hi[...], v) + dot(p_lo[...], v)))
    pp[...] = pp_now
    if tile is not None:
        at = lax.broadcasted_iota(jnp.int32, (SC, LANES), 0)
        here = side_by_side(fold(v.astype(F32)))
        tile = jnp.where(at == 3, col_sum(here * pp_now), tile)
        if pp_first is not None:
            tile = jnp.where(at == 4, col_sum(here * pp_first), tile)
        msg[rows : rows + SC, :] = tile


def first_kernel(n, own, part, place, pairs, *refs):
    msgs, (a_hi, a_lo, p_hi, p_lo, msg, pp, wide) = refs[:n], refs[n:]
    for k in range(n):
        at = pl.multiple_of(lax.bitwise_xor(place[0], k) * own, own)
        wide[pl.ds(at, own), :] = pair_up(msgs[k][...])[part]
    forward(pairs, (a_hi, a_lo, p_hi, p_lo), wide, msg, pp)


def next_kernel(n, oh, second, place, pairs, *refs):
    msgs, mats, rest = refs[:n], refs[n : n + 4], refs[n + 4 :]
    pp_first = None
    if second:
        pp_first, rest = rest[0][...], rest[1:]
    msg, pp, wide = rest
    for k in range(n):
        at = pl.multiple_of(lax.bitwise_xor(place[0], k) * (2 * oh), oh)
        a, b = pair_up(msgs[k][0:oh, :])
        wide[pl.ds(at, oh), :] = a
        wide[pl.ds(pl.multiple_of(at + oh, oh), oh), :] = b
    tile = add_all(msgs, slice(oh, oh + SC))
    forward(pairs, mats, wide, msg, pp, tile, pp_first)


def backward(n, oh, place, pairs, w, pp_now, t_hi, t_lo, full, outs, extra=None):
    wide = jnp.concatenate(pair_up(w), axis=0)
    full[...] = fold(dot(t_hi[...], wide) + dot(t_lo[...], wide))
    turned = turn(pp_now)
    low = low_half(pp_now.shape)
    at_i = pl.ds(pl.multiple_of(pairs[0] * BLK, BLK), BLK)
    at_j = pl.ds(pl.multiple_of(pairs[1] * BLK, BLK), BLK)
    full[at_i, :] += jnp.where(low, pp_now, turned)
    full[at_j, :] += jnp.where(low, turned, pp_now)
    for k in range(n):
        at = pl.multiple_of(lax.bitwise_xor(place[0], k) * (2 * oh), oh)
        outs[k][0:oh, :] = side_by_side(full[pl.ds(at, 2 * oh), :])
        if extra is not None:
            outs[k][oh : oh + extra.shape[0], :] = extra


def add_kernel(a, b, out):
    out[...] = a[...] + b[...]


def start_back_kernel(n, oh, lead, place, pairs, m1, m2, z, y, pp, t_hi, t_lo, *rest):
    extra = None
    if lead:
        extra, rest = rest[0][...], rest[1:]
    outs, (ax, full) = rest[:n], rest[n:]
    ax_now = m1[...] + m2[...]
    ax[...] = ax_now
    w = RHO * ax_now - (RHO * z[...] - y[...])
    backward(n, oh, place, pairs, w, pp[...], t_hi, t_lo, full, outs, extra)


def step_back_kernel(n, oh, place, pairs, m1, m2, pp, t_hi, t_lo, *rest):
    outs, (ad, scal, full) = rest[:n], rest[n:]
    rows = ad.shape[0]
    ad_now = m1[0:rows, :] + m2[0:rows, :]
    tile = m1[rows:, :] + m2[rows:, :]
    ad[...] = ad_now
    scal[...] = tile
    curve = RHO * col_sum(ad_now * ad_now) + tile[3:4]
    backward(n, oh, place, pairs, RHO * ad_now, pp[...], t_hi, t_lo, full, outs, pack_rows(curve))


def residual_kernel(n, oh, fresh, place, *refs):
    msgs, (x, q, pd, *rest) = refs[:n], refs[n:]
    if fresh:
        msg, res, dk, full = rest
        tile = add_all(msgs, slice(oh, msgs[0].shape[0]))
        for b in range(tile.shape[0]):
            full[b * BLK : (b + 1) * BLK, :] = jnp.broadcast_to(tile[b : b + 1], (BLK, LANES)).T
        at = pl.multiple_of(place[0] * (2 * oh), oh)
        diag = pd[...] + SIGMA + side_by_side(full[pl.ds(at, 2 * oh), :])
        dk[...] = diag
    else:
        dk, msg, res = rest
        diag = dk[...]
    r = -q[...] - pd[...] * x[...] - add_all(msgs, slice(0, oh))
    s = r / diag
    res[...] = r
    msg[0:oh, :] = s
    msg[oh : oh + SC, :] = pack_rows(col_sum(r * s), col_sum((pd[...] + SIGMA) * s * s))


def step_kernel(n, oh, *refs):
    msgs, (scal, prev, r, pd, dk, msg, step_out) = refs[:n], refs[n:]
    total = add_all(msgs)
    shift = pd[...] + SIGMA
    d = prev[0:oh, :]
    kd = shift * d + total[:oh]
    curve = total[oh : oh + 1] + scal[1:2, :]
    step = scal[0:1, :] / curve
    r_new = r[...] - step * kd
    s = r_new / dk[...]
    msg[0:oh, :] = s
    msg[oh : oh + SC, :] = pack_rows(col_sum(r_new * s), col_sum(shift * s * s), col_sum(shift * s * d))
    step_out[...] = jnp.broadcast_to(step, step_out.shape)


def curve_kernel(m1, m2, scal, ad, share, ad2, keep):
    rows = ad.shape[0]
    tile = m1[rows:, :] + m2[rows:, :]
    beta = tile[0:1] / scal[0:1, :]
    ad_now = m1[0:rows, :] + m2[0:rows, :] + beta * ad[...]
    ad2[...] = ad_now
    flat = tile[1:2] + 2.0 * beta * tile[2:3] + beta * beta * scal[1:2, :]
    pair = tile[3:4] + 2.0 * beta * tile[4:5] + beta * beta * scal[3:4, :]
    share[...] = pack_rows(RHO * col_sum(ad_now * ad_now) + pair)
    keep[...] = pack_rows(tile[0:1], beta, flat)


def admm_update(n, oh, refs):
    shares, rest = refs[:n], refs[n:]
    keep, step_in, ax, ad, ad2, z, y, lower, upper, x, msg1, msg2 = rest[:12]
    beta = keep[1:2, :]
    step1 = step_in[0:1, :]
    step2 = keep[0:1, :] / (add_all(shares)[0:1] + keep[2:3, :])
    d1 = msg1[0:oh, :]
    d2 = msg2[0:oh, :] + beta * d1
    x_hat = x[...] + step1 * d1 + step2 * d2
    x_new = RELAX * x_hat + (1.0 - RELAX) * x[...]
    ax_hat = ax[...] + step1 * ad[...] + step2 * ad2[...]
    relaxed = RELAX * ax_hat + (1.0 - RELAX) * z[...]
    z_new = jnp.clip(relaxed + y[...] / RHO, lower[...], upper[...])
    y_new = y[...] + RHO * (relaxed - z_new)
    return (beta, step1, step2, ax[...]), x_new, ax_hat, z_new, y_new, rest[12:]


def update_kernel(n, oh, place, pairs, *refs):
    (beta, step1, step2, ax), x_new, ax_hat, z_new, y_new, rest = admm_update(n, oh, refs)
    ppx, pp1, pp2, t_hi, t_lo = rest[:5]
    outs, (x_out, z_out, y_out, ax_out, full) = rest[5 : 5 + n], rest[5 + n :]
    x_out[...] = x_new
    z_out[...] = z_new
    y_out[...] = y_new
    ax_new = RELAX * ax_hat + (1.0 - RELAX) * ax
    ax_out[...] = ax_new
    pp_hat = ppx[...] + step1 * pp1[...] + step2 * (pp2[...] + beta * pp1[...])
    pp_new = RELAX * pp_hat + (1.0 - RELAX) * ppx[...]
    w = RHO * ax_new - (RHO * z_new - y_new)
    backward(n, oh, place, pairs, w, pp_new, t_hi, t_lo, full, outs)


def last_kernel(n, oh, *refs):
    _, x_new, _, z_new, y_new, (x_out, z_out, y_out) = admm_update(n, oh, refs)
    x_out[...] = x_new
    z_out[...] = z_new
    y_out[...] = y_new


def finish_kernel(n, oh, *refs):
    _, x_new, _, z_new, y_new, rest = admm_update(n, oh, refs)
    x_first, z_first, y_first, x_out, z_out, y_out = rest
    join_halves(x_first[...], x_new, x_out)
    join_halves(z_first[...], z_new, z_out)
    join_halves(y_first[...], y_new, y_out)


def local(x_state, q_lin, p_diag, z_state, y_state, lower_bound, upper_bound, a_blocks, a_cols, p_blocks, p_pairs):
    slab, per = a_cols.shape
    n = lax.axis_size("row")
    n_col = lax.axis_size("col")
    own = x_state.shape[0]
    oh = own // 2
    span = own * n
    n_range = span // BLK
    slab_rows = slab * BLK
    half_rows = slab_rows // 2
    place = lax.axis_index("row").astype(jnp.int32).reshape(1)

    def swap(v, axis, size, mask):
        return lax.ppermute(v, axis, [(i, i ^ mask) for i in range(size)])

    swaps = [2, 3, 1] if n == 4 else list(range(1, n))

    def to_row(pieces, order=None):
        got = {0: pieces[0]}
        for k in order or swaps:
            got[k] = swap(pieces[k], "row", n, k)
        return [got[k] for k in range(n)]

    def to_all_rows(v):
        return to_row([v] * n, swaps[::-1])

    cols = a_cols.reshape(-1)
    pairs = p_pairs.reshape(-1)
    pd = jnp.concatenate(
        [jnp.broadcast_to(p_diag[:oh, None], (oh, HALF)), jnp.broadcast_to(p_diag[oh:, None], (oh, HALF))], axis=1
    )
    own_shape = ((oh, LANES), F32)
    msg_shape = ((oh + SC, LANES), F32)
    slab_shape = ((half_rows, LANES), F32)
    out_shape = ((half_rows + SC, LANES), F32)
    tile_shape = ((SC, LANES), F32)
    pp_shape = ((BLK, LANES), F32)
    x_rows = to_all_rows(x_state)
    *mats, t_hi, t_lo, p_hi, p_lo, diag = call(
        functools.partial(prep_kernel, slab, per),
        [((slab_rows, span), BF16)] * 2
        + [((span, slab_rows), BF16)] * 2
        + [((2 * BLK, 2 * BLK), BF16)] * 2
        + [((n_range, LANES), F32)],
        [a_blocks.reshape(slab * per, BLK, BLK), p_blocks.reshape(4, BLK, BLK)],
        [cols, pairs],
        flops=10**8,
    )
    mats = [*mats, p_hi, p_lo]
    backs = [t_hi, t_lo]
    cuts = call(
        cut_kernel,
        [own_shape] * 4 + [slab_shape] * 8,
        [x_state, q_lin, z_state, y_state, lower_bound, upper_bound],
    )
    flops = 4 * span * slab_rows * LANES
    wide = [pltpu.VMEM((span, LANES), BF16)]
    full = [pltpu.VMEM((span, LANES), F32)]
    shared = {"last": None}

    def run(body, *rest, **more):
        outs = call(body, *rest, after=shared["last"], **more)
        shared["last"] = outs[0]
        return outs

    def chain(part):
        x, q, z, y, lower, upper = cuts[part::2]

        def over_col(v):
            mask = 1
            while mask * 2 < n_col:
                (v,) = run(add_kernel, [(v.shape, F32)], [v, swap(v, "col", n_col, mask)])
                mask *= 2
                yield
            return [v, swap(v, "col", n_col, mask)]

        msg, ppx = run(
            functools.partial(first_kernel, n, own, part),
            [slab_shape, pp_shape],
            [*x_rows, *mats],
            [place, pairs],
            wide,
            flops,
        )
        yield
        sums = yield from over_col(msg)
        lead = part == 0
        piece = ((oh + n_range, LANES), F32) if lead else own_shape
        *pieces, ax = run(
            functools.partial(start_back_kernel, n, oh, lead),
            [piece] * n + [slab_shape],
            [*sums, z, y, ppx, *backs] + [diag] * lead,
            [place, pairs],
            full,
            flops,
        )
        pieces = to_row(pieces)
        yield
        for outer in range(ADMM_ITERS):
            fresh = lead and outer == 0
            msg1, r, *made = run(
                functools.partial(residual_kernel, n, oh, fresh),
                [msg_shape, own_shape] + [own_shape] * fresh,
                [*pieces, x, q, pd] + ([] if fresh else [shared["dk"]]),
                [place],
                full * fresh,
            )
            if fresh:
                shared["dk"] = made[0]
            dk = shared["dk"]
            rows1 = to_all_rows(msg1)
            yield
            msg, pp1 = run(
                functools.partial(next_kernel, n, oh, False),
                [out_shape, pp_shape],
                [*rows1, *mats],
                [place, pairs],
                wide,
                flops,
            )
            yield
            sums = yield from over_col(msg)
            *pieces, ad, scal = run(
                functools.partial(step_back_kernel, n, oh),
                [msg_shape] * n + [slab_shape, tile_shape],
                [*sums, pp1, *backs],
                [place, pairs],
                full,
                flops,
            )
            pieces = to_row(pieces)
            yield
            msg2, step = run(
                functools.partial(step_kernel, n, oh),
                [msg_shape, tile_shape],
                [*pieces, scal, msg1, r, pd, dk],
            )
            rows2 = to_all_rows(msg2)
            yield
            msg, pp2 = run(
                functools.partial(next_kernel, n, oh, True),
                [out_shape, pp_shape],
                [*rows2, *mats, pp1],
                [place, pairs],
                wide,
                flops,
            )
            yield
            sums = yield from over_col(msg)
            share, ad2, keep = run(
                curve_kernel, [tile_shape, slab_shape, tile_shape], [*sums, scal, ad]
            )
            shares = to_all_rows(share)
            yield
            state = [*shares, keep, step, ax, ad, ad2, z, y, lower, upper, x, msg1, msg2]
            if outer + 1 < ADMM_ITERS:
                *pieces, x, z, y, ax = run(
                    functools.partial(update_kernel, n, oh),
                    [own_shape] * n + [own_shape, slab_shape, slab_shape, slab_shape],
                    [*state, ppx, pp1, pp2, *backs],
                    [place, pairs],
                    full,
                    flops,
                )
                pieces = to_row(pieces)
                yield
            elif lead:
                shared["first"] = run(
                    functools.partial(last_kernel, n, oh), [own_shape, slab_shape, slab_shape], state
                )
                yield
            else:
                whole = ((slab_rows, LANES), F32)
                shared["out"] = run(
                    functools.partial(finish_kernel, n, oh),
                    [((own, LANES), F32), whole, whole],
                    [*state, *shared["first"]],
                )

    chains = [chain(0), chain(1)]
    while "out" not in shared:
        for one in chains:
            next(one, None)
    return shared["out"]


def solution(mesh):
    placed = (
        P(("col", "row"), "grp"),
        P(("col", "row"), "grp"),
        P(("col", "row")),
        P("row", "grp"),
        P("row", "grp"),
        P("row", "grp"),
        P("row", "grp"),
        P("row", "col", None, None),
        P("row", "col"),
        P("col", "row", None, None),
        P("col", "row", None),
    )

    def run(*args):
        return tuple(local(*args))

    return jax.shard_map(
        run,
        mesh=mesh,
        in_specs=placed,
        out_specs=(P(("col", "row"), "grp"), P("row", "grp"), P("row", "grp")),
        check_vma=False,
    )
```

```python
import functools

import jax
import jax.numpy as jnp
from jax import lax
from jax.experimental import pallas as pl
from jax.experimental.pallas import tpu as pltpu
from jax.sharding import PartitionSpec as P

ADMM_ITERS = 2
RHO = 0.5
SIGMA = 1e-06
RELAX = 1.6
BLK = 128
LANES = 128
HALF = 64
SC = 8
F32 = jnp.float32
BF16 = jnp.bfloat16

VMEM = pl.BlockSpec(memory_space=pltpu.VMEM)
SMEM = pl.BlockSpec(memory_space=pltpu.SMEM)


def call(body, outs, ins, smem=(), scratch=(), flops=0):
    n_bytes = sum(v.size * v.dtype.itemsize for v in ins)
    return pl.pallas_call(
        body,
        out_shape=[jax.ShapeDtypeStruct(s, d) for s, d in outs],
        in_specs=[SMEM] * len(smem) + [VMEM] * len(ins),
        out_specs=[VMEM] * len(outs),
        scratch_shapes=list(scratch),
        compiler_params=pltpu.CompilerParams(vmem_limit_bytes=30 * 1024 * 1024),
        cost_estimate=pl.CostEstimate(flops=flops, bytes_accessed=n_bytes, transcendentals=0),
    )(*smem, *ins)


def low_half(shape):
    return lax.broadcasted_iota(jnp.int32, shape, 1) < HALF


def turn(v):
    return pltpu.roll(v, HALF, 1)


def fold(v):
    return v + turn(v)


def col_sum(v):
    return fold(jnp.sum(v, axis=0, keepdims=True))


def split_bf16(v):
    hi = v.astype(BF16).astype(F32)
    return hi, v - hi


def pair_up(v):
    hi, lo = split_bf16(v)
    low = low_half(v.shape)
    first = jnp.where(low, hi, turn(lo)).astype(BF16)
    second = jnp.where(low, turn(hi), lo).astype(BF16)
    return first, second


def dot(a, b):
    return jnp.dot(a, b, preferred_element_type=F32)


def pack_rows(*rows):
    at = lax.broadcasted_iota(jnp.int32, (SC, LANES), 0)
    tile = jnp.zeros((SC, LANES), F32)
    for k, row in enumerate(rows):
        tile = jnp.where(at == k, row, tile)
    return tile


def mix_cores(core, mine, other):
    low = low_half(mine.shape)
    a = jnp.where(core == 0, mine, turn(mine))
    b = jnp.where(core == 0, turn(other), other)
    return jnp.where(low, a, b)


def own_kernel(place, x, x_other, q, q_other, x_own, q_own):
    core = place[1]
    x_own[...] = mix_cores(core, x[...], x_other[...])
    q_own[...] = mix_cores(core, q[...], q_other[...])


def slab_kernel(place, *refs):
    core = place[1]
    count = len(refs) // 2
    for src, dst in zip(refs[:count], refs[count:]):
        rows = dst.shape[0]
        v = jnp.where(core == 0, src[...], turn(src[...]))
        dst[...] = jnp.where(low_half(dst.shape), v[:rows], turn(v[rows:]))


def flip_of(place, n_half):
    return place[2] * n_half


def prep_kernel(slab, per, place, cols, pairs, a_mine, a_other, p_mine, p_other, *outs):
    near, far, (p_hi, p_lo, diag) = outs[:4], outs[4:8], outs[8:]
    span = near[0].shape[1]
    n_half = span // 2 // BLK
    n_range = 2 * n_half
    for ref in outs[:8]:
        ref[...] = jnp.zeros(ref.shape, BF16)
    diag[...] = jnp.zeros(diag.shape, F32)
    for t, src in enumerate((a_mine, a_other)):
        for m in range(slab):
            rows = slice(m * BLK, (m + 1) * BLK)
            for s in range(per):
                k = m * per + s
                col = cols[t * slab * per + k]
                spot = lax.bitwise_xor(col, flip_of(place, n_half))
                at = pl.multiple_of((t * n_half + lax.rem(spot, n_half)) * BLK, BLK)
                block = src[k]
                hi, lo = split_bf16(block)
                hi_t, lo_t = split_bf16(block.T)
                values = [v.astype(BF16) for v in (hi, lo, hi_t, lo_t)]

                def store(refs, at=at, rows=rows, values=values):
                    refs[0][rows, pl.ds(at, BLK)] = values[0]
                    refs[1][rows, pl.ds(at, BLK)] = values[1]
                    refs[2][pl.ds(at, BLK), rows] = values[2]
                    refs[3][pl.ds(at, BLK), rows] = values[3]

                pl.when(spot < n_half)(functools.partial(store, near))
                pl.when(spot >= n_half)(functools.partial(store, far))
                here = pl.ds(t * n_range + col, 1)
                diag[here, :] += RHO * jnp.sum(block * block, axis=0, keepdims=True)
    shape = (BLK, BLK)
    eye = lax.broadcasted_iota(jnp.int32, shape, 0) == lax.broadcasted_iota(jnp.int32, shape, 1)
    for t, src in enumerate((p_mine, p_other)):
        for e in range(4):
            hi, lo = split_bf16(src[e])
            rows = slice((e // 2) * BLK, (e // 2 + 1) * BLK)
            lanes = slice((e % 2) * BLK, (e % 2 + 1) * BLK)
            p_hi[t, rows, lanes] = hi.astype(BF16)
            p_lo[t, rows, lanes] = lo.astype(BF16)
        for e in range(2):
            here = pl.ds(t * n_range + pairs[2 * t + e], 1)
            diag[here, :] += jnp.sum(jnp.where(eye, src[3 * e], 0.0), axis=0, keepdims=True)


def place_pieces(own, place, ks, msgs, others, wide, base):
    half = wide.shape[0] // 2 if base is None else base
    start = 0 if base is None else 2 * base
    for k, msg in zip(ks, msgs):
        v = msg[0:own, :]
        if others:
            v = mix_cores(place[1], v, others[ks.index(k)][...])
        at = pl.multiple_of(lax.rem(lax.bitwise_xor(place[0], k) * own, half), own)
        first, second = pair_up(v)
        wide[pl.ds(start + at, own), :] = first
        wide[pl.ds(pl.multiple_of(start + half + at, own), own), :] = second


def near_kernel(n, own, raw, place, *refs):
    m = n // 2
    msgs, rest = refs[:m], refs[m:]
    others = ()
    if raw:
        others, rest = rest[:m], rest[m:]
    a_hi, a_lo, part, wide = rest
    place_pieces(own, place, list(range(m)), msgs, others, wide, None)
    x = wide[...]
    part[...] = dot(a_hi[...], x) + dot(a_lo[...], x)


def forward_kernel(n, own, scalars, place, pairs, *refs):
    m = n // 2
    raw = scalars == 0
    msgs, rest = refs[:m], refs[m:]
    if raw:
        others, rest = rest[:m], rest[m:]
    else:
        others, near_msgs, rest = (), rest[:m], rest[m:]
    part, near_wide, a_hi, a_lo, p_hi, p_lo = rest[:6]
    rest = rest[6:]
    if scalars == 2:
        pp_first, rest = rest[0], rest[1:]
    msg, pp, wide = rest
    half = wide.shape[0] // 4
    n_half = half // BLK
    wide[0 : 2 * half, :] = near_wide[...]
    place_pieces(own, place, list(range(m, n)), msgs, others, wide, half)
    x = wide[2 * half :, :]
    total = fold(part[...] + dot(a_hi[...], x) + dot(a_lo[...], x))
    rows = total.shape[0] // 2
    msg[0:rows, :] = jnp.where(low_half((rows, LANES)), total[:rows], total[rows:])
    parts, picked = [], []
    for t in range(2):
        blocks = []
        for e in range(2):
            spot = lax.bitwise_xor(pairs[2 * t + e], flip_of(place, n_half))
            at = ((spot // n_half) * 2 + t) * half + lax.rem(spot, n_half) * BLK
            blocks.append(wide[pl.ds(pl.multiple_of(at, BLK), BLK), :])
        v = jnp.concatenate(blocks, axis=0)
        parts.append(fold(dot(p_hi[t], v) + dot(p_lo[t], v)))
        picked.append(fold(v.astype(F32)))
    low2 = low_half((2 * BLK, LANES))
    pp_now = jnp.where(low2, parts[0], parts[1])
    pp[...] = pp_now
    if scalars:
        vec = jnp.where(low2, picked[0], picked[1])
        tile = jnp.zeros((SC, LANES), F32)
        for ref in (*near_msgs, *msgs):
            tile = tile + ref[own : own + SC, :]
        tile = fold(tile)
        at = lax.broadcasted_iota(jnp.int32, (SC, LANES), 0)
        tile = jnp.where(at == 3, col_sum(vec * pp_now), tile)
        if scalars == 2:
            tile = jnp.where(at == 4, col_sum(vec * pp_first[...]), tile)
        msg[rows : rows + SC, :] = tile


def back_product(own, side, place, pairs, w, pp_now, t_hi, t_lo, total, outs, extra):
    half = total.shape[0]
    n_half = half // BLK
    if w.shape[0] == t_hi.shape[1]:
        wide = w
    else:
        wide = jnp.concatenate(pair_up(w), axis=0)
    part = fold(dot(t_hi[...], wide) + dot(t_lo[...], wide))
    total[...] = jnp.where(low_half((half, LANES)), part[:half], part[half:])
    low1 = low_half((BLK, LANES))
    for t in range(2):
        lanes = low1 if t == 0 else jnp.logical_not(low1)
        for e in range(2):
            spot = lax.bitwise_xor(pairs[2 * t + e], flip_of(place, n_half))
            wanted = jnp.logical_and(lanes, spot // n_half == side)
            at = pl.ds(pl.multiple_of(lax.rem(spot, n_half) * BLK, BLK), BLK)
            total[at, :] += jnp.where(wanted, pp_now[e * BLK : (e + 1) * BLK], 0.0)
    m = len(outs)
    for k, out in enumerate(outs):
        at = lax.rem(lax.bitwise_xor(place[0], k + side * m) * own, half)
        out[0:own, :] = total[pl.ds(pl.multiple_of(at, own), own), :]
        if extra is not None:
            out[own : own + extra.shape[0], :] = extra


def near_back_kernel(own, place, pairs, w, pp, extra, t_hi, t_lo, *rest):
    outs, total = rest[:-1], rest[-1]
    more = extra[...] if outs[0].shape[0] > own else None
    back_product(own, 0, place, pairs, w[...], pp[...], t_hi, t_lo, total, outs, more)


def start_back_kernel(n, nx, own, place, pairs, *refs):
    msgs, rest = refs[:nx], refs[nx:]
    z, y, pp, diag, t_hi, t_lo = rest[:6]
    outs, (ax, wide, total) = rest[6 : 6 + n // 2], rest[6 + n // 2 :]
    ax_now = msgs[0][...]
    for k in range(1, nx):
        ax_now = ax_now + msgs[k][...]
    ax[...] = ax_now
    w = jnp.concatenate(pair_up(RHO * ax_now - (RHO * z[...] - y[...])), axis=0)
    wide[...] = w
    back_product(own, 1, place, pairs, w, pp[...], t_hi, t_lo, total, outs, diag[...])


def step_back_kernel(n, nx, own, place, pairs, *refs):
    msgs, rest = refs[:nx], refs[nx:]
    pp, t_hi, t_lo = rest[:3]
    outs, (ad, scal, share, wide, total) = rest[3 : 3 + n // 2], rest[3 + n // 2 :]
    rows = ad.shape[0]
    v = msgs[0][...]
    for k in range(1, nx):
        v = v + msgs[k][...]
    ad_now = v[:rows]
    tile = v[rows:]
    ad[...] = ad_now
    scal[...] = tile
    extra = pack_rows(RHO * col_sum(ad_now * ad_now) + tile[3:4])
    share[...] = extra
    w = jnp.concatenate(pair_up(RHO * ad_now), axis=0)
    wide[...] = w
    back_product(own, 1, place, pairs, w, pp[...], t_hi, t_lo, total, outs, extra)


def residual_kernel(n, own, first, place, *refs):
    msgs, rest = refs[:n], refs[n:]
    if first:
        x, q, pd, msg, res, dk, full = rest
        rows = msgs[0].shape[0] - own
        tile = msgs[0][own:, :]
        for k in range(1, n):
            tile = tile + msgs[k][own:, :]
        n_range = rows // 2
        low1 = low_half((BLK, LANES))
        for b in range(n_range):
            mine = jnp.broadcast_to(tile[b : b + 1], (BLK, LANES)).T
            other = jnp.broadcast_to(tile[n_range + b : n_range + b + 1], (BLK, LANES)).T
            full[b * BLK : (b + 1) * BLK, :] = jnp.where(low1, mine, other)
        at = pl.multiple_of(place[0] * own, own)
        diag = pd[...] + SIGMA + full[pl.ds(at, own), :]
        dk[...] = diag
    else:
        x, q, pd, dk, msg, res = rest
        diag = dk[...]
    total = msgs[0][0:own, :]
    for k in range(1, n):
        total = total + msgs[k][0:own, :]
    r = -q[...] - pd[...] * x[...] - total
    s = r / diag
    res[...] = r
    msg[0:own, :] = s
    shift = pd[...] + SIGMA
    rz = jnp.sum(r * s, axis=0, keepdims=True)
    dd = jnp.sum(shift * s * s, axis=0, keepdims=True)
    msg[own : own + SC, :] = pack_rows(rz, dd)


def step_kernel(n, own, *refs):
    msgs, rest = refs[:n], refs[n:]
    scal, prev, r, pd, dk, msg, step_out = rest
    total = msgs[0][...]
    for k in range(1, n):
        total = total + msgs[k][...]
    shift = pd[...] + SIGMA
    d = prev[0:own, :]
    kd = shift * d + total[:own]
    curve = total[own : own + 1] + scal[1:2, :]
    step = scal[0:1, :] / curve
    r_new = r[...] - step * kd
    s = r_new / dk[...]
    msg[0:own, :] = s
    rz = jnp.sum(r_new * s, axis=0, keepdims=True)
    ss = jnp.sum(shift * s * s, axis=0, keepdims=True)
    sd = jnp.sum(shift * s * d, axis=0, keepdims=True)
    msg[own : own + SC, :] = pack_rows(rz, ss, sd)
    step_out[...] = jnp.broadcast_to(step, step_out.shape)


def curve_kernel(nx, *refs):
    msgs, rest = refs[:nx], refs[nx:]
    scal, ad, ad2, share, keep = rest
    rows = ad.shape[0]
    v = msgs[0][...]
    for k in range(1, nx):
        v = v + msgs[k][...]
    tile = v[rows:]
    beta = tile[0:1] / scal[0:1, :]
    ad_now = v[:rows] + beta * ad[...]
    ad2[...] = ad_now
    flat = tile[1:2] + 2.0 * beta * tile[2:3] + beta * beta * scal[1:2, :]
    pair = tile[3:4] + 2.0 * beta * tile[4:5] + beta * beta * scal[3:4, :]
    share[...] = pack_rows(RHO * col_sum(ad_now * ad_now) + pair)
    keep[...] = pack_rows(tile[0:1], beta, flat)


def admm_update(n, own, refs):
    shares, rest = refs[:n], refs[n:]
    keep, step_in, ax, ad, ad2, z, y, lower, upper, x, msg1, msg2 = rest[:12]
    tile = shares[0][...]
    for k in range(1, n):
        tile = tile + shares[k][...]
    beta = keep[1:2, :]
    step1 = step_in[0:1, :]
    step2 = keep[0:1, :] / (tile[0:1] + keep[2:3, :])
    d1 = msg1[0:own, :]
    d2 = msg2[0:own, :] + beta * d1
    x_hat = x[...] + step1 * d1 + step2 * d2
    x_new = RELAX * x_hat + (1.0 - RELAX) * x[...]
    ax_hat = ax[...] + step1 * ad[...] + step2 * ad2[...]
    relaxed = RELAX * ax_hat + (1.0 - RELAX) * z[...]
    z_new = jnp.clip(relaxed + y[...] / RHO, lower[...], upper[...])
    y_new = y[...] + RHO * (relaxed - z_new)
    return beta, step1, step2, x_new, ax_hat, z_new, y_new, rest[12:]


def update_kernel(n, own, place, pairs, *refs):
    beta, step1, step2, x_new, ax_hat, z_new, y_new, rest = admm_update(n, own, refs)
    ax = refs[n + 2]
    ppx, pp1, pp2, t_hi, t_lo = rest[:5]
    m = n // 2
    outs, (x_out, z_out, y_out, ax_out, ppx_out, wide, total) = rest[5 : 5 + m], rest[5 + m :]
    x_out[...] = x_new
    z_out[...] = z_new
    y_out[...] = y_new
    ax_new = RELAX * ax_hat + (1.0 - RELAX) * ax[...]
    ax_out[...] = ax_new
    pp_hat = ppx[...] + step1 * pp1[...] + step2 * (pp2[...] + beta * pp1[...])
    pp_new = RELAX * pp_hat + (1.0 - RELAX) * ppx[...]
    ppx_out[...] = pp_new
    w = jnp.concatenate(pair_up(RHO * ax_new - (RHO * z_new - y_new)), axis=0)
    wide[...] = w
    back_product(own, 1, place, pairs, w, pp_new, t_hi, t_lo, total, outs, None)


def last_kernel(n, own, *refs):
    _, _, _, x_new, _, z_new, y_new, rest = admm_update(n, own, refs)
    (out,) = rest
    rows = z_new.shape[0]
    out[0:rows, :] = z_new
    out[rows : 2 * rows, :] = y_new
    out[2 * rows :, :] = x_new


def finish_kernel(place, mine, got, x, z, y):
    core = place[1]
    rows = z.shape[0] // 2
    for k, dst in enumerate((z, y)):
        a = mine[k * rows : (k + 1) * rows, :]
        b = got[k * rows : (k + 1) * rows, :]
        low = low_half(a.shape)
        left = jnp.where(core == 0, a, b)
        right = jnp.where(core == 0, b, a)
        dst[0:rows, :] = jnp.where(low, left, turn(right))
        dst[rows : 2 * rows, :] = jnp.where(low, turn(left), right)
    a = mine[2 * rows :, :]
    b = got[2 * rows :, :]
    low = low_half(a.shape)
    x[...] = jnp.where(core == 0, jnp.where(low, a, b), jnp.where(low, turn(b), turn(a)))


def local(x_state, q_lin, p_diag, z_state, y_state, lower_bound, upper_bound, a_blocks, a_cols, p_blocks, p_pairs):
    slab, per = a_cols.shape
    n = lax.axis_size("row")
    n_col = lax.axis_size("col")
    nx = n_col // 2
    own = x_state.shape[0]
    span = own * n
    n_range = span // BLK
    slab_rows = slab * BLK
    half_rows = slab_rows // 2
    row_at = lax.axis_index("row")
    core_at = lax.axis_index("col") % 2
    place = jnp.stack([row_at, core_at, row_at // (n // 2)]).astype(jnp.int32)

    def to_core(v):
        return lax.ppermute(v, "col", [(c, c ^ 1) for c in range(n_col)])

    def to_x(v):
        return [v] + [lax.ppermute(v, "col", [(c, c ^ (2 * k)) for c in range(n_col)]) for k in range(1, nx)]

    m = n // 2

    def to_row(pieces, ks):
        return [lax.ppermute(v, "row", [(i, i ^ k) for i in range(n)]) for v, k in zip(pieces, ks)]

    def to_all_rows(v):
        ks = list(range(n - 1, 0, -1))
        return [v] + to_row([v] * (n - 1), ks)[::-1]

    a_mine = a_blocks.reshape(slab * per, BLK, BLK)
    p_mine = p_blocks.reshape(4, BLK, BLK)
    ints = jnp.concatenate([a_cols.reshape(-1), p_pairs.reshape(-1)])
    x_rows = to_all_rows(x_state)
    a_other = to_core(a_mine)
    ints_other = to_core(ints)
    p_other = to_core(p_mine)
    pd_other = to_core(p_diag)
    count = slab * per
    cols = jnp.concatenate([ints[:count], ints_other[:count]])
    pairs = jnp.concatenate([ints[count:], ints_other[count:]])
    pd = jnp.concatenate(
        [jnp.broadcast_to(p_diag[:, None], (own, HALF)), jnp.broadcast_to(pd_other[:, None], (own, HALF))], axis=1
    )
    z, y, lower, upper = call(
        slab_kernel, [((half_rows, LANES), F32)] * 4, [z_state, y_state, lower_bound, upper_bound], [place]
    )
    sides = [((slab_rows, span), BF16)] * 2 + [((span, slab_rows), BF16)] * 2
    *halves, p_hi, p_lo, diag = call(
        functools.partial(prep_kernel, slab, per),
        sides * 2 + [((2, 2 * BLK, 2 * BLK), BF16)] * 2 + [((2 * n_range, LANES), F32)],
        [a_mine, a_other, p_mine, p_other],
        [place, cols, pairs],
        flops=10**8,
    )
    near_a, near_t, far_a, far_t = halves[0:2], halves[2:4], halves[4:6], halves[6:8]
    *late, diag = lax.optimization_barrier((*x_rows[m:], diag))
    x_rows = [*x_rows[:m], *late]
    x_others = [to_core(v) for v in x_rows]
    x, q = call(own_kernel, [((own, LANES), F32)] * 2, [x_state, x_others[0], q_lin, to_core(q_lin)], [place])
    prod_flops = 2 * slab_rows * 2 * span * LANES
    total_scratch = [pltpu.VMEM((span // 2, LANES), F32)]

    def forward(msgs, scalars, pp_first=(), others=()):
        extra = SC if scalars else 0
        part, near_wide = call(
            functools.partial(near_kernel, n, own, scalars == 0),
            [((slab_rows, LANES), F32), ((span, LANES), BF16)],
            [*msgs[:m], *others[:m], *near_a],
            [place],
            flops=prod_flops,
        )
        return call(
            functools.partial(forward_kernel, n, own, scalars),
            [((half_rows + extra, LANES), F32), ((2 * BLK, LANES), F32)],
            [*msgs[m:], *(msgs[:m] if scalars else others[m:]), part, near_wide, *far_a, p_hi, p_lo, *pp_first],
            [place, pairs],
            [pltpu.VMEM((2 * span, LANES), BF16)],
            flops=prod_flops,
        )

    def backward(far_pieces, w, pp, extra):
        got = to_row(far_pieces, range(m, n))
        shape = far_pieces[0].shape
        near = call(
            functools.partial(near_back_kernel, own),
            [(shape, F32)] * m,
            [w, pp, extra, *near_t],
            [place, pairs],
            total_scratch,
            flops=prod_flops,
        )
        return [near[0], *to_row(near[1:], range(1, m)), *got]

    msg, ppx = forward(x_rows, 0, (), x_others)
    w_shape = ((slab_rows, LANES), BF16)
    *pieces, ax, w = call(
        functools.partial(start_back_kernel, n, nx, own),
        [((own + 2 * n_range, LANES), F32)] * m + [((half_rows, LANES), F32), w_shape],
        [*to_x(msg), z, y, ppx, diag, *far_t],
        [place, pairs],
        total_scratch,
        flops=prod_flops,
    )
    pieces = backward(pieces, w, ppx, diag)
    own_shape = ((own, LANES), F32)
    msg_shape = ((own + SC, LANES), F32)
    tile_shape = ((SC, LANES), F32)
    slab_shape = ((half_rows, LANES), F32)
    for outer in range(ADMM_ITERS):
        if outer == 0:
            msg1, r, dk = call(
                functools.partial(residual_kernel, n, own, True),
                [msg_shape, own_shape, own_shape],
                [*pieces, x, q, pd],
                [place],
                [pltpu.VMEM((span, LANES), F32)],
            )
        else:
            msg1, r = call(
                functools.partial(residual_kernel, n, own, False),
                [msg_shape, own_shape],
                [*pieces, x, q, pd, dk],
                [place],
            )
        msg, pp1 = forward(to_all_rows(msg1), 1)
        *pieces, ad, scal, curve, w = call(
            functools.partial(step_back_kernel, n, nx, own),
            [msg_shape] * m + [slab_shape, tile_shape, tile_shape, w_shape],
            [*to_x(msg), pp1, *far_t],
            [place, pairs],
            total_scratch,
            flops=prod_flops,
        )
        msg2, step = call(
            functools.partial(step_kernel, n, own),
            [msg_shape, tile_shape],
            [*backward(pieces, w, pp1, curve), scal, msg1, r, pd, dk],
        )
        msg, pp2 = forward(to_all_rows(msg2), 2, (pp1,))
        ad2, share, keep = call(
            functools.partial(curve_kernel, nx),
            [slab_shape, tile_shape, tile_shape],
            [*to_x(msg), scal, ad],
        )
        shares = to_all_rows(share)
        state = [*shares, keep, step, ax, ad, ad2, z, y, lower, upper, x, msg1, msg2]
        if outer + 1 < ADMM_ITERS:
            *pieces, x, z, y, ax, ppx, w = call(
                functools.partial(update_kernel, n, own),
                [own_shape] * m + [own_shape, slab_shape, slab_shape, slab_shape, ((2 * BLK, LANES), F32), w_shape],
                [*state, ppx, pp1, pp2, *far_t],
                [place, pairs],
                total_scratch,
                flops=prod_flops,
            )
            pieces = backward(pieces, w, ppx, share)
        else:
            (out,) = call(
                functools.partial(last_kernel, n, own), [((2 * half_rows + own, LANES), F32)], state
            )
    return call(
        finish_kernel,
        [own_shape, ((slab_rows, LANES), F32), ((slab_rows, LANES), F32)],
        [out, to_core(out)],
        [place],
    )


def solution(mesh):
    placed = (
        P(("col", "row"), "grp"),
        P(("col", "row"), "grp"),
        P(("col", "row")),
        P("row", "grp"),
        P("row", "grp"),
        P("row", "grp"),
        P("row", "grp"),
        P("row", "col", None, None),
        P("row", "col"),
        P("col", "row", None, None),
        P("col", "row", None),
    )

    def run(*args):
        return tuple(local(*args))

    return jax.shard_map(
        run,
        mesh=mesh,
        in_specs=placed,
        out_specs=(P(("col", "row"), "grp"), P("row", "grp"), P("row", "grp")),
        check_vma=False,
    )
```

```python
import functools

import jax
import jax.numpy as jnp
from jax import lax
from jax.experimental import pallas as pl
from jax.experimental.pallas import tpu as pltpu
from jax.sharding import PartitionSpec as P

ADMM_ITERS = 2
RHO = 0.5
SIGMA = 1e-06
RELAX = 1.6
BLK = 128
LANES = 128
HALF = 64
SC = 8
F32 = jnp.float32
BF16 = jnp.bfloat16

VMEM = pl.BlockSpec(memory_space=pltpu.VMEM)
SMEM = pl.BlockSpec(memory_space=pltpu.SMEM)


def call(body, outs, ins, smem=(), scratch=(), flops=0):
    n_bytes = sum(v.size * v.dtype.itemsize for v in ins)
    return pl.pallas_call(
        body,
        out_shape=[jax.ShapeDtypeStruct(s, d) for s, d in outs],
        in_specs=[SMEM] * len(smem) + [VMEM] * len(ins),
        out_specs=[VMEM] * len(outs),
        scratch_shapes=list(scratch),
        compiler_params=pltpu.CompilerParams(vmem_limit_bytes=30 * 1024 * 1024),
        cost_estimate=pl.CostEstimate(flops=flops, bytes_accessed=n_bytes, transcendentals=0),
    )(*smem, *ins)


def low_half(shape):
    return lax.broadcasted_iota(jnp.int32, shape, 1) < HALF


def turn(v):
    return pltpu.roll(v, HALF, 1)


def fold(v):
    return v + turn(v)


def col_sum(v):
    return fold(jnp.sum(v, axis=0, keepdims=True))


def split_bf16(v):
    hi = v.astype(BF16).astype(F32)
    return hi, v - hi


def pair_up(v):
    hi, lo = split_bf16(v)
    low = low_half(v.shape)
    first = jnp.where(low, hi, turn(lo)).astype(BF16)
    second = jnp.where(low, turn(hi), lo).astype(BF16)
    return first, second


def dot(a, b):
    return jnp.dot(a, b, preferred_element_type=F32)


def pack_rows(*rows):
    at = lax.broadcasted_iota(jnp.int32, (SC, LANES), 0)
    tile = jnp.zeros((SC, LANES), F32)
    for k, row in enumerate(rows):
        tile = jnp.where(at == k, row, tile)
    return tile


def mix_cores(core, mine, other):
    low = low_half(mine.shape)
    a = jnp.where(core == 0, mine, turn(mine))
    b = jnp.where(core == 0, turn(other), other)
    return jnp.where(low, a, b)


def own_kernel(place, x, x_other, q, q_other, x_own, q_own):
    core = place[1]
    x_own[...] = mix_cores(core, x[...], x_other[...])
    q_own[...] = mix_cores(core, q[...], q_other[...])


def slab_kernel(place, *refs):
    core = place[1]
    count = len(refs) // 2
    for src, dst in zip(refs[:count], refs[count:]):
        rows = dst.shape[0]
        v = jnp.where(core == 0, src[...], turn(src[...]))
        dst[...] = jnp.where(low_half(dst.shape), v[:rows], turn(v[rows:]))


def prep_kernel(slab, per, cols, pairs, a_mine, a_other, p_mine, p_other, a_hi, a_lo, t_hi, t_lo, p_hi, p_lo, diag):
    span = a_hi.shape[1] // 2
    n_range = span // BLK
    for ref in (a_hi, a_lo, t_hi, t_lo):
        ref[...] = jnp.zeros(ref.shape, BF16)
    diag[...] = jnp.zeros(diag.shape, F32)
    for t, src in enumerate((a_mine, a_other)):
        for m in range(slab):
            rows = slice(m * BLK, (m + 1) * BLK)
            for s in range(per):
                k = m * per + s
                col = cols[t * slab * per + k]
                at = pl.multiple_of(t * span + col * BLK, BLK)
                block = src[k]
                hi, lo = split_bf16(block)
                a_hi[rows, pl.ds(at, BLK)] = hi.astype(BF16)
                a_lo[rows, pl.ds(at, BLK)] = lo.astype(BF16)
                hi, lo = split_bf16(block.T)
                t_hi[pl.ds(at, BLK), rows] = hi.astype(BF16)
                t_lo[pl.ds(at, BLK), rows] = lo.astype(BF16)
                here = pl.ds(t * n_range + col, 1)
                diag[here, :] += RHO * jnp.sum(block * block, axis=0, keepdims=True)
    shape = (BLK, BLK)
    eye = lax.broadcasted_iota(jnp.int32, shape, 0) == lax.broadcasted_iota(jnp.int32, shape, 1)
    for t, src in enumerate((p_mine, p_other)):
        for e in range(4):
            hi, lo = split_bf16(src[e])
            rows = slice((e // 2) * BLK, (e // 2 + 1) * BLK)
            lanes = slice((e % 2) * BLK, (e % 2 + 1) * BLK)
            p_hi[t, rows, lanes] = hi.astype(BF16)
            p_lo[t, rows, lanes] = lo.astype(BF16)
        for e in range(2):
            here = pl.ds(t * n_range + pairs[2 * t + e], 1)
            diag[here, :] += jnp.sum(jnp.where(eye, src[3 * e], 0.0), axis=0, keepdims=True)


def forward_kernel(ks, own, scalars, place, pairs, *refs):
    n = len(ks)
    msgs, rest = refs[:n], refs[n:]
    if scalars == 0:
        others, rest = rest[:n], rest[n:]
    a_hi, a_lo, p_hi, p_lo = rest[:4]
    rest = rest[4:]
    if scalars == 2:
        pp_first, rest = rest[0], rest[1:]
    msg, pp, whole, wide = rest
    row = place[0]
    span = whole.shape[0]
    for i, k in enumerate(ks):
        at = pl.multiple_of(lax.bitwise_xor(row, k) * own, own)
        v = msgs[i][0:own, :]
        if scalars == 0:
            v = mix_cores(place[1], v, others[i][...])
        whole[pl.ds(at, own), :] = v
        first, second = pair_up(v)
        wide[pl.ds(at, own), :] = first
        wide[pl.ds(pl.multiple_of(span + at, own), own), :] = second
    x = wide[...]
    total = fold(dot(a_hi[...], x) + dot(a_lo[...], x))
    rows = total.shape[0] // 2
    msg[0:rows, :] = jnp.where(low_half((rows, LANES)), total[:rows], total[rows:])
    parts = []
    for t in range(2):
        at_i = pl.multiple_of(t * span + pairs[2 * t] * BLK, BLK)
        at_j = pl.multiple_of(t * span + pairs[2 * t + 1] * BLK, BLK)
        v = jnp.concatenate([wide[pl.ds(at_i, BLK), :], wide[pl.ds(at_j, BLK), :]], axis=0)
        parts.append(fold(dot(p_hi[t], v) + dot(p_lo[t], v)))
    low2 = low_half((2 * BLK, LANES))
    pp_now = jnp.where(low2, parts[0], parts[1])
    pp[...] = pp_now
    if scalars:
        picked = []
        for t in range(2):
            at_i = pl.multiple_of(pairs[2 * t] * BLK, BLK)
            at_j = pl.multiple_of(pairs[2 * t + 1] * BLK, BLK)
            picked.append(jnp.concatenate([whole[pl.ds(at_i, BLK), :], whole[pl.ds(at_j, BLK), :]], axis=0))
        vec = jnp.where(low2, picked[0], picked[1])
        tile = msgs[0][own : own + SC, :]
        for k in range(1, n):
            tile = tile + msgs[k][own : own + SC, :]
        tile = fold(tile)
        at = lax.broadcasted_iota(jnp.int32, (SC, LANES), 0)
        tile = jnp.where(at == 3, col_sum(vec * pp_now), tile)
        if scalars == 2:
            tile = jnp.where(at == 4, col_sum(vec * pp_first[...]), tile)
        msg[rows : rows + SC, :] = tile


def back_product(n, own, place, pairs, w, pp_now, t_hi, t_lo, total, outs, extra):
    row = place[0]
    span = total.shape[0]
    first, second = pair_up(w)
    wide = jnp.concatenate([first, second], axis=0)
    part = fold(dot(t_hi[...], wide) + dot(t_lo[...], wide))
    low = low_half((span, LANES))
    total[...] = jnp.where(low, part[:span], part[span:])
    low1 = low_half((BLK, LANES))
    for t in range(2):
        side = low1 if t == 0 else jnp.logical_not(low1)
        for e in range(2):
            at = pl.ds(pl.multiple_of(pairs[2 * t + e] * BLK, BLK), BLK)
            total[at, :] += jnp.where(side, pp_now[e * BLK : (e + 1) * BLK], 0.0)
    for k in range(n):
        at = pl.multiple_of(lax.bitwise_xor(row, k) * own, own)
        outs[k][0:own, :] = total[pl.ds(at, own), :]
        if extra is not None:
            outs[k][own : own + extra.shape[0], :] = extra


def start_back_kernel(n, nx, own, place, pairs, *refs):
    msgs, rest = refs[:nx], refs[nx:]
    z, y, pp, diag, t_hi, t_lo = rest[:6]
    outs, (ax, total) = rest[6 : 6 + n], rest[6 + n :]
    ax_now = msgs[0][...]
    for k in range(1, nx):
        ax_now = ax_now + msgs[k][...]
    ax[...] = ax_now
    w = RHO * ax_now - (RHO * z[...] - y[...])
    back_product(n, own, place, pairs, w, pp[...], t_hi, t_lo, total, outs, diag[...])


def step_back_kernel(n, nx, own, place, pairs, *refs):
    msgs, rest = refs[:nx], refs[nx:]
    pp, t_hi, t_lo = rest[:3]
    outs, (ad, scal, total) = rest[3 : 3 + n], rest[3 + n :]
    rows = ad.shape[0]
    v = msgs[0][...]
    for k in range(1, nx):
        v = v + msgs[k][...]
    ad_now = v[:rows]
    tile = v[rows:]
    ad[...] = ad_now
    scal[...] = tile
    curve = RHO * col_sum(ad_now * ad_now) + tile[3:4]
    back_product(
        n, own, place, pairs, RHO * ad_now, pp[...], t_hi, t_lo, total, outs, pack_rows(curve)
    )


def residual_kernel(n, own, first, place, *refs):
    msgs, rest = refs[:n], refs[n:]
    if first:
        x, q, pd, msg, res, dk, full = rest
        rows = msgs[0].shape[0] - own
        tile = msgs[0][own:, :]
        for k in range(1, n):
            tile = tile + msgs[k][own:, :]
        n_range = rows // 2
        low1 = low_half((BLK, LANES))
        for b in range(n_range):
            mine = jnp.broadcast_to(tile[b : b + 1], (BLK, LANES)).T
            other = jnp.broadcast_to(tile[n_range + b : n_range + b + 1], (BLK, LANES)).T
            full[b * BLK : (b + 1) * BLK, :] = jnp.where(low1, mine, other)
        at = pl.multiple_of(place[0] * own, own)
        diag = pd[...] + SIGMA + full[pl.ds(at, own), :]
        dk[...] = diag
    else:
        x, q, pd, dk, msg, res = rest
        diag = dk[...]
    total = msgs[0][0:own, :]
    for k in range(1, n):
        total = total + msgs[k][0:own, :]
    r = -q[...] - pd[...] * x[...] - total
    s = r / diag
    res[...] = r
    msg[0:own, :] = s
    shift = pd[...] + SIGMA
    rz = jnp.sum(r * s, axis=0, keepdims=True)
    dd = jnp.sum(shift * s * s, axis=0, keepdims=True)
    msg[own : own + SC, :] = pack_rows(rz, dd)


def step_kernel(n, own, *refs):
    msgs, rest = refs[:n], refs[n:]
    scal, prev, r, pd, dk, msg, step_out = rest
    total = msgs[0][...]
    for k in range(1, n):
        total = total + msgs[k][...]
    shift = pd[...] + SIGMA
    d = prev[0:own, :]
    kd = shift * d + total[:own]
    curve = total[own : own + 1] + scal[1:2, :]
    step = scal[0:1, :] / curve
    r_new = r[...] - step * kd
    s = r_new / dk[...]
    msg[0:own, :] = s
    rz = jnp.sum(r_new * s, axis=0, keepdims=True)
    ss = jnp.sum(shift * s * s, axis=0, keepdims=True)
    sd = jnp.sum(shift * s * d, axis=0, keepdims=True)
    msg[own : own + SC, :] = pack_rows(rz, ss, sd)
    step_out[...] = jnp.broadcast_to(step, step_out.shape)


def curve_kernel(nx, *refs):
    msgs, rest = refs[:nx], refs[nx:]
    scal, ad, ad2, share, keep = rest
    rows = ad.shape[0]
    v = msgs[0][...]
    for k in range(1, nx):
        v = v + msgs[k][...]
    tile = v[rows:]
    beta = tile[0:1] / scal[0:1, :]
    ad_now = v[:rows] + beta * ad[...]
    ad2[...] = ad_now
    flat = tile[1:2] + 2.0 * beta * tile[2:3] + beta * beta * scal[1:2, :]
    pair = tile[3:4] + 2.0 * beta * tile[4:5] + beta * beta * scal[3:4, :]
    share[...] = pack_rows(RHO * col_sum(ad_now * ad_now) + pair)
    keep[...] = pack_rows(tile[0:1], beta, flat)


def admm_update(n, own, refs):
    shares, rest = refs[:n], refs[n:]
    keep, step_in, ax, ad, ad2, z, y, lower, upper, x, msg1, msg2 = rest[:12]
    tile = shares[0][...]
    for k in range(1, n):
        tile = tile + shares[k][...]
    beta = keep[1:2, :]
    step1 = step_in[0:1, :]
    step2 = keep[0:1, :] / (tile[0:1] + keep[2:3, :])
    d1 = msg1[0:own, :]
    d2 = msg2[0:own, :] + beta * d1
    x_hat = x[...] + step1 * d1 + step2 * d2
    x_new = RELAX * x_hat + (1.0 - RELAX) * x[...]
    ax_hat = ax[...] + step1 * ad[...] + step2 * ad2[...]
    relaxed = RELAX * ax_hat + (1.0 - RELAX) * z[...]
    z_new = jnp.clip(relaxed + y[...] / RHO, lower[...], upper[...])
    y_new = y[...] + RHO * (relaxed - z_new)
    return beta, step1, step2, x_new, ax_hat, z_new, y_new, rest[12:]


def update_kernel(n, own, place, pairs, *refs):
    beta, step1, step2, x_new, ax_hat, z_new, y_new, rest = admm_update(n, own, refs)
    ax = refs[n + 2]
    ppx, pp1, pp2, t_hi, t_lo = rest[:5]
    outs, (x_out, z_out, y_out, ax_out, ppx_out, total) = rest[5 : 5 + n], rest[5 + n :]
    x_out[...] = x_new
    z_out[...] = z_new
    y_out[...] = y_new
    ax_new = RELAX * ax_hat + (1.0 - RELAX) * ax[...]
    ax_out[...] = ax_new
    pp_hat = ppx[...] + step1 * pp1[...] + step2 * (pp2[...] + beta * pp1[...])
    pp_new = RELAX * pp_hat + (1.0 - RELAX) * ppx[...]
    ppx_out[...] = pp_new
    w = RHO * ax_new - (RHO * z_new - y_new)
    back_product(n, own, place, pairs, w, pp_new, t_hi, t_lo, total, outs, None)


def last_kernel(n, own, *refs):
    _, _, _, x_new, _, z_new, y_new, rest = admm_update(n, own, refs)
    (out,) = rest
    rows = z_new.shape[0]
    out[0:rows, :] = z_new
    out[rows : 2 * rows, :] = y_new
    out[2 * rows :, :] = x_new


def finish_kernel(place, mine, got, x, z, y):
    core = place[1]
    rows = z.shape[0] // 2
    for k, dst in enumerate((z, y)):
        a = mine[k * rows : (k + 1) * rows, :]
        b = got[k * rows : (k + 1) * rows, :]
        low = low_half(a.shape)
        left = jnp.where(core == 0, a, b)
        right = jnp.where(core == 0, b, a)
        dst[0:rows, :] = jnp.where(low, left, turn(right))
        dst[rows : 2 * rows, :] = jnp.where(low, turn(left), right)
    a = mine[2 * rows :, :]
    b = got[2 * rows :, :]
    low = low_half(a.shape)
    x[...] = jnp.where(core == 0, jnp.where(low, a, b), jnp.where(low, turn(b), turn(a)))


def local(x_state, q_lin, p_diag, z_state, y_state, lower_bound, upper_bound, a_blocks, a_cols, p_blocks, p_pairs):
    slab, per = a_cols.shape
    n = lax.axis_size("row")
    n_col = lax.axis_size("col")
    nx = n_col // 2
    own = x_state.shape[0]
    span = own * n
    n_range = span // BLK
    slab_rows = slab * BLK
    half_rows = slab_rows // 2
    row_at = lax.axis_index("row")
    core_at = lax.axis_index("col") % 2
    place = jnp.stack([row_at, core_at]).astype(jnp.int32)

    def to_core(v):
        return lax.ppermute(v, "col", [(c, c ^ 1) for c in range(n_col)])

    def to_x(v):
        return [v] + [lax.ppermute(v, "col", [(c, c ^ (2 * k)) for c in range(n_col)]) for k in range(1, nx)]

    scalar_ks = list(range(1, n))
    row_ks = [2, 1, 3] if n == 4 else scalar_ks

    def over_row(v, k):
        return lax.ppermute(v, "row", [(i, i ^ k) for i in range(n)])

    def to_row(pieces):
        return [pieces[0]] + [over_row(pieces[k], k) for k in row_ks]

    def to_all_rows(v, ks):
        return [v] + [over_row(v, k) for k in ks]

    a_mine = a_blocks.reshape(slab * per, BLK, BLK)
    p_mine = p_blocks.reshape(4, BLK, BLK)
    ints = jnp.concatenate([a_cols.reshape(-1), p_pairs.reshape(-1)])
    x_rows = to_all_rows(x_state, row_ks)
    a_other = to_core(a_mine)
    ints_other = to_core(ints)
    p_other = to_core(p_mine)
    pd_other = to_core(p_diag)
    count = slab * per
    cols = jnp.concatenate([ints[:count], ints_other[:count]])
    pairs = jnp.concatenate([ints[count:], ints_other[count:]])
    pd = jnp.concatenate(
        [jnp.broadcast_to(p_diag[:, None], (own, HALF)), jnp.broadcast_to(pd_other[:, None], (own, HALF))], axis=1
    )
    z, y, lower, upper = call(
        slab_kernel, [((half_rows, LANES), F32)] * 4, [z_state, y_state, lower_bound, upper_bound], [place]
    )
    wide = 2 * span
    a_hi, a_lo, t_hi, t_lo, p_hi, p_lo, diag = call(
        functools.partial(prep_kernel, slab, per),
        [((slab_rows, wide), BF16)] * 2
        + [((wide, slab_rows), BF16)] * 2
        + [((2, 2 * BLK, 2 * BLK), BF16)] * 2
        + [((2 * n_range, LANES), F32)],
        [a_mine, a_other, p_mine, p_other],
        [cols, pairs],
        flops=10**8,
    )
    *late, diag = lax.optimization_barrier((*x_rows[1:], diag))
    x_rows = [x_state, *late]
    x_others = [to_core(v) for v in x_rows]
    x, q = call(own_kernel, [((own, LANES), F32)] * 2, [x_state, x_others[0], q_lin, to_core(q_lin)], [place])
    prod_flops = 4 * slab_rows * wide * LANES
    total_scratch = [pltpu.VMEM((span, LANES), F32)]

    def forward(msgs, scalars, pp_first=()):
        extra = SC if scalars else 0
        return call(
            functools.partial(forward_kernel, (0, *row_ks), own, scalars),
            [((half_rows + extra, LANES), F32), ((2 * BLK, LANES), F32)],
            [*msgs, a_hi, a_lo, p_hi, p_lo, *pp_first],
            [place, pairs],
            total_scratch + [pltpu.VMEM((wide, LANES), BF16)],
            flops=prod_flops,
        )

    msg, ppx = forward(x_rows + x_others, 0)
    *pieces, ax = call(
        functools.partial(start_back_kernel, n, nx, own),
        [((own + 2 * n_range, LANES), F32)] * n + [((half_rows, LANES), F32)],
        [*to_x(msg), z, y, ppx, diag, t_hi, t_lo],
        [place, pairs],
        total_scratch,
        flops=prod_flops,
    )
    own_shape = ((own, LANES), F32)
    msg_shape = ((own + SC, LANES), F32)
    tile_shape = ((SC, LANES), F32)
    slab_shape = ((half_rows, LANES), F32)
    for outer in range(ADMM_ITERS):
        if outer == 0:
            msg1, r, dk = call(
                functools.partial(residual_kernel, n, own, True),
                [msg_shape, own_shape, own_shape],
                [*to_row(pieces), x, q, pd],
                [place],
                total_scratch,
            )
        else:
            msg1, r = call(
                functools.partial(residual_kernel, n, own, False),
                [msg_shape, own_shape],
                [*to_row(pieces), x, q, pd, dk],
                [place],
            )
        msg, pp1 = forward(to_all_rows(msg1, row_ks), 1)
        *pieces, ad, scal = call(
            functools.partial(step_back_kernel, n, nx, own),
            [msg_shape] * n + [slab_shape, tile_shape],
            [*to_x(msg), pp1, t_hi, t_lo],
            [place, pairs],
            total_scratch,
            flops=prod_flops,
        )
        msg2, step = call(
            functools.partial(step_kernel, n, own),
            [msg_shape, tile_shape],
            [*to_row(pieces), scal, msg1, r, pd, dk],
        )
        msg, pp2 = forward(to_all_rows(msg2, row_ks), 2, (pp1,))
        ad2, share, keep = call(
            functools.partial(curve_kernel, nx),
            [slab_shape, tile_shape, tile_shape],
            [*to_x(msg), scal, ad],
        )
        shares = to_all_rows(share, scalar_ks)
        state = [*shares, keep, step, ax, ad, ad2, z, y, lower, upper, x, msg1, msg2]
        if outer + 1 < ADMM_ITERS:
            *pieces, x, z, y, ax, ppx = call(
                functools.partial(update_kernel, n, own),
                [own_shape] * n + [own_shape, slab_shape, slab_shape, slab_shape, ((2 * BLK, LANES), F32)],
                [*state, ppx, pp1, pp2, t_hi, t_lo],
                [place, pairs],
                total_scratch,
                flops=prod_flops,
            )
        else:
            (out,) = call(
                functools.partial(last_kernel, n, own), [((2 * half_rows + own, LANES), F32)], state
            )
    return call(
        finish_kernel,
        [own_shape, ((slab_rows, LANES), F32), ((slab_rows, LANES), F32)],
        [out, to_core(out)],
        [place],
    )


def solution(mesh):
    placed = (
        P(("col", "row"), "grp"),
        P(("col", "row"), "grp"),
        P(("col", "row")),
        P("row", "grp"),
        P("row", "grp"),
        P("row", "grp"),
        P("row", "grp"),
        P("row", "col", None, None),
        P("row", "col"),
        P("col", "row", None, None),
        P("col", "row", None),
    )

    def run(*args):
        return tuple(local(*args))

    return jax.shard_map(
        run,
        mesh=mesh,
        in_specs=placed,
        out_specs=(P(("col", "row"), "grp"), P("row", "grp"), P("row", "grp")),
        check_vma=False,
    )
```

```python
import functools

import jax
import jax.numpy as jnp
from jax import lax
from jax.experimental import pallas as pl
from jax.experimental.pallas import tpu as pltpu
from jax.sharding import PartitionSpec as P

ADMM_ITERS = 2
RHO = 0.5
SIGMA = 1e-06
RELAX = 1.6
BLK = 128
LANES = 128
HALF = 64
SC = 8
F32 = jnp.float32
BF16 = jnp.bfloat16

VMEM = pl.BlockSpec(memory_space=pltpu.VMEM)
SMEM = pl.BlockSpec(memory_space=pltpu.SMEM)

ANY = pl.BlockSpec(memory_space=pl.ANY)


def call(body, outs, ins, smem=(), scratch=(), flops=0, after=None):
    n_bytes = sum(v.size * v.dtype.itemsize for v in ins)
    tied = [] if after is None else [after]

    def run(*refs):
        body(*refs[len(tied) :])

    return pl.pallas_call(
        run,
        out_shape=[jax.ShapeDtypeStruct(s, d) for s, d in outs],
        in_specs=[ANY] * len(tied) + [SMEM] * len(smem) + [VMEM] * len(ins),
        out_specs=[VMEM] * len(outs),
        scratch_shapes=list(scratch),
        compiler_params=pltpu.CompilerParams(vmem_limit_bytes=30 * 1024 * 1024),
        cost_estimate=pl.CostEstimate(flops=flops, bytes_accessed=n_bytes, transcendentals=0),
    )(*tied, *smem, *ins)


def low_half(shape):
    return lax.broadcasted_iota(jnp.int32, shape, 1) < HALF


def turn(v):
    return pltpu.roll(v, HALF, 1)


def fold(v):
    return v + turn(v)


def col_sum(v):
    return fold(jnp.sum(v, axis=0, keepdims=True))


def split_bf16(v):
    hi = v.astype(BF16).astype(F32)
    return hi, v - hi


def pair_up(v):
    hi, lo = split_bf16(v)
    low = low_half(v.shape)
    first = jnp.where(low, hi, turn(lo)).astype(BF16)
    second = jnp.where(low, turn(hi), lo).astype(BF16)
    return first, second


def dot(a, b):
    return jnp.dot(a, b, preferred_element_type=F32)


def pack_rows(*rows):
    at = lax.broadcasted_iota(jnp.int32, (SC, LANES), 0)
    tile = jnp.zeros((SC, LANES), F32)
    for k, row in enumerate(rows):
        tile = jnp.where(at == k, row, tile)
    return tile


def mix_cores(core, mine, other):
    low = low_half(mine.shape)
    a = jnp.where(core == 0, mine, turn(mine))
    b = jnp.where(core == 0, turn(other), other)
    return jnp.where(low, a, b)


def own_kernel(place, x, x_other, q, q_other, x_own, q_own):
    core = place[1]
    x_own[...] = mix_cores(core, x[...], x_other[...])
    q_own[...] = mix_cores(core, q[...], q_other[...])


def slab_kernel(place, *refs):
    core = place[1]
    count = len(refs) // 2
    for src, dst in zip(refs[:count], refs[count:]):
        rows = dst.shape[0]
        v = jnp.where(core == 0, src[...], turn(src[...]))
        dst[...] = jnp.where(low_half(dst.shape), v[:rows], turn(v[rows:]))


def prep_kernel(slab, per, cols, pairs, a_in, p_in, a_hi, a_lo, t_hi, t_lo, p_hi, p_lo, diag):
    for ref in (a_hi, a_lo, t_hi, t_lo):
        ref[...] = jnp.zeros(ref.shape, BF16)
    diag[...] = jnp.zeros(diag.shape, F32)
    for m in range(slab):
        rows = slice(m * BLK, (m + 1) * BLK)
        for s in range(per):
            k = m * per + s
            col = cols[k]
            at = pl.multiple_of(col * BLK, BLK)
            block = a_in[k]
            hi, lo = split_bf16(block)
            a_hi[rows, pl.ds(at, BLK)] = hi.astype(BF16)
            a_lo[rows, pl.ds(at, BLK)] = lo.astype(BF16)
            hi, lo = split_bf16(block.T)
            t_hi[pl.ds(at, BLK), rows] = hi.astype(BF16)
            t_lo[pl.ds(at, BLK), rows] = lo.astype(BF16)
            diag[pl.ds(col, 1), :] += RHO * jnp.sum(block * block, axis=0, keepdims=True)
    shape = (BLK, BLK)
    eye = lax.broadcasted_iota(jnp.int32, shape, 0) == lax.broadcasted_iota(jnp.int32, shape, 1)
    for e in range(4):
        hi, lo = split_bf16(p_in[e])
        rows = slice((e // 2) * BLK, (e // 2 + 1) * BLK)
        lanes = slice((e % 2) * BLK, (e % 2 + 1) * BLK)
        p_hi[rows, lanes] = hi.astype(BF16)
        p_lo[rows, lanes] = lo.astype(BF16)
    for e in range(2):
        diag[pl.ds(pairs[e], 1), :] += jnp.sum(jnp.where(eye, p_in[3 * e], 0.0), axis=0, keepdims=True)


def first_kernel(n, own, place, pairs, *refs):
    msgs, (a_hi, a_lo, p_hi, p_lo, keep, send, wide) = refs[:n], refs[n:]
    core = place[1]
    for k in range(n):
        at = pl.multiple_of(lax.bitwise_xor(place[0], k) * own, own)
        hi, lo = split_bf16(msgs[k][...])
        wide[pl.ds(at, own), 0:LANES] = hi.astype(BF16)
        wide[pl.ds(at, own), LANES:] = lo.astype(BF16)
    x = wide[...]
    total = dot(a_hi[...], x) + dot(a_lo[...], x)
    total = total[:, :LANES] + total[:, LANES:]
    rows = total.shape[0] // 2
    keep[0:rows, :] = mix_cores(core, total[:rows], total[rows:])
    send[0:rows, :] = mix_cores(1 - core, total[:rows], total[rows:])
    at_i = pl.ds(pl.multiple_of(pairs[0] * BLK, BLK), BLK)
    at_j = pl.ds(pl.multiple_of(pairs[1] * BLK, BLK), BLK)
    v = jnp.concatenate([wide[at_i, :], wide[at_j, :]], axis=0)
    part = dot(p_hi[...], v) + dot(p_lo[...], v)
    part = part[:, :LANES] + part[:, LANES:]
    part = jnp.where(core == 0, part, turn(part))
    keep[rows:, :] = part
    send[rows:, :] = part


def meet_kernel(keep, got, msg, pp):
    rows = msg.shape[0]
    msg[...] = keep[0:rows, :] + got[0:rows, :]
    pp[...] = jnp.where(low_half(pp.shape), keep[rows:, :], got[rows:, :])


def forward_kernel(n, own, scalars, place, pairs, *refs):
    msgs, rest = refs[:n], refs[n:]
    a_mats, p_mats, rest = rest[:4], rest[4:8], rest[8:]
    if scalars == 2:
        pp_first, rest = rest[0], rest[1:]
    msg, pp, whole, wide = rest
    row = place[0]
    span = whole.shape[0]
    for k in range(n):
        at = pl.multiple_of(lax.bitwise_xor(row, k) * own, own)
        v = msgs[k][0:own, :]
        whole[pl.ds(at, own), :] = v
        first, second = pair_up(v)
        wide[pl.ds(at, own), :] = first
        wide[pl.ds(pl.multiple_of(span + at, own), own), :] = second
    total = jnp.zeros((a_mats[0].shape[0], LANES), F32)
    for t in range(2):
        x = wide[t * span : (t + 1) * span, :]
        total = total + (dot(a_mats[2 * t][...], x) + dot(a_mats[2 * t + 1][...], x))
    total = fold(total)
    rows = total.shape[0] // 2
    msg[0:rows, :] = jnp.where(low_half((rows, LANES)), total[:rows], total[rows:])
    parts = []
    for t in range(2):
        at_i = pl.multiple_of(t * span + pairs[2 * t] * BLK, BLK)
        at_j = pl.multiple_of(t * span + pairs[2 * t + 1] * BLK, BLK)
        v = jnp.concatenate([wide[pl.ds(at_i, BLK), :], wide[pl.ds(at_j, BLK), :]], axis=0)
        parts.append(fold(dot(p_mats[2 * t][...], v) + dot(p_mats[2 * t + 1][...], v)))
    low2 = low_half((2 * BLK, LANES))
    pp_now = jnp.where(low2, parts[0], parts[1])
    pp[...] = pp_now
    picked = []
    for t in range(2):
        at_i = pl.multiple_of(pairs[2 * t] * BLK, BLK)
        at_j = pl.multiple_of(pairs[2 * t + 1] * BLK, BLK)
        picked.append(jnp.concatenate([whole[pl.ds(at_i, BLK), :], whole[pl.ds(at_j, BLK), :]], axis=0))
    vec = jnp.where(low2, picked[0], picked[1])
    tile = msgs[0][own : own + SC, :]
    for k in range(1, n):
        tile = tile + msgs[k][own : own + SC, :]
    tile = fold(tile)
    at = lax.broadcasted_iota(jnp.int32, (SC, LANES), 0)
    tile = jnp.where(at == 3, col_sum(vec * pp_now), tile)
    if scalars == 2:
        tile = jnp.where(at == 4, col_sum(vec * pp_first[...]), tile)
    msg[rows : rows + SC, :] = tile


def back_product(n, own, place, pairs, w, pp_now, t_mats, total, outs, extra=()):
    row = place[0]
    span = total.shape[0]
    first, second = pair_up(w)
    wide = jnp.concatenate([first, second], axis=0)
    mine = fold(dot(t_mats[0][...], wide) + dot(t_mats[1][...], wide))
    other = fold(dot(t_mats[2][...], wide) + dot(t_mats[3][...], wide))
    total[...] = jnp.where(low_half((span, LANES)), mine, other)
    low1 = low_half((BLK, LANES))
    for t in range(2):
        side = low1 if t == 0 else jnp.logical_not(low1)
        for e in range(2):
            at = pl.ds(pl.multiple_of(pairs[2 * t + e] * BLK, BLK), BLK)
            total[at, :] += jnp.where(side, pp_now[e * BLK : (e + 1) * BLK], 0.0)
    for k in range(n):
        at = pl.multiple_of(lax.bitwise_xor(row, k) * own, own)
        outs[k][0:own, :] = total[pl.ds(at, own), :]
        at = own
        for rows in extra:
            outs[k][at : at + rows.shape[0], :] = rows
            at += rows.shape[0]


def start_back_kernel(n, nx, own, place, pairs, *refs):
    msgs, rest = refs[:nx], refs[nx:]
    z, y, pp, diag, diag_other, *t_mats = rest[:9]
    outs, (ax, total) = rest[9 : 9 + n], rest[9 + n :]
    ax_now = msgs[0][...]
    for k in range(1, nx):
        ax_now = ax_now + msgs[k][...]
    ax[...] = ax_now
    w = RHO * ax_now - (RHO * z[...] - y[...])
    back_product(n, own, place, pairs, w, pp[...], t_mats, total, outs, (diag[...], diag_other[...]))


def step_back_kernel(n, nx, own, place, pairs, *refs):
    msgs, rest = refs[:nx], refs[nx:]
    pp, *t_mats = rest[:5]
    outs, (ad, scal, total) = rest[5 : 5 + n], rest[5 + n :]
    rows = ad.shape[0]
    v = msgs[0][...]
    for k in range(1, nx):
        v = v + msgs[k][...]
    ad_now = v[:rows]
    tile = v[rows:]
    ad[...] = ad_now
    scal[...] = tile
    curve = RHO * col_sum(ad_now * ad_now) + tile[3:4]
    back_product(n, own, place, pairs, RHO * ad_now, pp[...], t_mats, total, outs, (pack_rows(curve),))


def residual_kernel(n, own, first, place, *refs):
    msgs, rest = refs[:n], refs[n:]
    if first:
        x, q, pd, msg, res, dk, full = rest
        rows = msgs[0].shape[0] - own
        tile = msgs[0][own:, :]
        for k in range(1, n):
            tile = tile + msgs[k][own:, :]
        n_range = rows // 2
        low1 = low_half((BLK, LANES))
        for b in range(n_range):
            mine = jnp.broadcast_to(tile[b : b + 1], (BLK, LANES)).T
            other = jnp.broadcast_to(tile[n_range + b : n_range + b + 1], (BLK, LANES)).T
            full[b * BLK : (b + 1) * BLK, :] = jnp.where(low1, mine, other)
        at = pl.multiple_of(place[0] * own, own)
        diag = pd[...] + SIGMA + full[pl.ds(at, own), :]
        dk[...] = diag
    else:
        x, q, pd, dk, msg, res = rest
        diag = dk[...]
    total = msgs[0][0:own, :]
    for k in range(1, n):
        total = total + msgs[k][0:own, :]
    r = -q[...] - pd[...] * x[...] - total
    s = r / diag
    res[...] = r
    msg[0:own, :] = s
    shift = pd[...] + SIGMA
    rz = jnp.sum(r * s, axis=0, keepdims=True)
    dd = jnp.sum(shift * s * s, axis=0, keepdims=True)
    msg[own : own + SC, :] = pack_rows(rz, dd)


def step_kernel(n, own, *refs):
    msgs, rest = refs[:n], refs[n:]
    scal, prev, r, pd, dk, msg, step_out = rest
    total = msgs[0][...]
    for k in range(1, n):
        total = total + msgs[k][...]
    shift = pd[...] + SIGMA
    d = prev[0:own, :]
    kd = shift * d + total[:own]
    curve = total[own : own + 1] + scal[1:2, :]
    step = scal[0:1, :] / curve
    r_new = r[...] - step * kd
    s = r_new / dk[...]
    msg[0:own, :] = s
    rz = jnp.sum(r_new * s, axis=0, keepdims=True)
    ss = jnp.sum(shift * s * s, axis=0, keepdims=True)
    sd = jnp.sum(shift * s * d, axis=0, keepdims=True)
    msg[own : own + SC, :] = pack_rows(rz, ss, sd)
    step_out[...] = jnp.broadcast_to(step, step_out.shape)


def curve_kernel(nx, *refs):
    msgs, rest = refs[:nx], refs[nx:]
    scal, ad, ad2, share, keep = rest
    rows = ad.shape[0]
    v = msgs[0][...]
    for k in range(1, nx):
        v = v + msgs[k][...]
    tile = v[rows:]
    beta = tile[0:1] / scal[0:1, :]
    ad_now = v[:rows] + beta * ad[...]
    ad2[...] = ad_now
    flat = tile[1:2] + 2.0 * beta * tile[2:3] + beta * beta * scal[1:2, :]
    pair = tile[3:4] + 2.0 * beta * tile[4:5] + beta * beta * scal[3:4, :]
    share[...] = pack_rows(RHO * col_sum(ad_now * ad_now) + pair)
    keep[...] = pack_rows(tile[0:1], beta, flat)


def admm_update(n, own, refs):
    shares, rest = refs[:n], refs[n:]
    keep, step_in, ax, ad, ad2, z, y, lower, upper, x, msg1, msg2 = rest[:12]
    tile = shares[0][...]
    for k in range(1, n):
        tile = tile + shares[k][...]
    beta = keep[1:2, :]
    step1 = step_in[0:1, :]
    step2 = keep[0:1, :] / (tile[0:1] + keep[2:3, :])
    d1 = msg1[0:own, :]
    d2 = msg2[0:own, :] + beta * d1
    x_hat = x[...] + step1 * d1 + step2 * d2
    x_new = RELAX * x_hat + (1.0 - RELAX) * x[...]
    ax_hat = ax[...] + step1 * ad[...] + step2 * ad2[...]
    relaxed = RELAX * ax_hat + (1.0 - RELAX) * z[...]
    z_new = jnp.clip(relaxed + y[...] / RHO, lower[...], upper[...])
    y_new = y[...] + RHO * (relaxed - z_new)
    return beta, step1, step2, x_new, ax_hat, z_new, y_new, rest[12:]


def update_kernel(n, own, place, pairs, *refs):
    beta, step1, step2, x_new, ax_hat, z_new, y_new, rest = admm_update(n, own, refs)
    ax = refs[n + 2]
    ppx, pp1, pp2, *t_mats = rest[:7]
    outs, (x_out, z_out, y_out, ax_out, ppx_out, total) = rest[7 : 7 + n], rest[7 + n :]
    x_out[...] = x_new
    z_out[...] = z_new
    y_out[...] = y_new
    ax_new = RELAX * ax_hat + (1.0 - RELAX) * ax[...]
    ax_out[...] = ax_new
    pp_hat = ppx[...] + step1 * pp1[...] + step2 * (pp2[...] + beta * pp1[...])
    pp_new = RELAX * pp_hat + (1.0 - RELAX) * ppx[...]
    ppx_out[...] = pp_new
    w = RHO * ax_new - (RHO * z_new - y_new)
    back_product(n, own, place, pairs, w, pp_new, t_mats, total, outs)


def last_kernel(n, own, *refs):
    _, _, _, x_new, _, z_new, y_new, rest = admm_update(n, own, refs)
    (out,) = rest
    rows = z_new.shape[0]
    out[0:rows, :] = z_new
    out[rows : 2 * rows, :] = y_new
    out[2 * rows :, :] = x_new


def finish_kernel(place, mine, got, x, z, y):
    core = place[1]
    rows = z.shape[0] // 2
    for k, dst in enumerate((z, y)):
        a = mine[k * rows : (k + 1) * rows, :]
        b = got[k * rows : (k + 1) * rows, :]
        low = low_half(a.shape)
        left = jnp.where(core == 0, a, b)
        right = jnp.where(core == 0, b, a)
        dst[0:rows, :] = jnp.where(low, left, turn(right))
        dst[rows : 2 * rows, :] = jnp.where(low, turn(left), right)
    a = mine[2 * rows :, :]
    b = got[2 * rows :, :]
    low = low_half(a.shape)
    x[...] = jnp.where(core == 0, jnp.where(low, a, b), jnp.where(low, turn(b), turn(a)))


def local(x_state, q_lin, p_diag, z_state, y_state, lower_bound, upper_bound, a_blocks, a_cols, p_blocks, p_pairs):
    slab, per = a_cols.shape
    n = lax.axis_size("row")
    n_col = lax.axis_size("col")
    nx = n_col // 2
    own = x_state.shape[0]
    span = own * n
    n_range = span // BLK
    slab_rows = slab * BLK
    half_rows = slab_rows // 2
    row_at = lax.axis_index("row")
    core_at = lax.axis_index("col") % 2
    place = jnp.stack([row_at, core_at]).astype(jnp.int32)

    def to_core(v):
        return lax.ppermute(v, "col", [(c, c ^ 1) for c in range(n_col)])

    def to_x(v):
        return [v] + [lax.ppermute(v, "col", [(c, c ^ (2 * k)) for c in range(n_col)]) for k in range(1, nx)]

    swaps = [2, 3, 1] if n == 4 else list(range(1, n))

    def to_row(pieces, order=None):
        got = {0: pieces[0]}
        for k in order or swaps:
            got[k] = lax.ppermute(pieces[k], "row", [(i, i ^ k) for i in range(n)])
        return [got[k] for k in range(n)]

    def to_all_rows(v):
        return to_row([v] * n, swaps[::-1])

    a_mine = a_blocks.reshape(slab * per, BLK, BLK)
    p_mine = p_blocks.reshape(4, BLK, BLK)
    ints = jnp.concatenate([a_cols.reshape(-1), p_pairs.reshape(-1)])
    x_rows = to_all_rows(x_state)
    a_other = to_core(a_mine)
    ints_other = to_core(ints)
    p_other = to_core(p_mine)
    pd_other = to_core(p_diag)
    count = slab * per
    pd = jnp.concatenate(
        [jnp.broadcast_to(p_diag[:, None], (own, HALF)), jnp.broadcast_to(pd_other[:, None], (own, HALF))], axis=1
    )
    x, q = call(
        own_kernel, [((own, LANES), F32)] * 2, [x_state, to_core(x_state), q_lin, to_core(q_lin)], [place]
    )
    z, y, lower, upper = call(
        slab_kernel, [((half_rows, LANES), F32)] * 4, [z_state, y_state, lower_bound, upper_bound], [place]
    )
    own_shape = ((own, LANES), F32)
    msg_shape = ((own + SC, LANES), F32)
    tile_shape = ((SC, LANES), F32)
    slab_shape = ((half_rows, LANES), F32)
    pp_shape = ((2 * BLK, LANES), F32)

    def prepare(a, p, at_cols, at_pairs, after=None):
        *mats, diag = call(
            functools.partial(prep_kernel, slab, per),
            [((slab_rows, span), BF16)] * 2
            + [((span, slab_rows), BF16)] * 2
            + [((2 * BLK, 2 * BLK), BF16)] * 2
            + [((n_range, LANES), F32)],
            [a, p],
            [at_cols, at_pairs],
            flops=10**8,
            after=after,
        )
        return mats[0:2], mats[2:4], mats[4:6], diag

    prod_flops = 4 * slab_rows * 2 * span * LANES
    total_scratch = [pltpu.VMEM((span, LANES), F32)]
    a_own, t_own, p_own, diag = prepare(a_mine, p_mine, a_cols.reshape(-1), p_pairs.reshape(-1))
    both_shape = ((half_rows + 2 * BLK, LANES), F32)
    keep, send = call(
        functools.partial(first_kernel, n, own),
        [both_shape, both_shape],
        [*x_rows, *a_own, *p_own],
        [place, p_pairs.reshape(-1)],
        [pltpu.VMEM((span, 2 * LANES), BF16)],
        flops=prod_flops,
    )
    msg, ppx = call(meet_kernel, [slab_shape, pp_shape], [keep, to_core(send)])
    a_far, t_far, p_far, diag_other = prepare(
        a_other, p_other, ints_other[:count], ints_other[count:], after=msg
    )
    a_mats, t_mats, p_mats = [*a_own, *a_far], [*t_own, *t_far], [*p_own, *p_far]
    pairs = jnp.concatenate([p_pairs.reshape(-1), ints_other[count:]])

    def forward(msgs, scalars, pp_first=()):
        return call(
            functools.partial(forward_kernel, n, own, scalars),
            [((half_rows + SC, LANES), F32), pp_shape],
            [*msgs, *a_mats, *p_mats, *pp_first],
            [place, pairs],
            total_scratch + [pltpu.VMEM((2 * span, LANES), BF16)],
            flops=prod_flops,
        )

    *pieces, ax = call(
        functools.partial(start_back_kernel, n, nx, own),
        [((own + 2 * n_range, LANES), F32)] * n + [((half_rows, LANES), F32)],
        [*to_x(msg), z, y, ppx, diag, diag_other, *t_mats],
        [place, pairs],
        total_scratch,
        flops=prod_flops,
    )
    for outer in range(ADMM_ITERS):
        if outer == 0:
            msg1, r, dk = call(
                functools.partial(residual_kernel, n, own, True),
                [msg_shape, own_shape, own_shape],
                [*to_row(pieces), x, q, pd],
                [place],
                total_scratch,
            )
        else:
            msg1, r = call(
                functools.partial(residual_kernel, n, own, False),
                [msg_shape, own_shape],
                [*to_row(pieces), x, q, pd, dk],
                [place],
            )
        msg, pp1 = forward(to_all_rows(msg1), 1)
        *pieces, ad, scal = call(
            functools.partial(step_back_kernel, n, nx, own),
            [msg_shape] * n + [slab_shape, tile_shape],
            [*to_x(msg), pp1, *t_mats],
            [place, pairs],
            total_scratch,
            flops=prod_flops,
        )
        msg2, step = call(
            functools.partial(step_kernel, n, own),
            [msg_shape, tile_shape],
            [*to_row(pieces), scal, msg1, r, pd, dk],
        )
        msg, pp2 = forward(to_all_rows(msg2), 2, (pp1,))
        ad2, share, keep = call(
            functools.partial(curve_kernel, nx),
            [slab_shape, tile_shape, tile_shape],
            [*to_x(msg), scal, ad],
        )
        shares = to_all_rows(share)
        state = [*shares, keep, step, ax, ad, ad2, z, y, lower, upper, x, msg1, msg2]
        if outer + 1 < ADMM_ITERS:
            *pieces, x, z, y, ax, ppx = call(
                functools.partial(update_kernel, n, own),
                [own_shape] * n + [own_shape, slab_shape, slab_shape, slab_shape, ((2 * BLK, LANES), F32)],
                [*state, ppx, pp1, pp2, *t_mats],
                [place, pairs],
                total_scratch,
                flops=prod_flops,
            )
        else:
            (out,) = call(
                functools.partial(last_kernel, n, own), [((2 * half_rows + own, LANES), F32)], state
            )
    return call(
        finish_kernel,
        [own_shape, ((slab_rows, LANES), F32), ((slab_rows, LANES), F32)],
        [out, to_core(out)],
        [place],
    )


def solution(mesh):
    placed = (
        P(("col", "row"), "grp"),
        P(("col", "row"), "grp"),
        P(("col", "row")),
        P("row", "grp"),
        P("row", "grp"),
        P("row", "grp"),
        P("row", "grp"),
        P("row", "col", None, None),
        P("row", "col"),
        P("col", "row", None, None),
        P("col", "row", None),
    )

    def run(*args):
        return tuple(local(*args))

    return jax.shard_map(
        run,
        mesh=mesh,
        in_specs=placed,
        out_specs=(P(("col", "row"), "grp"), P("row", "grp"), P("row", "grp")),
        check_vma=False,
    )
```

```python
import functools

import jax
import jax.numpy as jnp
from jax import lax
from jax.experimental import pallas as pl
from jax.experimental.pallas import tpu as pltpu
from jax.sharding import PartitionSpec as P

ADMM_ITERS = 2
RHO = 0.5
SIGMA = 1e-06
RELAX = 1.6
BLK = 128
LANES = 128
HALF = 64
SC = 8
F32 = jnp.float32
BF16 = jnp.bfloat16

VMEM = pl.BlockSpec(memory_space=pltpu.VMEM)
SMEM = pl.BlockSpec(memory_space=pltpu.SMEM)

ANY = pl.BlockSpec(memory_space=pl.ANY)


def call(body, outs, ins, smem=(), scratch=(), flops=0, after=None):
    n_bytes = sum(v.size * v.dtype.itemsize for v in ins)
    tied = [] if after is None else [after]

    def run(*refs):
        body(*refs[len(tied) :])

    return pl.pallas_call(
        run,
        out_shape=[jax.ShapeDtypeStruct(s, d) for s, d in outs],
        in_specs=[ANY] * len(tied) + [SMEM] * len(smem) + [VMEM] * len(ins),
        out_specs=[VMEM] * len(outs),
        scratch_shapes=list(scratch),
        compiler_params=pltpu.CompilerParams(vmem_limit_bytes=30 * 1024 * 1024),
        cost_estimate=pl.CostEstimate(flops=flops, bytes_accessed=n_bytes, transcendentals=0),
    )(*tied, *smem, *ins)


def low_half(shape):
    return lax.broadcasted_iota(jnp.int32, shape, 1) < HALF


def turn(v):
    return pltpu.roll(v, HALF, 1)


def fold(v):
    return v + turn(v)


def col_sum(v):
    return fold(jnp.sum(v, axis=0, keepdims=True))


def split_bf16(v):
    hi = v.astype(BF16).astype(F32)
    return hi, v - hi


def pair_up(v):
    hi, lo = split_bf16(v)
    low = low_half(v.shape)
    first = jnp.where(low, hi, turn(lo)).astype(BF16)
    second = jnp.where(low, turn(hi), lo).astype(BF16)
    return first, second


def dot(a, b):
    return jnp.dot(a, b, preferred_element_type=F32)


def pack_rows(*rows):
    at = lax.broadcasted_iota(jnp.int32, (SC, LANES), 0)
    tile = jnp.zeros((SC, LANES), F32)
    for k, row in enumerate(rows):
        tile = jnp.where(at == k, row, tile)
    return tile


def mix_cores(core, mine, other):
    low = low_half(mine.shape)
    a = jnp.where(core == 0, mine, turn(mine))
    b = jnp.where(core == 0, turn(other), other)
    return jnp.where(low, a, b)


def own_kernel(place, x, x_other, q, q_other, x_own, q_own):
    core = place[1]
    x_own[...] = mix_cores(core, x[...], x_other[...])
    q_own[...] = mix_cores(core, q[...], q_other[...])


def slab_kernel(place, *refs):
    core = place[1]
    count = len(refs) // 2
    for src, dst in zip(refs[:count], refs[count:]):
        rows = dst.shape[0]
        v = jnp.where(core == 0, src[...], turn(src[...]))
        dst[...] = jnp.where(low_half(dst.shape), v[:rows], turn(v[rows:]))


def prep_kernel(slab, per, cols, pairs, a_in, p_in, a_both, t_hi, t_lo, p_hi, p_lo, diag):
    for ref in (t_hi, t_lo):
        ref[...] = jnp.zeros(ref.shape, BF16)
    diag[...] = jnp.zeros(diag.shape, F32)
    for m in range(slab):
        rows = slice(m * BLK, (m + 1) * BLK)
        for s in range(per):
            k = m * per + s
            col = cols[k]
            at = pl.multiple_of(col * BLK, BLK)
            block = a_in[k]
            hi, lo = split_bf16(block)
            a_both[2 * m * BLK : (2 * m + 1) * BLK, s * BLK : (s + 1) * BLK] = hi.astype(BF16)
            a_both[(2 * m + 1) * BLK : (2 * m + 2) * BLK, s * BLK : (s + 1) * BLK] = lo.astype(BF16)
            hi, lo = split_bf16(block.T)
            t_hi[pl.ds(at, BLK), rows] = hi.astype(BF16)
            t_lo[pl.ds(at, BLK), rows] = lo.astype(BF16)
            diag[pl.ds(col, 1), :] += RHO * jnp.sum(block * block, axis=0, keepdims=True)
    shape = (BLK, BLK)
    eye = lax.broadcasted_iota(jnp.int32, shape, 0) == lax.broadcasted_iota(jnp.int32, shape, 1)
    for e in range(4):
        hi, lo = split_bf16(p_in[e])
        rows = slice((e // 2) * BLK, (e // 2 + 1) * BLK)
        lanes = slice((e % 2) * BLK, (e % 2 + 1) * BLK)
        p_hi[rows, lanes] = hi.astype(BF16)
        p_lo[rows, lanes] = lo.astype(BF16)
    for e in range(2):
        diag[pl.ds(pairs[e], 1), :] += jnp.sum(jnp.where(eye, p_in[3 * e], 0.0), axis=0, keepdims=True)


def slab_product(slab, cols, a_refs, starts, wide):
    per = cols.shape[0] // (slab * len(a_refs))
    sums = []
    for m in range(slab):
        total = None
        for t, a_ref in enumerate(a_refs):
            blocks = []
            for s in range(per):
                at = starts[t] + cols[(t * slab + m) * per + s] * BLK
                blocks.append(wide[pl.ds(pl.multiple_of(at, BLK), BLK), :])
            part = dot(a_ref[2 * m * BLK : (2 * m + 2) * BLK, :], jnp.concatenate(blocks, axis=0))
            total = part if total is None else total + part
        sums.append(total[:BLK] + total[BLK:])
    return jnp.concatenate(sums, axis=0)


def first_kernel(n, own, slab, place, pairs, cols, *refs):
    msgs, (a_both, p_hi, p_lo, keep, send, wide) = refs[:n], refs[n:]
    core = place[1]
    for k in range(n):
        at = pl.multiple_of(lax.bitwise_xor(place[0], k) * own, own)
        hi, lo = split_bf16(msgs[k][...])
        wide[pl.ds(at, own), 0:LANES] = hi.astype(BF16)
        wide[pl.ds(at, own), LANES:] = lo.astype(BF16)
    total = slab_product(slab, cols, [a_both], [0], wide)
    total = total[:, :LANES] + total[:, LANES:]
    rows = total.shape[0] // 2
    keep[0:rows, :] = mix_cores(core, total[:rows], total[rows:])
    send[0:rows, :] = mix_cores(1 - core, total[:rows], total[rows:])
    at_i = pl.ds(pl.multiple_of(pairs[0] * BLK, BLK), BLK)
    at_j = pl.ds(pl.multiple_of(pairs[1] * BLK, BLK), BLK)
    v = jnp.concatenate([wide[at_i, :], wide[at_j, :]], axis=0)
    part = dot(p_hi[...], v) + dot(p_lo[...], v)
    part = part[:, :LANES] + part[:, LANES:]
    part = jnp.where(core == 0, part, turn(part))
    keep[rows:, :] = part
    send[rows:, :] = part


def meet_kernel(keep, got, msg, pp):
    rows = msg.shape[0]
    msg[...] = keep[0:rows, :] + got[0:rows, :]
    pp[...] = jnp.where(low_half(pp.shape), keep[rows:, :], got[rows:, :])


def forward_kernel(n, own, slab, scalars, place, pairs, cols, *refs):
    msgs, rest = refs[:n], refs[n:]
    a_mats, p_mats, rest = rest[:2], rest[2:6], rest[6:]
    if scalars == 2:
        pp_first, rest = rest[0], rest[1:]
    msg, pp, whole, wide = rest
    row = place[0]
    span = whole.shape[0]
    for k in range(n):
        at = pl.multiple_of(lax.bitwise_xor(row, k) * own, own)
        v = msgs[k][0:own, :]
        whole[pl.ds(at, own), :] = v
        first, second = pair_up(v)
        wide[pl.ds(at, own), :] = first
        wide[pl.ds(pl.multiple_of(span + at, own), own), :] = second
    total = fold(slab_product(slab, cols, a_mats, [0, span], wide))
    rows = total.shape[0] // 2
    msg[0:rows, :] = jnp.where(low_half((rows, LANES)), total[:rows], total[rows:])
    parts = []
    for t in range(2):
        at_i = pl.multiple_of(t * span + pairs[2 * t] * BLK, BLK)
        at_j = pl.multiple_of(t * span + pairs[2 * t + 1] * BLK, BLK)
        v = jnp.concatenate([wide[pl.ds(at_i, BLK), :], wide[pl.ds(at_j, BLK), :]], axis=0)
        parts.append(fold(dot(p_mats[2 * t][...], v) + dot(p_mats[2 * t + 1][...], v)))
    low2 = low_half((2 * BLK, LANES))
    pp_now = jnp.where(low2, parts[0], parts[1])
    pp[...] = pp_now
    picked = []
    for t in range(2):
        at_i = pl.multiple_of(pairs[2 * t] * BLK, BLK)
        at_j = pl.multiple_of(pairs[2 * t + 1] * BLK, BLK)
        picked.append(jnp.concatenate([whole[pl.ds(at_i, BLK), :], whole[pl.ds(at_j, BLK), :]], axis=0))
    vec = jnp.where(low2, picked[0], picked[1])
    tile = msgs[0][own : own + SC, :]
    for k in range(1, n):
        tile = tile + msgs[k][own : own + SC, :]
    tile = fold(tile)
    at = lax.broadcasted_iota(jnp.int32, (SC, LANES), 0)
    tile = jnp.where(at == 3, col_sum(vec * pp_now), tile)
    if scalars == 2:
        tile = jnp.where(at == 4, col_sum(vec * pp_first[...]), tile)
    msg[rows : rows + SC, :] = tile


def back_product(n, own, place, pairs, w, pp_now, t_mats, total, outs, extra=()):
    row = place[0]
    span = total.shape[0]
    first, second = pair_up(w)
    wide = jnp.concatenate([first, second], axis=0)
    mine = fold(dot(t_mats[0][...], wide) + dot(t_mats[1][...], wide))
    other = fold(dot(t_mats[2][...], wide) + dot(t_mats[3][...], wide))
    total[...] = jnp.where(low_half((span, LANES)), mine, other)
    low1 = low_half((BLK, LANES))
    for t in range(2):
        side = low1 if t == 0 else jnp.logical_not(low1)
        for e in range(2):
            at = pl.ds(pl.multiple_of(pairs[2 * t + e] * BLK, BLK), BLK)
            total[at, :] += jnp.where(side, pp_now[e * BLK : (e + 1) * BLK], 0.0)
    for k in range(n):
        at = pl.multiple_of(lax.bitwise_xor(row, k) * own, own)
        outs[k][0:own, :] = total[pl.ds(at, own), :]
        at = own
        for rows in extra:
            outs[k][at : at + rows.shape[0], :] = rows
            at += rows.shape[0]


def start_back_kernel(n, nx, own, place, pairs, *refs):
    msgs, rest = refs[:nx], refs[nx:]
    z, y, pp, diag, diag_other, *t_mats = rest[:9]
    outs, (ax, total) = rest[9 : 9 + n], rest[9 + n :]
    ax_now = msgs[0][...]
    for k in range(1, nx):
        ax_now = ax_now + msgs[k][...]
    ax[...] = ax_now
    w = RHO * ax_now - (RHO * z[...] - y[...])
    back_product(n, own, place, pairs, w, pp[...], t_mats, total, outs, (diag[...], diag_other[...]))


def step_back_kernel(n, nx, own, place, pairs, *refs):
    msgs, rest = refs[:nx], refs[nx:]
    pp, *t_mats = rest[:5]
    outs, (ad, scal, total) = rest[5 : 5 + n], rest[5 + n :]
    rows = ad.shape[0]
    v = msgs[0][...]
    for k in range(1, nx):
        v = v + msgs[k][...]
    ad_now = v[:rows]
    tile = v[rows:]
    ad[...] = ad_now
    scal[...] = tile
    curve = RHO * col_sum(ad_now * ad_now) + tile[3:4]
    back_product(n, own, place, pairs, RHO * ad_now, pp[...], t_mats, total, outs, (pack_rows(curve),))


def residual_kernel(n, own, first, place, *refs):
    msgs, rest = refs[:n], refs[n:]
    if first:
        x, q, pd, msg, res, dk, full = rest
        rows = msgs[0].shape[0] - own
        tile = msgs[0][own:, :]
        for k in range(1, n):
            tile = tile + msgs[k][own:, :]
        n_range = rows // 2
        low1 = low_half((BLK, LANES))
        for b in range(n_range):
            mine = jnp.broadcast_to(tile[b : b + 1], (BLK, LANES)).T
            other = jnp.broadcast_to(tile[n_range + b : n_range + b + 1], (BLK, LANES)).T
            full[b * BLK : (b + 1) * BLK, :] = jnp.where(low1, mine, other)
        at = pl.multiple_of(place[0] * own, own)
        diag = pd[...] + SIGMA + full[pl.ds(at, own), :]
        dk[...] = diag
    else:
        x, q, pd, dk, msg, res = rest
        diag = dk[...]
    total = msgs[0][0:own, :]
    for k in range(1, n):
        total = total + msgs[k][0:own, :]
    r = -q[...] - pd[...] * x[...] - total
    s = r / diag
    res[...] = r
    msg[0:own, :] = s
    shift = pd[...] + SIGMA
    rz = jnp.sum(r * s, axis=0, keepdims=True)
    dd = jnp.sum(shift * s * s, axis=0, keepdims=True)
    msg[own : own + SC, :] = pack_rows(rz, dd)


def step_kernel(n, own, *refs):
    msgs, rest = refs[:n], refs[n:]
    scal, prev, r, pd, dk, msg, step_out = rest
    total = msgs[0][...]
    for k in range(1, n):
        total = total + msgs[k][...]
    shift = pd[...] + SIGMA
    d = prev[0:own, :]
    kd = shift * d + total[:own]
    curve = total[own : own + 1] + scal[1:2, :]
    step = scal[0:1, :] / curve
    r_new = r[...] - step * kd
    s = r_new / dk[...]
    msg[0:own, :] = s
    rz = jnp.sum(r_new * s, axis=0, keepdims=True)
    ss = jnp.sum(shift * s * s, axis=0, keepdims=True)
    sd = jnp.sum(shift * s * d, axis=0, keepdims=True)
    msg[own : own + SC, :] = pack_rows(rz, ss, sd)
    step_out[...] = jnp.broadcast_to(step, step_out.shape)


def curve_kernel(nx, *refs):
    msgs, rest = refs[:nx], refs[nx:]
    scal, ad, ad2, share, keep = rest
    rows = ad.shape[0]
    v = msgs[0][...]
    for k in range(1, nx):
        v = v + msgs[k][...]
    tile = v[rows:]
    beta = tile[0:1] / scal[0:1, :]
    ad_now = v[:rows] + beta * ad[...]
    ad2[...] = ad_now
    flat = tile[1:2] + 2.0 * beta * tile[2:3] + beta * beta * scal[1:2, :]
    pair = tile[3:4] + 2.0 * beta * tile[4:5] + beta * beta * scal[3:4, :]
    share[...] = pack_rows(RHO * col_sum(ad_now * ad_now) + pair)
    keep[...] = pack_rows(tile[0:1], beta, flat)


def admm_update(n, own, refs):
    shares, rest = refs[:n], refs[n:]
    keep, step_in, ax, ad, ad2, z, y, lower, upper, x, msg1, msg2 = rest[:12]
    tile = shares[0][...]
    for k in range(1, n):
        tile = tile + shares[k][...]
    beta = keep[1:2, :]
    step1 = step_in[0:1, :]
    step2 = keep[0:1, :] / (tile[0:1] + keep[2:3, :])
    d1 = msg1[0:own, :]
    d2 = msg2[0:own, :] + beta * d1
    x_hat = x[...] + step1 * d1 + step2 * d2
    x_new = RELAX * x_hat + (1.0 - RELAX) * x[...]
    ax_hat = ax[...] + step1 * ad[...] + step2 * ad2[...]
    relaxed = RELAX * ax_hat + (1.0 - RELAX) * z[...]
    z_new = jnp.clip(relaxed + y[...] / RHO, lower[...], upper[...])
    y_new = y[...] + RHO * (relaxed - z_new)
    return beta, step1, step2, x_new, ax_hat, z_new, y_new, rest[12:]


def update_kernel(n, own, place, pairs, *refs):
    beta, step1, step2, x_new, ax_hat, z_new, y_new, rest = admm_update(n, own, refs)
    ax = refs[n + 2]
    ppx, pp1, pp2, *t_mats = rest[:7]
    outs, (x_out, z_out, y_out, ax_out, ppx_out, total) = rest[7 : 7 + n], rest[7 + n :]
    x_out[...] = x_new
    z_out[...] = z_new
    y_out[...] = y_new
    ax_new = RELAX * ax_hat + (1.0 - RELAX) * ax[...]
    ax_out[...] = ax_new
    pp_hat = ppx[...] + step1 * pp1[...] + step2 * (pp2[...] + beta * pp1[...])
    pp_new = RELAX * pp_hat + (1.0 - RELAX) * ppx[...]
    ppx_out[...] = pp_new
    w = RHO * ax_new - (RHO * z_new - y_new)
    back_product(n, own, place, pairs, w, pp_new, t_mats, total, outs)


def last_kernel(n, own, *refs):
    _, _, _, x_new, _, z_new, y_new, rest = admm_update(n, own, refs)
    (out,) = rest
    rows = z_new.shape[0]
    out[0:rows, :] = z_new
    out[rows : 2 * rows, :] = y_new
    out[2 * rows :, :] = x_new


def finish_kernel(place, mine, got, x, z, y):
    core = place[1]
    rows = z.shape[0] // 2
    for k, dst in enumerate((z, y)):
        a = mine[k * rows : (k + 1) * rows, :]
        b = got[k * rows : (k + 1) * rows, :]
        low = low_half(a.shape)
        left = jnp.where(core == 0, a, b)
        right = jnp.where(core == 0, b, a)
        dst[0:rows, :] = jnp.where(low, left, turn(right))
        dst[rows : 2 * rows, :] = jnp.where(low, turn(left), right)
    a = mine[2 * rows :, :]
    b = got[2 * rows :, :]
    low = low_half(a.shape)
    x[...] = jnp.where(core == 0, jnp.where(low, a, b), jnp.where(low, turn(b), turn(a)))


def local(x_state, q_lin, p_diag, z_state, y_state, lower_bound, upper_bound, a_blocks, a_cols, p_blocks, p_pairs):
    slab, per = a_cols.shape
    n = lax.axis_size("row")
    n_col = lax.axis_size("col")
    nx = n_col // 2
    own = x_state.shape[0]
    span = own * n
    n_range = span // BLK
    slab_rows = slab * BLK
    half_rows = slab_rows // 2
    row_at = lax.axis_index("row")
    core_at = lax.axis_index("col") % 2
    place = jnp.stack([row_at, core_at]).astype(jnp.int32)

    def to_core(v):
        return lax.ppermute(v, "col", [(c, c ^ 1) for c in range(n_col)])

    def to_x(v):
        return [v] + [lax.ppermute(v, "col", [(c, c ^ (2 * k)) for c in range(n_col)]) for k in range(1, nx)]

    ks = range(1, n)

    def over_row(v, k):
        return lax.ppermute(v, "row", [(i, i ^ k) for i in range(n)])

    def to_row(pieces):
        return [pieces[0]] + [over_row(pieces[k], k) for k in ks]

    def to_all_rows(v):
        return [v] + [over_row(v, k) for k in ks]

    a_mine = a_blocks.reshape(slab * per, BLK, BLK)
    p_mine = p_blocks.reshape(4, BLK, BLK)
    ints = jnp.concatenate([a_cols.reshape(-1), p_pairs.reshape(-1)])
    x_rows = to_all_rows(x_state)
    a_other = to_core(a_mine)
    ints_other = to_core(ints)
    p_other = to_core(p_mine)
    pd_other = to_core(p_diag)
    count = slab * per
    pd = jnp.concatenate(
        [jnp.broadcast_to(p_diag[:, None], (own, HALF)), jnp.broadcast_to(pd_other[:, None], (own, HALF))], axis=1
    )
    x, q = call(
        own_kernel, [((own, LANES), F32)] * 2, [x_state, to_core(x_state), q_lin, to_core(q_lin)], [place]
    )
    z, y, lower, upper = call(
        slab_kernel, [((half_rows, LANES), F32)] * 4, [z_state, y_state, lower_bound, upper_bound], [place]
    )
    own_shape = ((own, LANES), F32)
    msg_shape = ((own + SC, LANES), F32)
    tile_shape = ((SC, LANES), F32)
    slab_shape = ((half_rows, LANES), F32)
    pp_shape = ((2 * BLK, LANES), F32)

    def prepare(a, p, at_cols, at_pairs, after=None):
        *mats, diag = call(
            functools.partial(prep_kernel, slab, per),
            [((2 * slab_rows, per * BLK), BF16)]
            + [((span, slab_rows), BF16)] * 2
            + [((2 * BLK, 2 * BLK), BF16)] * 2
            + [((n_range, LANES), F32)],
            [a, p],
            [at_cols, at_pairs],
            flops=10**8,
            after=after,
        )
        return mats[0:1], mats[1:3], mats[3:5], diag

    prod_flops = 4 * slab_rows * 2 * span * LANES
    total_scratch = [pltpu.VMEM((span, LANES), F32)]
    a_own, t_own, p_own, diag = prepare(a_mine, p_mine, a_cols.reshape(-1), p_pairs.reshape(-1))
    both_shape = ((half_rows + 2 * BLK, LANES), F32)
    keep, send = call(
        functools.partial(first_kernel, n, own, slab),
        [both_shape, both_shape],
        [*x_rows, *a_own, *p_own],
        [place, p_pairs.reshape(-1), a_cols.reshape(-1)],
        [pltpu.VMEM((span, 2 * LANES), BF16)],
        flops=prod_flops,
    )
    msg, ppx = call(meet_kernel, [slab_shape, pp_shape], [keep, to_core(send)])
    a_far, t_far, p_far, diag_other = prepare(
        a_other, p_other, ints_other[:count], ints_other[count:], after=msg
    )
    a_mats, t_mats, p_mats = [*a_own, *a_far], [*t_own, *t_far], [*p_own, *p_far]
    pairs = jnp.concatenate([p_pairs.reshape(-1), ints_other[count:]])
    cols = jnp.concatenate([a_cols.reshape(-1), ints_other[:count]])

    def forward(msgs, scalars, pp_first=()):
        return call(
            functools.partial(forward_kernel, n, own, slab, scalars),
            [((half_rows + SC, LANES), F32), pp_shape],
            [*msgs, *a_mats, *p_mats, *pp_first],
            [place, pairs, cols],
            total_scratch + [pltpu.VMEM((2 * span, LANES), BF16)],
            flops=prod_flops,
        )

    *pieces, ax = call(
        functools.partial(start_back_kernel, n, nx, own),
        [((own + 2 * n_range, LANES), F32)] * n + [((half_rows, LANES), F32)],
        [*to_x(msg), z, y, ppx, diag, diag_other, *t_mats],
        [place, pairs],
        total_scratch,
        flops=prod_flops,
    )
    for outer in range(ADMM_ITERS):
        if outer == 0:
            msg1, r, dk = call(
                functools.partial(residual_kernel, n, own, True),
                [msg_shape, own_shape, own_shape],
                [*to_row(pieces), x, q, pd],
                [place],
                total_scratch,
            )
        else:
            msg1, r = call(
                functools.partial(residual_kernel, n, own, False),
                [msg_shape, own_shape],
                [*to_row(pieces), x, q, pd, dk],
                [place],
            )
        msg, pp1 = forward(to_all_rows(msg1), 1)
        *pieces, ad, scal = call(
            functools.partial(step_back_kernel, n, nx, own),
            [msg_shape] * n + [slab_shape, tile_shape],
            [*to_x(msg), pp1, *t_mats],
            [place, pairs],
            total_scratch,
            flops=prod_flops,
        )
        msg2, step = call(
            functools.partial(step_kernel, n, own),
            [msg_shape, tile_shape],
            [*to_row(pieces), scal, msg1, r, pd, dk],
        )
        msg, pp2 = forward(to_all_rows(msg2), 2, (pp1,))
        ad2, share, keep = call(
            functools.partial(curve_kernel, nx),
            [slab_shape, tile_shape, tile_shape],
            [*to_x(msg), scal, ad],
        )
        shares = to_all_rows(share)
        state = [*shares, keep, step, ax, ad, ad2, z, y, lower, upper, x, msg1, msg2]
        if outer + 1 < ADMM_ITERS:
            *pieces, x, z, y, ax, ppx = call(
                functools.partial(update_kernel, n, own),
                [own_shape] * n + [own_shape, slab_shape, slab_shape, slab_shape, ((2 * BLK, LANES), F32)],
                [*state, ppx, pp1, pp2, *t_mats],
                [place, pairs],
                total_scratch,
                flops=prod_flops,
            )
        else:
            (out,) = call(
                functools.partial(last_kernel, n, own), [((2 * half_rows + own, LANES), F32)], state
            )
    return call(
        finish_kernel,
        [own_shape, ((slab_rows, LANES), F32), ((slab_rows, LANES), F32)],
        [out, to_core(out)],
        [place],
    )


def solution(mesh):
    placed = (
        P(("col", "row"), "grp"),
        P(("col", "row"), "grp"),
        P(("col", "row")),
        P("row", "grp"),
        P("row", "grp"),
        P("row", "grp"),
        P("row", "grp"),
        P("row", "col", None, None),
        P("row", "col"),
        P("col", "row", None, None),
        P("col", "row", None),
    )

    def run(*args):
        return tuple(local(*args))

    return jax.shard_map(
        run,
        mesh=mesh,
        in_specs=placed,
        out_specs=(P(("col", "row"), "grp"), P("row", "grp"), P("row", "grp")),
        check_vma=False,
    )
```

```python
import functools

import jax
import jax.numpy as jnp
from jax import lax
from jax.experimental import pallas as pl
from jax.experimental.pallas import tpu as pltpu
from jax.sharding import PartitionSpec as P

ADMM_ITERS = 2
RHO = 0.5
SIGMA = 1e-06
RELAX = 1.6
BLK = 128
LANES = 128
HALF = 64
SC = 8
F32 = jnp.float32
BF16 = jnp.bfloat16

VMEM = pl.BlockSpec(memory_space=pltpu.VMEM)
SMEM = pl.BlockSpec(memory_space=pltpu.SMEM)

ANY = pl.BlockSpec(memory_space=pl.ANY)


def call(body, outs, ins, smem=(), scratch=(), flops=0, after=None):
    n_bytes = sum(v.size * v.dtype.itemsize for v in ins)
    tied = [] if after is None else [after]

    def run(*refs):
        body(*refs[len(tied) :])

    return pl.pallas_call(
        run,
        out_shape=[jax.ShapeDtypeStruct(s, d) for s, d in outs],
        in_specs=[ANY] * len(tied) + [SMEM] * len(smem) + [VMEM] * len(ins),
        out_specs=[VMEM] * len(outs),
        scratch_shapes=list(scratch),
        compiler_params=pltpu.CompilerParams(vmem_limit_bytes=30 * 1024 * 1024),
        cost_estimate=pl.CostEstimate(flops=flops, bytes_accessed=n_bytes, transcendentals=0),
    )(*tied, *smem, *ins)


def low_half(shape):
    return lax.broadcasted_iota(jnp.int32, shape, 1) < HALF


def turn(v):
    return pltpu.roll(v, HALF, 1)


def fold(v):
    return v + turn(v)


def col_sum(v):
    return fold(jnp.sum(v, axis=0, keepdims=True))


def split_bf16(v):
    hi = v.astype(BF16).astype(F32)
    return hi, v - hi


def pair_up(v):
    hi, lo = split_bf16(v)
    low = low_half(v.shape)
    first = jnp.where(low, hi, turn(lo)).astype(BF16)
    second = jnp.where(low, turn(hi), lo).astype(BF16)
    return first, second


def dot(a, b):
    return jnp.dot(a, b, preferred_element_type=F32)


def pack_rows(*rows):
    at = lax.broadcasted_iota(jnp.int32, (SC, LANES), 0)
    tile = jnp.zeros((SC, LANES), F32)
    for k, row in enumerate(rows):
        tile = jnp.where(at == k, row, tile)
    return tile


def mix_cores(core, mine, other):
    low = low_half(mine.shape)
    a = jnp.where(core == 0, mine, turn(mine))
    b = jnp.where(core == 0, turn(other), other)
    return jnp.where(low, a, b)


def own_kernel(place, x, x_other, q, q_other, x_own, q_own):
    core = place[1]
    x_own[...] = mix_cores(core, x[...], x_other[...])
    q_own[...] = mix_cores(core, q[...], q_other[...])


def slab_kernel(place, *refs):
    core = place[1]
    count = len(refs) // 2
    for src, dst in zip(refs[:count], refs[count:]):
        rows = dst.shape[0]
        v = jnp.where(core == 0, src[...], turn(src[...]))
        dst[...] = jnp.where(low_half(dst.shape), v[:rows], turn(v[rows:]))


def prep_kernel(slab, per, cols, pairs, a_in, p_in, a_both, t_both, p_hi, p_lo, diag):
    diag[...] = jnp.zeros(diag.shape, F32)
    for m in range(slab):
        for s in range(per):
            k = m * per + s
            col = cols[k]
            block = a_in[k]
            hi, lo = split_bf16(block)
            a_both[2 * m * BLK : (2 * m + 1) * BLK, s * BLK : (s + 1) * BLK] = hi.astype(BF16)
            a_both[(2 * m + 1) * BLK : (2 * m + 2) * BLK, s * BLK : (s + 1) * BLK] = lo.astype(BF16)
            hi, lo = split_bf16(block.T)
            t_both[k * BLK : (k + 1) * BLK, :BLK] = hi.astype(BF16)
            t_both[k * BLK : (k + 1) * BLK, BLK:] = lo.astype(BF16)
            diag[pl.ds(col, 1), :] += RHO * jnp.sum(block * block, axis=0, keepdims=True)
    shape = (BLK, BLK)
    eye = lax.broadcasted_iota(jnp.int32, shape, 0) == lax.broadcasted_iota(jnp.int32, shape, 1)
    for e in range(4):
        hi, lo = split_bf16(p_in[e])
        rows = slice((e // 2) * BLK, (e // 2 + 1) * BLK)
        lanes = slice((e % 2) * BLK, (e % 2 + 1) * BLK)
        p_hi[rows, lanes] = hi.astype(BF16)
        p_lo[rows, lanes] = lo.astype(BF16)
    for e in range(2):
        diag[pl.ds(pairs[e], 1), :] += jnp.sum(jnp.where(eye, p_in[3 * e], 0.0), axis=0, keepdims=True)


def slab_product(slab, cols, a_refs, starts, wide):
    per = cols.shape[0] // (slab * len(a_refs))
    sums = []
    for m in range(slab):
        total = None
        for t, a_ref in enumerate(a_refs):
            blocks = []
            for s in range(per):
                at = starts[t] + cols[(t * slab + m) * per + s] * BLK
                blocks.append(wide[pl.ds(pl.multiple_of(at, BLK), BLK), :])
            part = dot(a_ref[2 * m * BLK : (2 * m + 2) * BLK, :], jnp.concatenate(blocks, axis=0))
            total = part if total is None else total + part
        sums.append(total[:BLK] + total[BLK:])
    return jnp.concatenate(sums, axis=0)


def first_kernel(n, own, slab, place, pairs, cols, *refs):
    msgs, (a_both, p_hi, p_lo, keep, send, wide) = refs[:n], refs[n:]
    core = place[1]
    for k in range(n):
        at = pl.multiple_of(lax.bitwise_xor(place[0], k) * own, own)
        hi, lo = split_bf16(msgs[k][...])
        wide[pl.ds(at, own), 0:LANES] = hi.astype(BF16)
        wide[pl.ds(at, own), LANES:] = lo.astype(BF16)
    total = slab_product(slab, cols, [a_both], [0], wide)
    total = total[:, :LANES] + total[:, LANES:]
    rows = total.shape[0] // 2
    keep[0:rows, :] = mix_cores(core, total[:rows], total[rows:])
    send[0:rows, :] = mix_cores(1 - core, total[:rows], total[rows:])
    at_i = pl.ds(pl.multiple_of(pairs[0] * BLK, BLK), BLK)
    at_j = pl.ds(pl.multiple_of(pairs[1] * BLK, BLK), BLK)
    v = jnp.concatenate([wide[at_i, :], wide[at_j, :]], axis=0)
    part = dot(p_hi[...], v) + dot(p_lo[...], v)
    part = part[:, :LANES] + part[:, LANES:]
    part = jnp.where(core == 0, part, turn(part))
    keep[rows:, :] = part
    send[rows:, :] = part


def meet_kernel(keep, got, msg, pp):
    rows = msg.shape[0]
    msg[...] = keep[0:rows, :] + got[0:rows, :]
    pp[...] = jnp.where(low_half(pp.shape), keep[rows:, :], got[rows:, :])


def forward_kernel(n, own, slab, scalars, place, pairs, cols, *refs):
    msgs, rest = refs[:n], refs[n:]
    a_mats, p_mats, rest = rest[:2], rest[2:6], rest[6:]
    if scalars == 2:
        pp_first, rest = rest[0], rest[1:]
    msg, pp, whole, wide = rest
    row = place[0]
    span = whole.shape[0]
    for k in range(n):
        at = pl.multiple_of(lax.bitwise_xor(row, k) * own, own)
        v = msgs[k][0:own, :]
        whole[pl.ds(at, own), :] = v
        first, second = pair_up(v)
        wide[pl.ds(at, own), :] = first
        wide[pl.ds(pl.multiple_of(span + at, own), own), :] = second
    total = fold(slab_product(slab, cols, a_mats, [0, span], wide))
    rows = total.shape[0] // 2
    msg[0:rows, :] = jnp.where(low_half((rows, LANES)), total[:rows], total[rows:])
    parts = []
    for t in range(2):
        at_i = pl.multiple_of(t * span + pairs[2 * t] * BLK, BLK)
        at_j = pl.multiple_of(t * span + pairs[2 * t + 1] * BLK, BLK)
        v = jnp.concatenate([wide[pl.ds(at_i, BLK), :], wide[pl.ds(at_j, BLK), :]], axis=0)
        parts.append(fold(dot(p_mats[2 * t][...], v) + dot(p_mats[2 * t + 1][...], v)))
    low2 = low_half((2 * BLK, LANES))
    pp_now = jnp.where(low2, parts[0], parts[1])
    pp[...] = pp_now
    picked = []
    for t in range(2):
        at_i = pl.multiple_of(pairs[2 * t] * BLK, BLK)
        at_j = pl.multiple_of(pairs[2 * t + 1] * BLK, BLK)
        picked.append(jnp.concatenate([whole[pl.ds(at_i, BLK), :], whole[pl.ds(at_j, BLK), :]], axis=0))
    vec = jnp.where(low2, picked[0], picked[1])
    tile = msgs[0][own : own + SC, :]
    for k in range(1, n):
        tile = tile + msgs[k][own : own + SC, :]
    tile = fold(tile)
    at = lax.broadcasted_iota(jnp.int32, (SC, LANES), 0)
    tile = jnp.where(at == 3, col_sum(vec * pp_now), tile)
    if scalars == 2:
        tile = jnp.where(at == 4, col_sum(vec * pp_first[...]), tile)
    msg[rows : rows + SC, :] = tile


def back_product(n, own, place, pairs, cols, w, pp_now, t_mats, total, outs, extra=()):
    row = place[0]
    span = total.shape[0] // 2
    wide = jnp.concatenate(pair_up(w), axis=0)
    slab = wide.shape[0] // BLK
    per = t_mats[0].shape[0] // wide.shape[0]
    for t in range(2):
        total[t * span : (t + 1) * span, :] = jnp.zeros((span, LANES), F32)
    for m in range(slab):
        v = wide[m * BLK : (m + 1) * BLK]
        v = jnp.concatenate([v, v], axis=0)
        for t in range(2):
            part = dot(t_mats[t][m * per * BLK : (m + 1) * per * BLK, :], v)
            for s in range(per):
                at = t * span + cols[(t * slab + m) * per + s] * BLK
                total[pl.ds(pl.multiple_of(at, BLK), BLK), :] += part[s * BLK : (s + 1) * BLK]
    total[0:span, :] = jnp.where(low_half((span, LANES)), fold(total[0:span, :]), fold(total[span:, :]))
    low1 = low_half((BLK, LANES))
    for t in range(2):
        side = low1 if t == 0 else jnp.logical_not(low1)
        for e in range(2):
            at = pl.ds(pl.multiple_of(pairs[2 * t + e] * BLK, BLK), BLK)
            total[at, :] += jnp.where(side, pp_now[e * BLK : (e + 1) * BLK], 0.0)
    for k in range(n):
        at = pl.multiple_of(lax.bitwise_xor(row, k) * own, own)
        outs[k][0:own, :] = total[pl.ds(at, own), :]
        at = own
        for rows in extra:
            outs[k][at : at + rows.shape[0], :] = rows
            at += rows.shape[0]


def start_back_kernel(n, nx, own, place, pairs, cols, *refs):
    msgs, rest = refs[:nx], refs[nx:]
    z, y, pp, diag, diag_other, *t_mats = rest[:7]
    outs, (ax, total) = rest[7 : 7 + n], rest[7 + n :]
    ax_now = msgs[0][...]
    for k in range(1, nx):
        ax_now = ax_now + msgs[k][...]
    ax[...] = ax_now
    w = RHO * ax_now - (RHO * z[...] - y[...])
    back_product(n, own, place, pairs, cols, w, pp[...], t_mats, total, outs, (diag[...], diag_other[...]))


def step_back_kernel(n, nx, own, place, pairs, cols, *refs):
    msgs, rest = refs[:nx], refs[nx:]
    pp, *t_mats = rest[:3]
    outs, (ad, scal, total) = rest[3 : 3 + n], rest[3 + n :]
    rows = ad.shape[0]
    v = msgs[0][...]
    for k in range(1, nx):
        v = v + msgs[k][...]
    ad_now = v[:rows]
    tile = v[rows:]
    ad[...] = ad_now
    scal[...] = tile
    curve = RHO * col_sum(ad_now * ad_now) + tile[3:4]
    back_product(n, own, place, pairs, cols, RHO * ad_now, pp[...], t_mats, total, outs, (pack_rows(curve),))


def residual_kernel(n, own, first, place, *refs):
    msgs, rest = refs[:n], refs[n:]
    if first:
        x, q, pd, msg, res, dk, full = rest
        rows = msgs[0].shape[0] - own
        tile = msgs[0][own:, :]
        for k in range(1, n):
            tile = tile + msgs[k][own:, :]
        n_range = rows // 2
        low1 = low_half((BLK, LANES))
        for b in range(n_range):
            mine = jnp.broadcast_to(tile[b : b + 1], (BLK, LANES)).T
            other = jnp.broadcast_to(tile[n_range + b : n_range + b + 1], (BLK, LANES)).T
            full[b * BLK : (b + 1) * BLK, :] = jnp.where(low1, mine, other)
        at = pl.multiple_of(place[0] * own, own)
        diag = pd[...] + SIGMA + full[pl.ds(at, own), :]
        dk[...] = diag
    else:
        x, q, pd, dk, msg, res = rest
        diag = dk[...]
    total = msgs[0][0:own, :]
    for k in range(1, n):
        total = total + msgs[k][0:own, :]
    r = -q[...] - pd[...] * x[...] - total
    s = r / diag
    res[...] = r
    msg[0:own, :] = s
    shift = pd[...] + SIGMA
    rz = jnp.sum(r * s, axis=0, keepdims=True)
    dd = jnp.sum(shift * s * s, axis=0, keepdims=True)
    msg[own : own + SC, :] = pack_rows(rz, dd)


def step_kernel(n, own, *refs):
    msgs, rest = refs[:n], refs[n:]
    scal, prev, r, pd, dk, msg, step_out = rest
    total = msgs[0][...]
    for k in range(1, n):
        total = total + msgs[k][...]
    shift = pd[...] + SIGMA
    d = prev[0:own, :]
    kd = shift * d + total[:own]
    curve = total[own : own + 1] + scal[1:2, :]
    step = scal[0:1, :] / curve
    r_new = r[...] - step * kd
    s = r_new / dk[...]
    msg[0:own, :] = s
    rz = jnp.sum(r_new * s, axis=0, keepdims=True)
    ss = jnp.sum(shift * s * s, axis=0, keepdims=True)
    sd = jnp.sum(shift * s * d, axis=0, keepdims=True)
    msg[own : own + SC, :] = pack_rows(rz, ss, sd)
    step_out[...] = jnp.broadcast_to(step, step_out.shape)


def curve_kernel(nx, *refs):
    msgs, rest = refs[:nx], refs[nx:]
    scal, ad, ad2, share, keep = rest
    rows = ad.shape[0]
    v = msgs[0][...]
    for k in range(1, nx):
        v = v + msgs[k][...]
    tile = v[rows:]
    beta = tile[0:1] / scal[0:1, :]
    ad_now = v[:rows] + beta * ad[...]
    ad2[...] = ad_now
    flat = tile[1:2] + 2.0 * beta * tile[2:3] + beta * beta * scal[1:2, :]
    pair = tile[3:4] + 2.0 * beta * tile[4:5] + beta * beta * scal[3:4, :]
    share[...] = pack_rows(RHO * col_sum(ad_now * ad_now) + pair)
    keep[...] = pack_rows(tile[0:1], beta, flat)


def admm_update(n, own, refs):
    shares, rest = refs[:n], refs[n:]
    keep, step_in, ax, ad, ad2, z, y, lower, upper, x, msg1, msg2 = rest[:12]
    tile = shares[0][...]
    for k in range(1, n):
        tile = tile + shares[k][...]
    beta = keep[1:2, :]
    step1 = step_in[0:1, :]
    step2 = keep[0:1, :] / (tile[0:1] + keep[2:3, :])
    d1 = msg1[0:own, :]
    d2 = msg2[0:own, :] + beta * d1
    x_hat = x[...] + step1 * d1 + step2 * d2
    x_new = RELAX * x_hat + (1.0 - RELAX) * x[...]
    ax_hat = ax[...] + step1 * ad[...] + step2 * ad2[...]
    relaxed = RELAX * ax_hat + (1.0 - RELAX) * z[...]
    z_new = jnp.clip(relaxed + y[...] / RHO, lower[...], upper[...])
    y_new = y[...] + RHO * (relaxed - z_new)
    return beta, step1, step2, x_new, ax_hat, z_new, y_new, rest[12:]


def update_kernel(n, own, place, pairs, cols, *refs):
    beta, step1, step2, x_new, ax_hat, z_new, y_new, rest = admm_update(n, own, refs)
    ax = refs[n + 2]
    ppx, pp1, pp2, *t_mats = rest[:5]
    outs, (x_out, z_out, y_out, ax_out, ppx_out, total) = rest[5 : 5 + n], rest[5 + n :]
    x_out[...] = x_new
    z_out[...] = z_new
    y_out[...] = y_new
    ax_new = RELAX * ax_hat + (1.0 - RELAX) * ax[...]
    ax_out[...] = ax_new
    pp_hat = ppx[...] + step1 * pp1[...] + step2 * (pp2[...] + beta * pp1[...])
    pp_new = RELAX * pp_hat + (1.0 - RELAX) * ppx[...]
    ppx_out[...] = pp_new
    w = RHO * ax_new - (RHO * z_new - y_new)
    back_product(n, own, place, pairs, cols, w, pp_new, t_mats, total, outs)


def last_kernel(n, own, *refs):
    _, _, _, x_new, _, z_new, y_new, rest = admm_update(n, own, refs)
    (out,) = rest
    rows = z_new.shape[0]
    out[0:rows, :] = z_new
    out[rows : 2 * rows, :] = y_new
    out[2 * rows :, :] = x_new


def finish_kernel(place, mine, got, x, z, y):
    core = place[1]
    rows = z.shape[0] // 2
    for k, dst in enumerate((z, y)):
        a = mine[k * rows : (k + 1) * rows, :]
        b = got[k * rows : (k + 1) * rows, :]
        low = low_half(a.shape)
        left = jnp.where(core == 0, a, b)
        right = jnp.where(core == 0, b, a)
        dst[0:rows, :] = jnp.where(low, left, turn(right))
        dst[rows : 2 * rows, :] = jnp.where(low, turn(left), right)
    a = mine[2 * rows :, :]
    b = got[2 * rows :, :]
    low = low_half(a.shape)
    x[...] = jnp.where(core == 0, jnp.where(low, a, b), jnp.where(low, turn(b), turn(a)))


def local(x_state, q_lin, p_diag, z_state, y_state, lower_bound, upper_bound, a_blocks, a_cols, p_blocks, p_pairs):
    slab, per = a_cols.shape
    n = lax.axis_size("row")
    n_col = lax.axis_size("col")
    nx = n_col // 2
    own = x_state.shape[0]
    span = own * n
    n_range = span // BLK
    slab_rows = slab * BLK
    half_rows = slab_rows // 2
    row_at = lax.axis_index("row")
    core_at = lax.axis_index("col") % 2
    place = jnp.stack([row_at, core_at]).astype(jnp.int32)

    def to_core(v):
        return lax.ppermute(v, "col", [(c, c ^ 1) for c in range(n_col)])

    def to_x(v):
        return [v] + [lax.ppermute(v, "col", [(c, c ^ (2 * k)) for c in range(n_col)]) for k in range(1, nx)]

    ks = range(1, n)
    scatter_ks = (2, 1, 3) if n == 4 else ks

    def over_row(v, k):
        return lax.ppermute(v, "row", [(i, i ^ k) for i in range(n)])

    def to_row(pieces):
        return [pieces[0]] + [over_row(pieces[k], k) for k in scatter_ks]

    def to_all_rows(v):
        return [v] + [over_row(v, k) for k in ks]

    a_mine = a_blocks.reshape(slab * per, BLK, BLK)
    p_mine = p_blocks.reshape(4, BLK, BLK)
    ints = jnp.concatenate([a_cols.reshape(-1), p_pairs.reshape(-1)])
    x_rows = to_all_rows(x_state)
    a_other = to_core(a_mine)
    ints_other = to_core(ints)
    p_other = to_core(p_mine)
    pd_other = to_core(p_diag)
    count = slab * per
    pd = jnp.concatenate(
        [jnp.broadcast_to(p_diag[:, None], (own, HALF)), jnp.broadcast_to(pd_other[:, None], (own, HALF))], axis=1
    )
    x, q = call(
        own_kernel, [((own, LANES), F32)] * 2, [x_state, to_core(x_state), q_lin, to_core(q_lin)], [place]
    )
    z, y, lower, upper = call(
        slab_kernel, [((half_rows, LANES), F32)] * 4, [z_state, y_state, lower_bound, upper_bound], [place]
    )
    own_shape = ((own, LANES), F32)
    msg_shape = ((own + SC, LANES), F32)
    tile_shape = ((SC, LANES), F32)
    slab_shape = ((half_rows, LANES), F32)
    pp_shape = ((2 * BLK, LANES), F32)

    def prepare(a, p, at_cols, at_pairs, after=None):
        *mats, diag = call(
            functools.partial(prep_kernel, slab, per),
            [((2 * slab_rows, per * BLK), BF16)]
            + [((slab * per * BLK, 2 * BLK), BF16)]
            + [((2 * BLK, 2 * BLK), BF16)] * 2
            + [((n_range, LANES), F32)],
            [a, p],
            [at_cols, at_pairs],
            flops=10**8,
            after=after,
        )
        return mats[0:1], mats[1:2], mats[2:4], diag

    prod_flops = 4 * slab_rows * 2 * span * LANES
    total_scratch = [pltpu.VMEM((span, LANES), F32)]
    back_scratch = [pltpu.VMEM((2 * span, LANES), F32)]
    a_own, t_own, p_own, diag = prepare(a_mine, p_mine, a_cols.reshape(-1), p_pairs.reshape(-1))
    both_shape = ((half_rows + 2 * BLK, LANES), F32)
    keep, send = call(
        functools.partial(first_kernel, n, own, slab),
        [both_shape, both_shape],
        [*x_rows, *a_own, *p_own],
        [place, p_pairs.reshape(-1), a_cols.reshape(-1)],
        [pltpu.VMEM((span, 2 * LANES), BF16)],
        flops=prod_flops,
    )
    msg, ppx = call(meet_kernel, [slab_shape, pp_shape], [keep, to_core(send)])
    a_far, t_far, p_far, diag_other = prepare(
        a_other, p_other, ints_other[:count], ints_other[count:], after=msg
    )
    a_mats, t_mats, p_mats = [*a_own, *a_far], [*t_own, *t_far], [*p_own, *p_far]
    pairs = jnp.concatenate([p_pairs.reshape(-1), ints_other[count:]])
    cols = jnp.concatenate([a_cols.reshape(-1), ints_other[:count]])

    def forward(msgs, scalars, pp_first=()):
        return call(
            functools.partial(forward_kernel, n, own, slab, scalars),
            [((half_rows + SC, LANES), F32), pp_shape],
            [*msgs, *a_mats, *p_mats, *pp_first],
            [place, pairs, cols],
            total_scratch + [pltpu.VMEM((2 * span, LANES), BF16)],
            flops=prod_flops,
        )

    *pieces, ax = call(
        functools.partial(start_back_kernel, n, nx, own),
        [((own + 2 * n_range, LANES), F32)] * n + [((half_rows, LANES), F32)],
        [*to_x(msg), z, y, ppx, diag, diag_other, *t_mats],
        [place, pairs, cols],
        back_scratch,
        flops=prod_flops,
    )
    for outer in range(ADMM_ITERS):
        if outer == 0:
            msg1, r, dk = call(
                functools.partial(residual_kernel, n, own, True),
                [msg_shape, own_shape, own_shape],
                [*to_row(pieces), x, q, pd],
                [place],
                total_scratch,
            )
        else:
            msg1, r = call(
                functools.partial(residual_kernel, n, own, False),
                [msg_shape, own_shape],
                [*to_row(pieces), x, q, pd, dk],
                [place],
            )
        msg, pp1 = forward(to_all_rows(msg1), 1)
        *pieces, ad, scal = call(
            functools.partial(step_back_kernel, n, nx, own),
            [msg_shape] * n + [slab_shape, tile_shape],
            [*to_x(msg), pp1, *t_mats],
            [place, pairs, cols],
            back_scratch,
            flops=prod_flops,
        )
        msg2, step = call(
            functools.partial(step_kernel, n, own),
            [msg_shape, tile_shape],
            [*to_row(pieces), scal, msg1, r, pd, dk],
        )
        msg, pp2 = forward(to_all_rows(msg2), 2, (pp1,))
        ad2, share, keep = call(
            functools.partial(curve_kernel, nx),
            [slab_shape, tile_shape, tile_shape],
            [*to_x(msg), scal, ad],
        )
        shares = to_all_rows(share)
        state = [*shares, keep, step, ax, ad, ad2, z, y, lower, upper, x, msg1, msg2]
        if outer + 1 < ADMM_ITERS:
            *pieces, x, z, y, ax, ppx = call(
                functools.partial(update_kernel, n, own),
                [own_shape] * n + [own_shape, slab_shape, slab_shape, slab_shape, ((2 * BLK, LANES), F32)],
                [*state, ppx, pp1, pp2, *t_mats],
                [place, pairs, cols],
                back_scratch,
                flops=prod_flops,
            )
        else:
            (out,) = call(
                functools.partial(last_kernel, n, own), [((2 * half_rows + own, LANES), F32)], state
            )
    return call(
        finish_kernel,
        [own_shape, ((slab_rows, LANES), F32), ((slab_rows, LANES), F32)],
        [out, to_core(out)],
        [place],
    )


def solution(mesh):
    placed = (
        P(("col", "row"), "grp"),
        P(("col", "row"), "grp"),
        P(("col", "row")),
        P("row", "grp"),
        P("row", "grp"),
        P("row", "grp"),
        P("row", "grp"),
        P("row", "col", None, None),
        P("row", "col"),
        P("col", "row", None, None),
        P("col", "row", None),
    )

    def run(*args):
        return tuple(local(*args))

    return jax.shard_map(
        run,
        mesh=mesh,
        in_specs=placed,
        out_specs=(P(("col", "row"), "grp"), P("row", "grp"), P("row", "grp")),
        check_vma=False,
    )
```

```python
import functools

import jax
import jax.numpy as jnp
from jax import lax
from jax.experimental import pallas as pl
from jax.experimental.pallas import tpu as pltpu
from jax.sharding import PartitionSpec as P

ADMM_ITERS = 2
RHO = 0.5
SIGMA = 1e-06
RELAX = 1.6
BLK = 128
LANES = 128
HALF = 64
SC = 8
F32 = jnp.float32
BF16 = jnp.bfloat16

VMEM = pl.BlockSpec(memory_space=pltpu.VMEM)
SMEM = pl.BlockSpec(memory_space=pltpu.SMEM)

ANY = pl.BlockSpec(memory_space=pl.ANY)


def call(body, outs, ins, smem=(), scratch=(), flops=0, after=None):
    n_bytes = sum(v.size * v.dtype.itemsize for v in ins)
    tied = [] if after is None else [after]

    def run(*refs):
        body(*refs[len(tied) :])

    return pl.pallas_call(
        run,
        out_shape=[jax.ShapeDtypeStruct(s, d) for s, d in outs],
        in_specs=[ANY] * len(tied) + [SMEM] * len(smem) + [VMEM] * len(ins),
        out_specs=[VMEM] * len(outs),
        scratch_shapes=list(scratch),
        compiler_params=pltpu.CompilerParams(vmem_limit_bytes=30 * 1024 * 1024),
        cost_estimate=pl.CostEstimate(flops=flops, bytes_accessed=n_bytes, transcendentals=0),
    )(*tied, *smem, *ins)


def low_half(shape):
    return lax.broadcasted_iota(jnp.int32, shape, 1) < HALF


def turn(v):
    return pltpu.roll(v, HALF, 1)


def fold(v):
    return v + turn(v)


def col_sum(v):
    return fold(jnp.sum(v, axis=0, keepdims=True))


def split_bf16(v):
    hi = v.astype(BF16).astype(F32)
    return hi, v - hi


def pair_up(v):
    hi, lo = split_bf16(v)
    low = low_half(v.shape)
    first = jnp.where(low, hi, turn(lo)).astype(BF16)
    second = jnp.where(low, turn(hi), lo).astype(BF16)
    return first, second


def dot(a, b):
    return jnp.dot(a, b, preferred_element_type=F32)


def pack_rows(*rows):
    at = lax.broadcasted_iota(jnp.int32, (SC, LANES), 0)
    tile = jnp.zeros((SC, LANES), F32)
    for k, row in enumerate(rows):
        tile = jnp.where(at == k, row, tile)
    return tile


def mix_cores(core, mine, other):
    low = low_half(mine.shape)
    a = jnp.where(core == 0, mine, turn(mine))
    b = jnp.where(core == 0, turn(other), other)
    return jnp.where(low, a, b)


def own_kernel(place, x, x_other, q, q_other, x_own, q_own):
    core = place[1]
    x_own[...] = mix_cores(core, x[...], x_other[...])
    q_own[...] = mix_cores(core, q[...], q_other[...])


def slab_kernel(place, *refs):
    core = place[1]
    count = len(refs) // 2
    for src, dst in zip(refs[:count], refs[count:]):
        rows = dst.shape[0]
        v = jnp.where(core == 0, src[...], turn(src[...]))
        dst[...] = jnp.where(low_half(dst.shape), v[:rows], turn(v[rows:]))


def prep_kernel(slab, per, cols, pairs, a_in, p_in, a_both, t_hi, t_lo, p_hi, p_lo, diag):
    for ref in (t_hi, t_lo):
        ref[...] = jnp.zeros(ref.shape, BF16)
    diag[...] = jnp.zeros(diag.shape, F32)
    for m in range(slab):
        rows = slice(m * BLK, (m + 1) * BLK)
        for s in range(per):
            k = m * per + s
            col = cols[k]
            at = pl.multiple_of(col * BLK, BLK)
            block = a_in[k]
            hi, lo = split_bf16(block)
            a_both[2 * m * BLK : (2 * m + 1) * BLK, s * BLK : (s + 1) * BLK] = hi.astype(BF16)
            a_both[(2 * m + 1) * BLK : (2 * m + 2) * BLK, s * BLK : (s + 1) * BLK] = lo.astype(BF16)
            hi, lo = split_bf16(block.T)
            t_hi[pl.ds(at, BLK), rows] = hi.astype(BF16)
            t_lo[pl.ds(at, BLK), rows] = lo.astype(BF16)
            diag[pl.ds(col, 1), :] += RHO * jnp.sum(block * block, axis=0, keepdims=True)
    shape = (BLK, BLK)
    eye = lax.broadcasted_iota(jnp.int32, shape, 0) == lax.broadcasted_iota(jnp.int32, shape, 1)
    for e in range(4):
        hi, lo = split_bf16(p_in[e])
        rows = slice((e // 2) * BLK, (e // 2 + 1) * BLK)
        lanes = slice((e % 2) * BLK, (e % 2 + 1) * BLK)
        p_hi[rows, lanes] = hi.astype(BF16)
        p_lo[rows, lanes] = lo.astype(BF16)
    for e in range(2):
        diag[pl.ds(pairs[e], 1), :] += jnp.sum(jnp.where(eye, p_in[3 * e], 0.0), axis=0, keepdims=True)


def slab_product(slab, cols, a_refs, starts, wide):
    per = cols.shape[0] // (slab * len(a_refs))
    sums = []
    for m in range(slab):
        total = None
        for t, a_ref in enumerate(a_refs):
            blocks = []
            for s in range(per):
                at = starts[t] + cols[(t * slab + m) * per + s] * BLK
                blocks.append(wide[pl.ds(pl.multiple_of(at, BLK), BLK), :])
            part = dot(a_ref[2 * m * BLK : (2 * m + 2) * BLK, :], jnp.concatenate(blocks, axis=0))
            total = part if total is None else total + part
        sums.append(total[:BLK] + total[BLK:])
    return jnp.concatenate(sums, axis=0)


def first_kernel(n, own, slab, place, pairs, cols, *refs):
    msgs, (a_both, p_hi, p_lo, keep, send, wide) = refs[:n], refs[n:]
    core = place[1]
    for k in range(n):
        at = pl.multiple_of(lax.bitwise_xor(place[0], k) * own, own)
        hi, lo = split_bf16(msgs[k][...])
        wide[pl.ds(at, own), 0:LANES] = hi.astype(BF16)
        wide[pl.ds(at, own), LANES:] = lo.astype(BF16)
    total = slab_product(slab, cols, [a_both], [0], wide)
    total = total[:, :LANES] + total[:, LANES:]
    rows = total.shape[0] // 2
    keep[0:rows, :] = mix_cores(core, total[:rows], total[rows:])
    send[0:rows, :] = mix_cores(1 - core, total[:rows], total[rows:])
    at_i = pl.ds(pl.multiple_of(pairs[0] * BLK, BLK), BLK)
    at_j = pl.ds(pl.multiple_of(pairs[1] * BLK, BLK), BLK)
    v = jnp.concatenate([wide[at_i, :], wide[at_j, :]], axis=0)
    part = dot(p_hi[...], v) + dot(p_lo[...], v)
    part = part[:, :LANES] + part[:, LANES:]
    part = jnp.where(core == 0, part, turn(part))
    keep[rows:, :] = part
    send[rows:, :] = part


def meet_kernel(keep, got, msg, pp):
    rows = msg.shape[0]
    msg[...] = keep[0:rows, :] + got[0:rows, :]
    pp[...] = jnp.where(low_half(pp.shape), keep[rows:, :], got[rows:, :])


def forward_kernel(n, own, slab, scalars, place, pairs, cols, *refs):
    msgs, rest = refs[:n], refs[n:]
    a_mats, p_mats, rest = rest[:2], rest[2:6], rest[6:]
    if scalars == 2:
        pp_first, rest = rest[0], rest[1:]
    msg, pp, whole, wide = rest
    row = place[0]
    span = whole.shape[0]
    for k in range(n):
        at = pl.multiple_of(lax.bitwise_xor(row, k) * own, own)
        v = msgs[k][0:own, :]
        whole[pl.ds(at, own), :] = v
        first, second = pair_up(v)
        wide[pl.ds(at, own), :] = first
        wide[pl.ds(pl.multiple_of(span + at, own), own), :] = second
    total = fold(slab_product(slab, cols, a_mats, [0, span], wide))
    rows = total.shape[0] // 2
    msg[0:rows, :] = jnp.where(low_half((rows, LANES)), total[:rows], total[rows:])
    parts = []
    for t in range(2):
        at_i = pl.multiple_of(t * span + pairs[2 * t] * BLK, BLK)
        at_j = pl.multiple_of(t * span + pairs[2 * t + 1] * BLK, BLK)
        v = jnp.concatenate([wide[pl.ds(at_i, BLK), :], wide[pl.ds(at_j, BLK), :]], axis=0)
        parts.append(fold(dot(p_mats[2 * t][...], v) + dot(p_mats[2 * t + 1][...], v)))
    low2 = low_half((2 * BLK, LANES))
    pp_now = jnp.where(low2, parts[0], parts[1])
    pp[...] = pp_now
    picked = []
    for t in range(2):
        at_i = pl.multiple_of(pairs[2 * t] * BLK, BLK)
        at_j = pl.multiple_of(pairs[2 * t + 1] * BLK, BLK)
        picked.append(jnp.concatenate([whole[pl.ds(at_i, BLK), :], whole[pl.ds(at_j, BLK), :]], axis=0))
    vec = jnp.where(low2, picked[0], picked[1])
    tile = msgs[0][own : own + SC, :]
    for k in range(1, n):
        tile = tile + msgs[k][own : own + SC, :]
    tile = fold(tile)
    at = lax.broadcasted_iota(jnp.int32, (SC, LANES), 0)
    tile = jnp.where(at == 3, col_sum(vec * pp_now), tile)
    if scalars == 2:
        tile = jnp.where(at == 4, col_sum(vec * pp_first[...]), tile)
    msg[rows : rows + SC, :] = tile


def back_product(n, own, place, pairs, w, pp_now, t_mats, total, outs, extra=()):
    row = place[0]
    span = total.shape[0]
    first, second = pair_up(w)
    wide = jnp.concatenate([first, second], axis=0)
    mine = fold(dot(t_mats[0][...], wide) + dot(t_mats[1][...], wide))
    other = fold(dot(t_mats[2][...], wide) + dot(t_mats[3][...], wide))
    total[...] = jnp.where(low_half((span, LANES)), mine, other)
    low1 = low_half((BLK, LANES))
    for t in range(2):
        side = low1 if t == 0 else jnp.logical_not(low1)
        for e in range(2):
            at = pl.ds(pl.multiple_of(pairs[2 * t + e] * BLK, BLK), BLK)
            total[at, :] += jnp.where(side, pp_now[e * BLK : (e + 1) * BLK], 0.0)
    for k in range(n):
        at = pl.multiple_of(lax.bitwise_xor(row, k) * own, own)
        outs[k][0:own, :] = total[pl.ds(at, own), :]
        at = own
        for rows in extra:
            outs[k][at : at + rows.shape[0], :] = rows
            at += rows.shape[0]


def start_back_kernel(n, nx, own, place, pairs, *refs):
    msgs, rest = refs[:nx], refs[nx:]
    z, y, pp, diag, diag_other, *t_mats = rest[:9]
    outs, (ax, total) = rest[9 : 9 + n], rest[9 + n :]
    ax_now = msgs[0][...]
    for k in range(1, nx):
        ax_now = ax_now + msgs[k][...]
    ax[...] = ax_now
    w = RHO * ax_now - (RHO * z[...] - y[...])
    back_product(n, own, place, pairs, w, pp[...], t_mats, total, outs, (diag[...], diag_other[...]))


def step_back_kernel(n, nx, own, place, pairs, *refs):
    msgs, rest = refs[:nx], refs[nx:]
    pp, *t_mats = rest[:5]
    outs, (ad, scal, total) = rest[5 : 5 + n], rest[5 + n :]
    rows = ad.shape[0]
    v = msgs[0][...]
    for k in range(1, nx):
        v = v + msgs[k][...]
    ad_now = v[:rows]
    tile = v[rows:]
    ad[...] = ad_now
    scal[...] = tile
    curve = RHO * col_sum(ad_now * ad_now) + tile[3:4]
    back_product(n, own, place, pairs, RHO * ad_now, pp[...], t_mats, total, outs, (pack_rows(curve),))


def residual_kernel(n, own, first, place, *refs):
    msgs, rest = refs[:n], refs[n:]
    if first:
        x, q, pd, msg, res, dk, full = rest
        rows = msgs[0].shape[0] - own
        tile = msgs[0][own:, :]
        for k in range(1, n):
            tile = tile + msgs[k][own:, :]
        n_range = rows // 2
        low1 = low_half((BLK, LANES))
        for b in range(n_range):
            mine = jnp.broadcast_to(tile[b : b + 1], (BLK, LANES)).T
            other = jnp.broadcast_to(tile[n_range + b : n_range + b + 1], (BLK, LANES)).T
            full[b * BLK : (b + 1) * BLK, :] = jnp.where(low1, mine, other)
        at = pl.multiple_of(place[0] * own, own)
        diag = pd[...] + SIGMA + full[pl.ds(at, own), :]
        dk[...] = diag
    else:
        x, q, pd, dk, msg, res = rest
        diag = dk[...]
    total = msgs[0][0:own, :]
    for k in range(1, n):
        total = total + msgs[k][0:own, :]
    r = -q[...] - pd[...] * x[...] - total
    s = r / diag
    res[...] = r
    msg[0:own, :] = s
    shift = pd[...] + SIGMA
    rz = jnp.sum(r * s, axis=0, keepdims=True)
    dd = jnp.sum(shift * s * s, axis=0, keepdims=True)
    msg[own : own + SC, :] = pack_rows(rz, dd)


def step_kernel(n, own, *refs):
    msgs, rest = refs[:n], refs[n:]
    scal, prev, r, pd, dk, msg, step_out = rest
    total = msgs[0][...]
    for k in range(1, n):
        total = total + msgs[k][...]
    shift = pd[...] + SIGMA
    d = prev[0:own, :]
    kd = shift * d + total[:own]
    curve = total[own : own + 1] + scal[1:2, :]
    step = scal[0:1, :] / curve
    r_new = r[...] - step * kd
    s = r_new / dk[...]
    msg[0:own, :] = s
    rz = jnp.sum(r_new * s, axis=0, keepdims=True)
    ss = jnp.sum(shift * s * s, axis=0, keepdims=True)
    sd = jnp.sum(shift * s * d, axis=0, keepdims=True)
    msg[own : own + SC, :] = pack_rows(rz, ss, sd)
    step_out[...] = jnp.broadcast_to(step, step_out.shape)


def curve_kernel(nx, *refs):
    msgs, rest = refs[:nx], refs[nx:]
    scal, ad, ad2, share, keep = rest
    rows = ad.shape[0]
    v = msgs[0][...]
    for k in range(1, nx):
        v = v + msgs[k][...]
    tile = v[rows:]
    beta = tile[0:1] / scal[0:1, :]
    ad_now = v[:rows] + beta * ad[...]
    ad2[...] = ad_now
    flat = tile[1:2] + 2.0 * beta * tile[2:3] + beta * beta * scal[1:2, :]
    pair = tile[3:4] + 2.0 * beta * tile[4:5] + beta * beta * scal[3:4, :]
    share[...] = pack_rows(RHO * col_sum(ad_now * ad_now) + pair)
    keep[...] = pack_rows(tile[0:1], beta, flat)


def admm_update(n, own, refs):
    shares, rest = refs[:n], refs[n:]
    keep, step_in, ax, ad, ad2, z, y, lower, upper, x, msg1, msg2 = rest[:12]
    tile = shares[0][...]
    for k in range(1, n):
        tile = tile + shares[k][...]
    beta = keep[1:2, :]
    step1 = step_in[0:1, :]
    step2 = keep[0:1, :] / (tile[0:1] + keep[2:3, :])
    d1 = msg1[0:own, :]
    d2 = msg2[0:own, :] + beta * d1
    x_hat = x[...] + step1 * d1 + step2 * d2
    x_new = RELAX * x_hat + (1.0 - RELAX) * x[...]
    ax_hat = ax[...] + step1 * ad[...] + step2 * ad2[...]
    relaxed = RELAX * ax_hat + (1.0 - RELAX) * z[...]
    z_new = jnp.clip(relaxed + y[...] / RHO, lower[...], upper[...])
    y_new = y[...] + RHO * (relaxed - z_new)
    return beta, step1, step2, x_new, ax_hat, z_new, y_new, rest[12:]


def update_kernel(n, own, place, pairs, *refs):
    beta, step1, step2, x_new, ax_hat, z_new, y_new, rest = admm_update(n, own, refs)
    ax = refs[n + 2]
    ppx, pp1, pp2, *t_mats = rest[:7]
    outs, (x_out, z_out, y_out, ax_out, ppx_out, total) = rest[7 : 7 + n], rest[7 + n :]
    x_out[...] = x_new
    z_out[...] = z_new
    y_out[...] = y_new
    ax_new = RELAX * ax_hat + (1.0 - RELAX) * ax[...]
    ax_out[...] = ax_new
    pp_hat = ppx[...] + step1 * pp1[...] + step2 * (pp2[...] + beta * pp1[...])
    pp_new = RELAX * pp_hat + (1.0 - RELAX) * ppx[...]
    ppx_out[...] = pp_new
    w = RHO * ax_new - (RHO * z_new - y_new)
    back_product(n, own, place, pairs, w, pp_new, t_mats, total, outs)


def last_kernel(n, own, *refs):
    _, _, _, x_new, _, z_new, y_new, rest = admm_update(n, own, refs)
    (out,) = rest
    rows = z_new.shape[0]
    out[0:rows, :] = z_new
    out[rows : 2 * rows, :] = y_new
    out[2 * rows :, :] = x_new


def finish_kernel(place, mine, got, x, z, y):
    core = place[1]
    rows = z.shape[0] // 2
    for k, dst in enumerate((z, y)):
        a = mine[k * rows : (k + 1) * rows, :]
        b = got[k * rows : (k + 1) * rows, :]
        low = low_half(a.shape)
        left = jnp.where(core == 0, a, b)
        right = jnp.where(core == 0, b, a)
        dst[0:rows, :] = jnp.where(low, left, turn(right))
        dst[rows : 2 * rows, :] = jnp.where(low, turn(left), right)
    a = mine[2 * rows :, :]
    b = got[2 * rows :, :]
    low = low_half(a.shape)
    x[...] = jnp.where(core == 0, jnp.where(low, a, b), jnp.where(low, turn(b), turn(a)))


def local(x_state, q_lin, p_diag, z_state, y_state, lower_bound, upper_bound, a_blocks, a_cols, p_blocks, p_pairs):
    slab, per = a_cols.shape
    n = lax.axis_size("row")
    n_col = lax.axis_size("col")
    nx = n_col // 2
    own = x_state.shape[0]
    span = own * n
    n_range = span // BLK
    slab_rows = slab * BLK
    half_rows = slab_rows // 2
    row_at = lax.axis_index("row")
    core_at = lax.axis_index("col") % 2
    place = jnp.stack([row_at, core_at]).astype(jnp.int32)

    def to_core(v):
        return lax.ppermute(v, "col", [(c, c ^ 1) for c in range(n_col)])

    def to_x(v):
        return [v] + [lax.ppermute(v, "col", [(c, c ^ (2 * k)) for c in range(n_col)]) for k in range(1, nx)]

    ks = range(1, n)
    scalar_ks = (1, 3, 2) if n == 4 else ks

    def over_row(v, k):
        return lax.ppermute(v, "row", [(i, i ^ k) for i in range(n)])

    def to_row(pieces):
        return [pieces[0]] + [over_row(pieces[k], k) for k in ks]

    def to_all_rows(v):
        return [v] + [over_row(v, k) for k in ks]

    a_mine = a_blocks.reshape(slab * per, BLK, BLK)
    p_mine = p_blocks.reshape(4, BLK, BLK)
    ints = jnp.concatenate([a_cols.reshape(-1), p_pairs.reshape(-1)])
    x_rows = to_all_rows(x_state)
    a_other = to_core(a_mine)
    ints_other = to_core(ints)
    p_other = to_core(p_mine)
    pd_other = to_core(p_diag)
    count = slab * per
    pd = jnp.concatenate(
        [jnp.broadcast_to(p_diag[:, None], (own, HALF)), jnp.broadcast_to(pd_other[:, None], (own, HALF))], axis=1
    )
    x, q = call(
        own_kernel, [((own, LANES), F32)] * 2, [x_state, to_core(x_state), q_lin, to_core(q_lin)], [place]
    )
    z, y, lower, upper = call(
        slab_kernel, [((half_rows, LANES), F32)] * 4, [z_state, y_state, lower_bound, upper_bound], [place]
    )
    own_shape = ((own, LANES), F32)
    msg_shape = ((own + SC, LANES), F32)
    tile_shape = ((SC, LANES), F32)
    slab_shape = ((half_rows, LANES), F32)
    pp_shape = ((2 * BLK, LANES), F32)

    def prepare(a, p, at_cols, at_pairs, after=None):
        *mats, diag = call(
            functools.partial(prep_kernel, slab, per),
            [((2 * slab_rows, per * BLK), BF16)]
            + [((span, slab_rows), BF16)] * 2
            + [((2 * BLK, 2 * BLK), BF16)] * 2
            + [((n_range, LANES), F32)],
            [a, p],
            [at_cols, at_pairs],
            flops=10**8,
            after=after,
        )
        return mats[0:1], mats[1:3], mats[3:5], diag

    prod_flops = 4 * slab_rows * 2 * span * LANES
    total_scratch = [pltpu.VMEM((span, LANES), F32)]
    a_own, t_own, p_own, diag = prepare(a_mine, p_mine, a_cols.reshape(-1), p_pairs.reshape(-1))
    both_shape = ((half_rows + 2 * BLK, LANES), F32)
    keep, send = call(
        functools.partial(first_kernel, n, own, slab),
        [both_shape, both_shape],
        [*x_rows, *a_own, *p_own],
        [place, p_pairs.reshape(-1), a_cols.reshape(-1)],
        [pltpu.VMEM((span, 2 * LANES), BF16)],
        flops=prod_flops,
    )
    msg, ppx = call(meet_kernel, [slab_shape, pp_shape], [keep, to_core(send)])
    a_far, t_far, p_far, diag_other = prepare(
        a_other, p_other, ints_other[:count], ints_other[count:], after=msg
    )
    a_mats, t_mats, p_mats = [*a_own, *a_far], [*t_own, *t_far], [*p_own, *p_far]
    pairs = jnp.concatenate([p_pairs.reshape(-1), ints_other[count:]])
    cols = jnp.concatenate([a_cols.reshape(-1), ints_other[:count]])

    def forward(msgs, scalars, pp_first=()):
        return call(
            functools.partial(forward_kernel, n, own, slab, scalars),
            [((half_rows + SC, LANES), F32), pp_shape],
            [*msgs, *a_mats, *p_mats, *pp_first],
            [place, pairs, cols],
            total_scratch + [pltpu.VMEM((2 * span, LANES), BF16)],
            flops=prod_flops,
        )

    *pieces, ax = call(
        functools.partial(start_back_kernel, n, nx, own),
        [((own + 2 * n_range, LANES), F32)] * n + [((half_rows, LANES), F32)],
        [*to_x(msg), z, y, ppx, diag, diag_other, *t_mats],
        [place, pairs],
        total_scratch,
        flops=prod_flops,
    )
    for outer in range(ADMM_ITERS):
        if outer == 0:
            msg1, r, dk = call(
                functools.partial(residual_kernel, n, own, True),
                [msg_shape, own_shape, own_shape],
                [*to_row(pieces), x, q, pd],
                [place],
                total_scratch,
            )
        else:
            msg1, r = call(
                functools.partial(residual_kernel, n, own, False),
                [msg_shape, own_shape],
                [*to_row(pieces), x, q, pd, dk],
                [place],
            )
        msg, pp1 = forward(to_all_rows(msg1), 1)
        *pieces, ad, scal = call(
            functools.partial(step_back_kernel, n, nx, own),
            [msg_shape] * n + [slab_shape, tile_shape],
            [*to_x(msg), pp1, *t_mats],
            [place, pairs],
            total_scratch,
            flops=prod_flops,
        )
        msg2, step = call(
            functools.partial(step_kernel, n, own),
            [msg_shape, tile_shape],
            [*to_row(pieces), scal, msg1, r, pd, dk],
        )
        msg, pp2 = forward(to_all_rows(msg2), 2, (pp1,))
        ad2, share, keep = call(
            functools.partial(curve_kernel, nx),
            [slab_shape, tile_shape, tile_shape],
            [*to_x(msg), scal, ad],
        )
        shares = [share] + [over_row(share, k) for k in scalar_ks]
        state = [*shares, keep, step, ax, ad, ad2, z, y, lower, upper, x, msg1, msg2]
        if outer + 1 < ADMM_ITERS:
            *pieces, x, z, y, ax, ppx = call(
                functools.partial(update_kernel, n, own),
                [own_shape] * n + [own_shape, slab_shape, slab_shape, slab_shape, ((2 * BLK, LANES), F32)],
                [*state, ppx, pp1, pp2, *t_mats],
                [place, pairs],
                total_scratch,
                flops=prod_flops,
            )
        else:
            (out,) = call(
                functools.partial(last_kernel, n, own), [((2 * half_rows + own, LANES), F32)], state
            )
    return call(
        finish_kernel,
        [own_shape, ((slab_rows, LANES), F32), ((slab_rows, LANES), F32)],
        [out, to_core(out)],
        [place],
    )


def solution(mesh):
    placed = (
        P(("col", "row"), "grp"),
        P(("col", "row"), "grp"),
        P(("col", "row")),
        P("row", "grp"),
        P("row", "grp"),
        P("row", "grp"),
        P("row", "grp"),
        P("row", "col", None, None),
        P("row", "col"),
        P("col", "row", None, None),
        P("col", "row", None),
    )

    def run(*args):
        return tuple(local(*args))

    return jax.shard_map(
        run,
        mesh=mesh,
        in_specs=placed,
        out_specs=(P(("col", "row"), "grp"), P("row", "grp"), P("row", "grp")),
        check_vma=False,
    )
```

```python
import functools

import jax
import jax.numpy as jnp
from jax import lax
from jax.experimental import pallas as pl
from jax.experimental.pallas import tpu as pltpu
from jax.sharding import PartitionSpec as P

ADMM_ITERS = 2
RHO = 0.5
SIGMA = 1e-06
RELAX = 1.6
BLK = 128
LANES = 128
HALF = 64
SC = 8
F32 = jnp.float32
BF16 = jnp.bfloat16

VMEM = pl.BlockSpec(memory_space=pltpu.VMEM)
SMEM = pl.BlockSpec(memory_space=pltpu.SMEM)

ANY = pl.BlockSpec(memory_space=pl.ANY)


def call(body, outs, ins, smem=(), scratch=(), flops=0, after=None):
    n_bytes = sum(v.size * v.dtype.itemsize for v in ins)
    tied = [] if after is None else [after]

    def run(*refs):
        body(*refs[len(tied) :])

    return pl.pallas_call(
        run,
        out_shape=[jax.ShapeDtypeStruct(s, d) for s, d in outs],
        in_specs=[ANY] * len(tied) + [SMEM] * len(smem) + [VMEM] * len(ins),
        out_specs=[VMEM] * len(outs),
        scratch_shapes=list(scratch),
        compiler_params=pltpu.CompilerParams(vmem_limit_bytes=30 * 1024 * 1024),
        cost_estimate=pl.CostEstimate(flops=flops, bytes_accessed=n_bytes, transcendentals=0),
    )(*tied, *smem, *ins)


def low_half(shape):
    return lax.broadcasted_iota(jnp.int32, shape, 1) < HALF


def turn(v):
    return pltpu.roll(v, HALF, 1)


def fold(v):
    return v + turn(v)


def col_sum(v):
    return fold(jnp.sum(v, axis=0, keepdims=True))


def split_bf16(v):
    hi = v.astype(BF16).astype(F32)
    return hi, v - hi


def pair_up(v):
    hi, lo = split_bf16(v)
    low = low_half(v.shape)
    first = jnp.where(low, hi, turn(lo)).astype(BF16)
    second = jnp.where(low, turn(hi), lo).astype(BF16)
    return first, second


def dot(a, b):
    return jnp.dot(a, b, preferred_element_type=F32)


def pack_rows(*rows):
    at = lax.broadcasted_iota(jnp.int32, (SC, LANES), 0)
    tile = jnp.zeros((SC, LANES), F32)
    for k, row in enumerate(rows):
        tile = jnp.where(at == k, row, tile)
    return tile


def mix_cores(core, mine, other):
    low = low_half(mine.shape)
    a = jnp.where(core == 0, mine, turn(mine))
    b = jnp.where(core == 0, turn(other), other)
    return jnp.where(low, a, b)


def own_kernel(place, x, x_other, q, q_other, x_own, q_own):
    core = place[1]
    x_own[...] = mix_cores(core, x[...], x_other[...])
    q_own[...] = mix_cores(core, q[...], q_other[...])


def slab_kernel(place, *refs):
    core = place[1]
    count = len(refs) // 2
    for src, dst in zip(refs[:count], refs[count:]):
        rows = dst.shape[0]
        v = jnp.where(core == 0, src[...], turn(src[...]))
        dst[...] = jnp.where(low_half(dst.shape), v[:rows], turn(v[rows:]))


def prep_kernel(slab, per, cols, pairs, a_in, p_in, a_both, t_hi, t_lo, p_hi, p_lo, diag):
    for ref in (t_hi, t_lo):
        ref[...] = jnp.zeros(ref.shape, BF16)
    diag[...] = jnp.zeros(diag.shape, F32)
    for m in range(slab):
        rows = slice(m * BLK, (m + 1) * BLK)
        for s in range(per):
            k = m * per + s
            col = cols[k]
            at = pl.multiple_of(col * BLK, BLK)
            block = a_in[k]
            hi, lo = split_bf16(block)
            a_both[2 * m * BLK : (2 * m + 1) * BLK, s * BLK : (s + 1) * BLK] = hi.astype(BF16)
            a_both[(2 * m + 1) * BLK : (2 * m + 2) * BLK, s * BLK : (s + 1) * BLK] = lo.astype(BF16)
            hi, lo = split_bf16(block.T)
            t_hi[pl.ds(at, BLK), rows] = hi.astype(BF16)
            t_lo[pl.ds(at, BLK), rows] = lo.astype(BF16)
            diag[pl.ds(col, 1), :] += RHO * jnp.sum(block * block, axis=0, keepdims=True)
    shape = (BLK, BLK)
    eye = lax.broadcasted_iota(jnp.int32, shape, 0) == lax.broadcasted_iota(jnp.int32, shape, 1)
    for e in range(4):
        hi, lo = split_bf16(p_in[e])
        rows = slice((e // 2) * BLK, (e // 2 + 1) * BLK)
        lanes = slice((e % 2) * BLK, (e % 2 + 1) * BLK)
        p_hi[rows, lanes] = hi.astype(BF16)
        p_lo[rows, lanes] = lo.astype(BF16)
    for e in range(2):
        diag[pl.ds(pairs[e], 1), :] += jnp.sum(jnp.where(eye, p_in[3 * e], 0.0), axis=0, keepdims=True)


def slab_product(slab, cols, a_refs, starts, wide):
    per = cols.shape[0] // (slab * len(a_refs))
    sums = []
    for m in range(slab):
        total = None
        for t, a_ref in enumerate(a_refs):
            blocks = []
            for s in range(per):
                at = starts[t] + cols[(t * slab + m) * per + s] * BLK
                blocks.append(wide[pl.ds(pl.multiple_of(at, BLK), BLK), :])
            part = dot(a_ref[2 * m * BLK : (2 * m + 2) * BLK, :], jnp.concatenate(blocks, axis=0))
            total = part if total is None else total + part
        sums.append(total[:BLK] + total[BLK:])
    return jnp.concatenate(sums, axis=0)


def first_kernel(n, own, slab, place, pairs, cols, *refs):
    msgs, (a_both, p_hi, p_lo, keep, send, wide) = refs[:n], refs[n:]
    core = place[1]
    for k in range(n):
        at = pl.multiple_of(lax.bitwise_xor(place[0], k) * own, own)
        hi, lo = split_bf16(msgs[k][...])
        wide[pl.ds(at, own), 0:LANES] = hi.astype(BF16)
        wide[pl.ds(at, own), LANES:] = lo.astype(BF16)
    total = slab_product(slab, cols, [a_both], [0], wide)
    total = total[:, :LANES] + total[:, LANES:]
    rows = total.shape[0] // 2
    keep[0:rows, :] = mix_cores(core, total[:rows], total[rows:])
    send[0:rows, :] = mix_cores(1 - core, total[:rows], total[rows:])
    at_i = pl.ds(pl.multiple_of(pairs[0] * BLK, BLK), BLK)
    at_j = pl.ds(pl.multiple_of(pairs[1] * BLK, BLK), BLK)
    v = jnp.concatenate([wide[at_i, :], wide[at_j, :]], axis=0)
    part = dot(p_hi[...], v) + dot(p_lo[...], v)
    part = part[:, :LANES] + part[:, LANES:]
    part = jnp.where(core == 0, part, turn(part))
    keep[rows:, :] = part
    send[rows:, :] = part


def meet_kernel(keep, got, msg, pp):
    rows = msg.shape[0]
    msg[...] = keep[0:rows, :] + got[0:rows, :]
    pp[...] = jnp.where(low_half(pp.shape), keep[rows:, :], got[rows:, :])


def forward_kernel(n, own, slab, scalars, place, pairs, cols, *refs):
    msgs, rest = refs[:n], refs[n:]
    a_mats, p_mats, rest = rest[:2], rest[2:6], rest[6:]
    if scalars == 2:
        pp_first, rest = rest[0], rest[1:]
    msg, pp, whole, wide = rest
    row = place[0]
    span = whole.shape[0]
    for k in range(n):
        at = pl.multiple_of(lax.bitwise_xor(row, k) * own, own)
        v = msgs[k][0:own, :]
        whole[pl.ds(at, own), :] = v
        first, second = pair_up(v)
        wide[pl.ds(at, own), :] = first
        wide[pl.ds(pl.multiple_of(span + at, own), own), :] = second
    total = fold(slab_product(slab, cols, a_mats, [0, span], wide))
    rows = total.shape[0] // 2
    msg[0:rows, :] = jnp.where(low_half((rows, LANES)), total[:rows], total[rows:])
    parts = []
    for t in range(2):
        at_i = pl.multiple_of(t * span + pairs[2 * t] * BLK, BLK)
        at_j = pl.multiple_of(t * span + pairs[2 * t + 1] * BLK, BLK)
        v = jnp.concatenate([wide[pl.ds(at_i, BLK), :], wide[pl.ds(at_j, BLK), :]], axis=0)
        parts.append(fold(dot(p_mats[2 * t][...], v) + dot(p_mats[2 * t + 1][...], v)))
    low2 = low_half((2 * BLK, LANES))
    pp_now = jnp.where(low2, parts[0], parts[1])
    pp[...] = pp_now
    picked = []
    for t in range(2):
        at_i = pl.multiple_of(pairs[2 * t] * BLK, BLK)
        at_j = pl.multiple_of(pairs[2 * t + 1] * BLK, BLK)
        picked.append(jnp.concatenate([whole[pl.ds(at_i, BLK), :], whole[pl.ds(at_j, BLK), :]], axis=0))
    vec = jnp.where(low2, picked[0], picked[1])
    tile = msgs[0][own : own + SC, :]
    for k in range(1, n):
        tile = tile + msgs[k][own : own + SC, :]
    tile = fold(tile)
    at = lax.broadcasted_iota(jnp.int32, (SC, LANES), 0)
    tile = jnp.where(at == 3, col_sum(vec * pp_now), tile)
    if scalars == 2:
        tile = jnp.where(at == 4, col_sum(vec * pp_first[...]), tile)
    msg[rows : rows + SC, :] = tile


def back_product(n, own, place, pairs, w, pp_now, t_mats, total, outs, extra=()):
    row = place[0]
    span = total.shape[0]
    first, second = pair_up(w)
    wide = jnp.concatenate([first, second], axis=0)
    mine = fold(dot(t_mats[0][...], wide) + dot(t_mats[1][...], wide))
    other = fold(dot(t_mats[2][...], wide) + dot(t_mats[3][...], wide))
    total[...] = jnp.where(low_half((span, LANES)), mine, other)
    low1 = low_half((BLK, LANES))
    for t in range(2):
        side = low1 if t == 0 else jnp.logical_not(low1)
        for e in range(2):
            at = pl.ds(pl.multiple_of(pairs[2 * t + e] * BLK, BLK), BLK)
            total[at, :] += jnp.where(side, pp_now[e * BLK : (e + 1) * BLK], 0.0)
    for k in range(n):
        at = pl.multiple_of(lax.bitwise_xor(row, k) * own, own)
        outs[k][0:own, :] = total[pl.ds(at, own), :]
        at = own
        for rows in extra:
            outs[k][at : at + rows.shape[0], :] = rows
            at += rows.shape[0]


def start_back_kernel(n, nx, own, place, pairs, *refs):
    msgs, rest = refs[:nx], refs[nx:]
    z, y, pp, diag, diag_other, *t_mats = rest[:9]
    outs, (ax, total) = rest[9 : 9 + n], rest[9 + n :]
    ax_now = msgs[0][...]
    for k in range(1, nx):
        ax_now = ax_now + msgs[k][...]
    ax[...] = ax_now
    w = RHO * ax_now - (RHO * z[...] - y[...])
    back_product(n, own, place, pairs, w, pp[...], t_mats, total, outs, (diag[...], diag_other[...]))


def step_back_kernel(n, nx, own, place, pairs, *refs):
    msgs, rest = refs[:nx], refs[nx:]
    pp, *t_mats = rest[:5]
    outs, (ad, scal, total) = rest[5 : 5 + n], rest[5 + n :]
    rows = ad.shape[0]
    v = msgs[0][...]
    for k in range(1, nx):
        v = v + msgs[k][...]
    ad_now = v[:rows]
    tile = v[rows:]
    ad[...] = ad_now
    scal[...] = tile
    curve = RHO * col_sum(ad_now * ad_now) + tile[3:4]
    back_product(n, own, place, pairs, RHO * ad_now, pp[...], t_mats, total, outs, (pack_rows(curve),))


def residual_kernel(n, own, first, place, *refs):
    msgs, rest = refs[:n], refs[n:]
    if first:
        x, q, pd, msg, res, dk, full = rest
        rows = msgs[0].shape[0] - own
        tile = msgs[0][own:, :]
        for k in range(1, n):
            tile = tile + msgs[k][own:, :]
        n_range = rows // 2
        low1 = low_half((BLK, LANES))
        for b in range(n_range):
            mine = jnp.broadcast_to(tile[b : b + 1], (BLK, LANES)).T
            other = jnp.broadcast_to(tile[n_range + b : n_range + b + 1], (BLK, LANES)).T
            full[b * BLK : (b + 1) * BLK, :] = jnp.where(low1, mine, other)
        at = pl.multiple_of(place[0] * own, own)
        diag = pd[...] + SIGMA + full[pl.ds(at, own), :]
        dk[...] = diag
    else:
        base, pd, dk, msg, res = rest
        diag = dk[...]
    total = msgs[0][0:own, :]
    for k in range(1, n):
        total = total + msgs[k][0:own, :]
    r = (-q[...] - pd[...] * x[...] if first else base[...]) - total
    s = r / diag
    res[...] = r
    msg[0:own, :] = s
    shift = pd[...] + SIGMA
    rz = jnp.sum(r * s, axis=0, keepdims=True)
    dd = jnp.sum(shift * s * s, axis=0, keepdims=True)
    msg[own : own + SC, :] = pack_rows(rz, dd)


def base_kernel(x, q, pd, dk, base, pd_out, dk_out):
    base[...] = -q[...] - pd[...] * x[...]
    pd_out[...] = pd[...]
    dk_out[...] = dk[...]


def step_kernel(n, own, *refs):
    msgs, rest = refs[:n], refs[n:]
    scal, prev, r, pd, dk, msg, step_out = rest
    total = msgs[0][...]
    for k in range(1, n):
        total = total + msgs[k][...]
    shift = pd[...] + SIGMA
    d = prev[0:own, :]
    kd = shift * d + total[:own]
    curve = total[own : own + 1] + scal[1:2, :]
    step = scal[0:1, :] / curve
    r_new = r[...] - step * kd
    s = r_new / dk[...]
    msg[0:own, :] = s
    rz = jnp.sum(r_new * s, axis=0, keepdims=True)
    ss = jnp.sum(shift * s * s, axis=0, keepdims=True)
    sd = jnp.sum(shift * s * d, axis=0, keepdims=True)
    msg[own : own + SC, :] = pack_rows(rz, ss, sd)
    step_out[...] = jnp.broadcast_to(step, step_out.shape)


def curve_kernel(nx, *refs):
    msgs, rest = refs[:nx], refs[nx:]
    scal, ad, ad2, share, keep = rest
    rows = ad.shape[0]
    v = msgs[0][...]
    for k in range(1, nx):
        v = v + msgs[k][...]
    tile = v[rows:]
    beta = tile[0:1] / scal[0:1, :]
    ad_now = v[:rows] + beta * ad[...]
    ad2[...] = ad_now
    flat = tile[1:2] + 2.0 * beta * tile[2:3] + beta * beta * scal[1:2, :]
    pair = tile[3:4] + 2.0 * beta * tile[4:5] + beta * beta * scal[3:4, :]
    share[...] = pack_rows(RHO * col_sum(ad_now * ad_now) + pair)
    keep[...] = pack_rows(tile[0:1], beta, flat)


def admm_update(n, own, refs):
    shares, rest = refs[:n], refs[n:]
    keep, step_in, ax, ad, ad2, z, y, lower, upper, x, msg1, msg2 = rest[:12]
    tile = shares[0][...]
    for k in range(1, n):
        tile = tile + shares[k][...]
    beta = keep[1:2, :]
    step1 = step_in[0:1, :]
    step2 = keep[0:1, :] / (tile[0:1] + keep[2:3, :])
    d1 = msg1[0:own, :]
    d2 = msg2[0:own, :] + beta * d1
    x_hat = x[...] + step1 * d1 + step2 * d2
    x_new = RELAX * x_hat + (1.0 - RELAX) * x[...]
    ax_hat = ax[...] + step1 * ad[...] + step2 * ad2[...]
    relaxed = RELAX * ax_hat + (1.0 - RELAX) * z[...]
    z_new = jnp.clip(relaxed + y[...] / RHO, lower[...], upper[...])
    y_new = y[...] + RHO * (relaxed - z_new)
    return beta, step1, step2, x_new, ax_hat, z_new, y_new, rest[12:]


def update_kernel(n, own, place, pairs, *refs):
    beta, step1, step2, x_new, ax_hat, z_new, y_new, rest = admm_update(n, own, refs)
    ax = refs[n + 2]
    ppx, pp1, pp2, *t_mats = rest[:7]
    outs, (x_out, z_out, y_out, ax_out, ppx_out, total) = rest[7 : 7 + n], rest[7 + n :]
    x_out[...] = x_new
    z_out[...] = z_new
    y_out[...] = y_new
    ax_new = RELAX * ax_hat + (1.0 - RELAX) * ax[...]
    ax_out[...] = ax_new
    pp_hat = ppx[...] + step1 * pp1[...] + step2 * (pp2[...] + beta * pp1[...])
    pp_new = RELAX * pp_hat + (1.0 - RELAX) * ppx[...]
    ppx_out[...] = pp_new
    w = RHO * ax_new - (RHO * z_new - y_new)
    back_product(n, own, place, pairs, w, pp_new, t_mats, total, outs)


def last_kernel(n, own, *refs):
    _, _, _, x_new, _, z_new, y_new, rest = admm_update(n, own, refs)
    (out,) = rest
    rows = z_new.shape[0]
    out[0:rows, :] = z_new
    out[rows : 2 * rows, :] = y_new
    out[2 * rows :, :] = x_new


def finish_kernel(place, mine, got, x, z, y):
    core = place[1]
    rows = z.shape[0] // 2
    for k, dst in enumerate((z, y)):
        a = mine[k * rows : (k + 1) * rows, :]
        b = got[k * rows : (k + 1) * rows, :]
        low = low_half(a.shape)
        left = jnp.where(core == 0, a, b)
        right = jnp.where(core == 0, b, a)
        dst[0:rows, :] = jnp.where(low, left, turn(right))
        dst[rows : 2 * rows, :] = jnp.where(low, turn(left), right)
    a = mine[2 * rows :, :]
    b = got[2 * rows :, :]
    low = low_half(a.shape)
    x[...] = jnp.where(core == 0, jnp.where(low, a, b), jnp.where(low, turn(b), turn(a)))


def local(x_state, q_lin, p_diag, z_state, y_state, lower_bound, upper_bound, a_blocks, a_cols, p_blocks, p_pairs):
    slab, per = a_cols.shape
    n = lax.axis_size("row")
    n_col = lax.axis_size("col")
    nx = n_col // 2
    own = x_state.shape[0]
    span = own * n
    n_range = span // BLK
    slab_rows = slab * BLK
    half_rows = slab_rows // 2
    row_at = lax.axis_index("row")
    core_at = lax.axis_index("col") % 2
    place = jnp.stack([row_at, core_at]).astype(jnp.int32)

    def to_core(v):
        return lax.ppermute(v, "col", [(c, c ^ 1) for c in range(n_col)])

    def to_x(v):
        return [v] + [lax.ppermute(v, "col", [(c, c ^ (2 * k)) for c in range(n_col)]) for k in range(1, nx)]

    ks = range(1, n)
    scalar_ks = (1, 3, 2) if n == 4 else ks

    def over_row(v, k):
        return lax.ppermute(v, "row", [(i, i ^ k) for i in range(n)])

    def to_row(pieces):
        return [pieces[0]] + [over_row(pieces[k], k) for k in ks]

    def to_all_rows(v):
        return [v] + [over_row(v, k) for k in ks]

    a_mine = a_blocks.reshape(slab * per, BLK, BLK)
    p_mine = p_blocks.reshape(4, BLK, BLK)
    ints = jnp.concatenate([a_cols.reshape(-1), p_pairs.reshape(-1)])
    x_rows = to_all_rows(x_state)
    a_other = to_core(a_mine)
    ints_other = to_core(ints)
    p_other = to_core(p_mine)
    pd_other = to_core(p_diag)
    count = slab * per
    pd = jnp.concatenate(
        [jnp.broadcast_to(p_diag[:, None], (own, HALF)), jnp.broadcast_to(pd_other[:, None], (own, HALF))], axis=1
    )
    x, q = call(
        own_kernel, [((own, LANES), F32)] * 2, [x_state, to_core(x_state), q_lin, to_core(q_lin)], [place]
    )
    z, y, lower, upper = call(
        slab_kernel, [((half_rows, LANES), F32)] * 4, [z_state, y_state, lower_bound, upper_bound], [place]
    )
    own_shape = ((own, LANES), F32)
    msg_shape = ((own + SC, LANES), F32)
    tile_shape = ((SC, LANES), F32)
    slab_shape = ((half_rows, LANES), F32)
    pp_shape = ((2 * BLK, LANES), F32)

    def prepare(a, p, at_cols, at_pairs, after=None):
        *mats, diag = call(
            functools.partial(prep_kernel, slab, per),
            [((2 * slab_rows, per * BLK), BF16)]
            + [((span, slab_rows), BF16)] * 2
            + [((2 * BLK, 2 * BLK), BF16)] * 2
            + [((n_range, LANES), F32)],
            [a, p],
            [at_cols, at_pairs],
            flops=10**8,
            after=after,
        )
        return mats[0:1], mats[1:3], mats[3:5], diag

    prod_flops = 4 * slab_rows * 2 * span * LANES
    total_scratch = [pltpu.VMEM((span, LANES), F32)]
    a_own, t_own, p_own, diag = prepare(a_mine, p_mine, a_cols.reshape(-1), p_pairs.reshape(-1))
    both_shape = ((half_rows + 2 * BLK, LANES), F32)
    keep, send = call(
        functools.partial(first_kernel, n, own, slab),
        [both_shape, both_shape],
        [*x_rows, *a_own, *p_own],
        [place, p_pairs.reshape(-1), a_cols.reshape(-1)],
        [pltpu.VMEM((span, 2 * LANES), BF16)],
        flops=prod_flops,
    )
    msg, ppx = call(meet_kernel, [slab_shape, pp_shape], [keep, to_core(send)])
    a_far, t_far, p_far, diag_other = prepare(
        a_other, p_other, ints_other[:count], ints_other[count:], after=msg
    )
    a_mats, t_mats, p_mats = [*a_own, *a_far], [*t_own, *t_far], [*p_own, *p_far]
    pairs = jnp.concatenate([p_pairs.reshape(-1), ints_other[count:]])
    cols = jnp.concatenate([a_cols.reshape(-1), ints_other[:count]])

    def forward(msgs, scalars, pp_first=()):
        return call(
            functools.partial(forward_kernel, n, own, slab, scalars),
            [((half_rows + SC, LANES), F32), pp_shape],
            [*msgs, *a_mats, *p_mats, *pp_first],
            [place, pairs, cols],
            total_scratch + [pltpu.VMEM((2 * span, LANES), BF16)],
            flops=prod_flops,
        )

    *pieces, ax = call(
        functools.partial(start_back_kernel, n, nx, own),
        [((own + 2 * n_range, LANES), F32)] * n + [((half_rows, LANES), F32)],
        [*to_x(msg), z, y, ppx, diag, diag_other, *t_mats],
        [place, pairs],
        total_scratch,
        flops=prod_flops,
    )
    for outer in range(ADMM_ITERS):
        if outer == 0:
            msg1, r, dk = call(
                functools.partial(residual_kernel, n, own, True),
                [msg_shape, own_shape, own_shape],
                [*to_row(pieces), x, q, pd],
                [place],
                total_scratch,
            )
        else:
            base, pd, dk = call(base_kernel, [own_shape] * 3, [x, q, pd, dk], after=pieces[0])
            msg1, r = call(
                functools.partial(residual_kernel, n, own, False),
                [msg_shape, own_shape],
                [*to_row(pieces), base, pd, dk],
                [place],
            )
        msg, pp1 = forward(to_all_rows(msg1), 1)
        *pieces, ad, scal = call(
            functools.partial(step_back_kernel, n, nx, own),
            [msg_shape] * n + [slab_shape, tile_shape],
            [*to_x(msg), pp1, *t_mats],
            [place, pairs],
            total_scratch,
            flops=prod_flops,
        )
        msg2, step = call(
            functools.partial(step_kernel, n, own),
            [msg_shape, tile_shape],
            [*to_row(pieces), scal, msg1, r, pd, dk],
        )
        msg, pp2 = forward(to_all_rows(msg2), 2, (pp1,))
        ad2, share, keep = call(
            functools.partial(curve_kernel, nx),
            [slab_shape, tile_shape, tile_shape],
            [*to_x(msg), scal, ad],
        )
        shares = [share] + [over_row(share, k) for k in scalar_ks]
        state = [*shares, keep, step, ax, ad, ad2, z, y, lower, upper, x, msg1, msg2]
        if outer + 1 < ADMM_ITERS:
            *pieces, x, z, y, ax, ppx = call(
                functools.partial(update_kernel, n, own),
                [own_shape] * n + [own_shape, slab_shape, slab_shape, slab_shape, ((2 * BLK, LANES), F32)],
                [*state, ppx, pp1, pp2, *t_mats],
                [place, pairs],
                total_scratch,
                flops=prod_flops,
            )
        else:
            (out,) = call(
                functools.partial(last_kernel, n, own), [((2 * half_rows + own, LANES), F32)], state
            )
    return call(
        finish_kernel,
        [own_shape, ((slab_rows, LANES), F32), ((slab_rows, LANES), F32)],
        [out, to_core(out)],
        [place],
    )


def solution(mesh):
    placed = (
        P(("col", "row"), "grp"),
        P(("col", "row"), "grp"),
        P(("col", "row")),
        P("row", "grp"),
        P("row", "grp"),
        P("row", "grp"),
        P("row", "grp"),
        P("row", "col", None, None),
        P("row", "col"),
        P("col", "row", None, None),
        P("col", "row", None),
    )

    def run(*args):
        return tuple(local(*args))

    return jax.shard_map(
        run,
        mesh=mesh,
        in_specs=placed,
        out_specs=(P(("col", "row"), "grp"), P("row", "grp"), P("row", "grp")),
        check_vma=False,
    )
```
